32 devices in a mesh: tm: 8 (over z, x), cuts: 4 (over y, core).
Axes of the slice: x: 2, y: 2, z: 4, core: 2. Of those that a mesh axis runs over, the one named last changes fastest.
Arguments:
- start_image: float32 [32, 2, 128, 256], P(('cuts', 'tm')), parts along dimension 0, may hold values from -6 to 6
- sensitivity: bfloat16 [32, 2, 128, 256], P('cuts'), parts along dimension 0, may hold values from -2 to 2
- kspace: bfloat16 [32, 8, 2, 128, 256], P(('cuts', 'tm')), parts along dimension 0, may hold values from -6 to 6
- sampled: int32 [32, 8, 256], P(('cuts', 'tm')), parts along dimension 0, may hold values from 0 to 1
- offsets: int32 [8, 2], P('cuts'), parts along dimension 0, may hold values from 0 to 15
Outputs:
- reconstruction: float32 [32, 2, 128, 256], P(('cuts', 'tm')), parts along dimension 0
The draws below stay inside these ranges and needn't reach their ends.
There are 4 independent parts, one for each index of `cuts`. The reference program is written for one: setup_inputs(seed, part) draws one part's arguments, and reference() takes and returns one part's arrays. A program takes and returns all parts, laid end to end along the dimension named above; each array names one. Nothing has to cross between parts.
All inputs are finite; a program needn't handle non-finite values. Where the reference program divides by a largest or mean magnitude, that divisor is 1e-20 or more.
Results may differ from the reference program's by a relative error of at most 0.0037.
Values sent between devices are 32-bit elements; how exact they have to be, the bound alone decides.
No kernel may reach another device: no remote copies, remote signals or barrier semaphores. Data moves between devices by JAX's collectives and lax.ppermute only.
A program may use at most 64 MiB of HBM per device.

```python
import math
import jax
import jax.numpy as jnp
from jax import lax

NY = 256
COILS = 8
XW = 128
BS = 16
ITERS = 2
NEWTON = 4
FRAMES = 8


def draw_sampled(key, part):
    levels = jax.random.randint(jax.random.fold_in(key, 11), (FRAMES, COILS, NY), 0, 1000)
    frame_index = jnp.arange(FRAMES, dtype=jnp.int32)
    limits = 150 + 450 * frame_index // max(FRAMES - 1, 1)
    return (levels < limits[:, None, None]).astype(jnp.int32)


def plant(values, key, low, largest):
    extent = values.shape
    place = [jax.random.randint(jax.random.fold_in(key, axis), (), 0, extent[axis]) for axis in range(len(extent))]
    values = values.at[tuple(place)].set(low)
    longest = extent.index(max(extent))
    place[longest] = (place[longest] + 1) % extent[longest]
    return values.at[tuple(place)].set(largest)


def shard_levels(stream_key, extent, pieces, least, largest):
    factor_of, own = 1.0, jax.random.fold_in(stream_key, 6)
    for position, blocks in pieces:
        steps = jnp.exp(jax.random.uniform(jax.random.fold_in(own, position), (blocks,), jnp.float32, least / len(pieces), largest / len(pieces)))
        factor_of = factor_of * jnp.repeat(steps, extent[position] // blocks).reshape([-1 if axis == position else 1 for axis in range(len(extent))])
    return factor_of


def bell_draw(own_key, dims, scale, bound, split=(), kind=jnp.bfloat16):
    result = scale * jax.random.normal(own_key, dims, jnp.float32)
    if split:
        result = result * shard_levels(own_key, dims, split, -0.22, 0.18)
    return jnp.clip(result, -bound, bound).astype(kind)


def setup_inputs(seed: int = 0, part: int = 0) -> dict:
    key_of = jax.random.split(jax.random.key(seed), 6)
    part_keys = jax.random.split(jax.random.fold_in(key_of[5], part), 6)
    return {
        "start_image": bell_draw(part_keys[0], (FRAMES, 2, XW, NY), 1.0, 6.0, ((0, 8),), jnp.float32),
        "sensitivity": bell_draw(part_keys[1], (COILS, 2, XW, NY), 0.35, 2.0),
        "kspace": bell_draw(part_keys[2], (FRAMES, COILS, 2, XW, NY), 1.0, 6.0, ((0, 8),)),
        "sampled": draw_sampled(jax.random.fold_in(jax.random.fold_in(key_of[5], part), 71), part),
        "offsets": plant(jax.random.randint(part_keys[4], (ITERS, 2), 0, BS), jax.random.fold_in(part_keys[4], 1), 0, BS - 1).astype(jnp.int32),
    }


shrink_ratio = 0.5
epsilon = 1e-06

def dft_tables(length):
    indices = jnp.arange(length, dtype=jnp.int32)
    phases = indices[:, None] * indices[None, :] % length
    angles = phases.astype(jnp.float32) * (2.0 * math.pi / length)
    norm_scale = 1.0 / math.sqrt(length)
    return ((jnp.cos(angles) * norm_scale).astype(jnp.bfloat16), (jnp.sin(angles) * norm_scale).astype(jnp.bfloat16))

def forward(real_part, imag_part, cosine_table, sine_table):
    out_real = jnp.dot(real_part, cosine_table, preferred_element_type=jnp.float32) + jnp.dot(imag_part, sine_table, preferred_element_type=jnp.float32)
    out_imag = jnp.dot(imag_part, cosine_table, preferred_element_type=jnp.float32) - jnp.dot(real_part, sine_table, preferred_element_type=jnp.float32)
    return (out_real, out_imag)

def inverse(real_part, imag_part, cosine_table, sine_table):
    out_real = jnp.dot(real_part, cosine_table, preferred_element_type=jnp.float32) - jnp.dot(imag_part, sine_table, preferred_element_type=jnp.float32)
    out_imag = jnp.dot(imag_part, cosine_table, preferred_element_type=jnp.float32) + jnp.dot(real_part, sine_table, preferred_element_type=jnp.float32)
    return (out_real, out_imag)

def coil_spectra(field, sens_real, sens_imag, cosine_table, sine_table):
    coils, width, length = sens_real.shape
    coil_real = (sens_real * field[0] - sens_imag * field[1]).astype(jnp.bfloat16).reshape(coils * width, length)
    coil_imag = (sens_real * field[1] + sens_imag * field[0]).astype(jnp.bfloat16).reshape(coils * width, length)
    spec_real, spec_imag = forward(coil_real, coil_imag, cosine_table, sine_table)
    return (spec_real.reshape(coils, width, length), spec_imag.reshape(coils, width, length))

def frame_terms(field, sensitivity, data, lines, cosine_table, sine_table):
    sens_real = sensitivity[:, 0].astype(jnp.float32)
    sens_imag = sensitivity[:, 1].astype(jnp.float32)
    coils, width, length = sens_real.shape
    weight = lines.astype(jnp.float32)[:, None, :]
    spec_real, spec_imag = coil_spectra(field, sens_real, sens_imag, cosine_table, sine_table)
    misfit_real = (weight * (spec_real - data[:, 0].astype(jnp.float32))).astype(jnp.bfloat16)
    misfit_imag = (weight * (spec_imag - data[:, 1].astype(jnp.float32))).astype(jnp.bfloat16)
    back_real, back_imag = inverse(misfit_real.reshape(coils * width, length), misfit_imag.reshape(coils * width, length), cosine_table, sine_table)
    back_real = back_real.reshape(coils, width, length)
    back_imag = back_imag.reshape(coils, width, length)
    grad_real = lax.optimization_barrier(jnp.sum(sens_real * back_real + sens_imag * back_imag, axis=0))
    grad_imag = lax.optimization_barrier(jnp.sum(sens_real * back_imag - sens_imag * back_real, axis=0))
    gradient = jnp.stack([grad_real, grad_imag])
    numerator = jnp.sum(gradient * gradient)
    probe_real, probe_imag = coil_spectra(gradient, sens_real, sens_imag, cosine_table, sine_table)
    denominator = jnp.sum(weight * (probe_real * probe_real + probe_imag * probe_imag))
    return (gradient, numerator, denominator)

def shrink(casorati):
    highest = lax.Precision.HIGHEST
    gram = jnp.einsum('bfv,bgv->bfg', casorati, casorati, precision=highest)
    frames = gram.shape[1]
    identity = jnp.eye(frames, dtype=jnp.float32)
    shrink_level = shrink_ratio * jnp.trace(gram, axis1=1, axis2=2) / frames + epsilon
    system = gram + shrink_level[:, None, None] * identity
    row_bound = lax.optimization_barrier(jnp.max(lax.optimization_barrier(jnp.sum(jnp.abs(system), axis=2)), axis=1))
    approx = identity[None] / row_bound[:, None, None]
    for newton in range(NEWTON):
        product = jnp.einsum('bfg,bgh->bfh', system, approx, precision=highest)
        approx = jnp.einsum('bfg,bgh->bfh', approx, 2.0 * identity - product, precision=highest)
    return casorati - shrink_level[:, None, None] * jnp.einsum('bfg,bgv->bfv', approx, casorati, precision=highest)

def to_blocks(field):
    frames, parts, width, length = field.shape
    blocks = field.reshape(frames, parts, width // BS, BS, length // BS, BS)
    blocks = blocks.transpose(2, 4, 0, 1, 3, 5)
    return blocks.reshape(width // BS * (length // BS), frames, parts * BS * BS)

def from_blocks(blocks, width, length):
    frames = blocks.shape[1]
    field = blocks.reshape(width // BS, length // BS, frames, 2, BS, BS)
    field = field.transpose(2, 3, 0, 4, 1, 5)
    return field.reshape(frames, 2, width, length)

def reference(start_image, sensitivity, kspace, sampled, offsets):
    width, length = (start_image.shape[2], start_image.shape[3])
    cosine_table, sine_table = dft_tables(length)
    estimate = start_image

    def per_frame(frame_items):
        field, data, lines = frame_items
        return frame_terms(field, sensitivity, data, lines, cosine_table, sine_table)
    for iteration in range(ITERS):
        gradient, numerator, denominator = lax.map(per_frame, (estimate, kspace, sampled))
        step_length = jnp.sum(numerator) / (jnp.sum(denominator) + epsilon)
        moved = estimate - step_length * gradient
        offset_pair = offsets[iteration]
        rolled = jnp.roll(moved, (offset_pair[0], offset_pair[1]), axis=(2, 3))
        shrunk = shrink(to_blocks(rolled))
        placed = from_blocks(shrunk, width, length)
        estimate = jnp.roll(placed, (-offset_pair[0], -offset_pair[1]), axis=(2, 3))
    return estimate
```

```python
import math

import jax
import jax.numpy as jnp
import ml_dtypes
import numpy as np
from jax import lax
from jax.experimental import pallas as pl
from jax.experimental.pallas import tpu as pltpu
from jax.sharding import PartitionSpec as P

BS = 16
ITERS = 2
NEWTON = 4
LANES = 128
SUBLANES = 8


shrink_ratio = 0.5
epsilon = 1e-06


def dft_tables(length):
    indices = jnp.arange(length, dtype=jnp.int32)
    phases = indices[:, None] * indices[None, :] % length
    angles = phases.astype(jnp.float32) * (2.0 * math.pi / length)
    norm_scale = 1.0 / math.sqrt(length)
    return (
        (jnp.cos(angles) * norm_scale).astype(jnp.bfloat16),
        (jnp.sin(angles) * norm_scale).astype(jnp.bfloat16),
    )


def forward(real_part, imag_part, cosine_table, sine_table):
    out_real = jnp.dot(real_part, cosine_table, preferred_element_type=jnp.float32) + jnp.dot(
        imag_part, sine_table, preferred_element_type=jnp.float32
    )
    out_imag = jnp.dot(imag_part, cosine_table, preferred_element_type=jnp.float32) - jnp.dot(
        real_part, sine_table, preferred_element_type=jnp.float32
    )
    return (out_real, out_imag)


def inverse(real_part, imag_part, cosine_table, sine_table):
    out_real = jnp.dot(real_part, cosine_table, preferred_element_type=jnp.float32) - jnp.dot(
        imag_part, sine_table, preferred_element_type=jnp.float32
    )
    out_imag = jnp.dot(imag_part, cosine_table, preferred_element_type=jnp.float32) + jnp.dot(
        real_part, sine_table, preferred_element_type=jnp.float32
    )
    return (out_real, out_imag)


def coil_spectra(field, sens_real, sens_imag, cosine_table, sine_table):
    coils, width, length = sens_real.shape
    coil_real = (
        (sens_real * field[0] - sens_imag * field[1])
        .astype(jnp.bfloat16)
        .reshape(coils * width, length)
    )
    coil_imag = (
        (sens_real * field[1] + sens_imag * field[0])
        .astype(jnp.bfloat16)
        .reshape(coils * width, length)
    )
    spec_real, spec_imag = forward(coil_real, coil_imag, cosine_table, sine_table)
    return (spec_real.reshape(coils, width, length), spec_imag.reshape(coils, width, length))


def frame_terms(field, sensitivity, data, lines, cosine_table, sine_table):
    sens_real = sensitivity[:, 0].astype(jnp.float32)
    sens_imag = sensitivity[:, 1].astype(jnp.float32)
    coils, width, length = sens_real.shape
    weight = lines.astype(jnp.float32)[:, None, :]
    spec_real, spec_imag = coil_spectra(field, sens_real, sens_imag, cosine_table, sine_table)
    misfit_real = (weight * (spec_real - data[:, 0].astype(jnp.float32))).astype(jnp.bfloat16)
    misfit_imag = (weight * (spec_imag - data[:, 1].astype(jnp.float32))).astype(jnp.bfloat16)
    back_real, back_imag = inverse(
        misfit_real.reshape(coils * width, length),
        misfit_imag.reshape(coils * width, length),
        cosine_table,
        sine_table,
    )
    back_real = back_real.reshape(coils, width, length)
    back_imag = back_imag.reshape(coils, width, length)
    grad_real = jnp.sum(sens_real * back_real + sens_imag * back_imag, axis=0)
    grad_imag = jnp.sum(sens_real * back_imag - sens_imag * back_real, axis=0)
    gradient = jnp.stack([grad_real, grad_imag])
    numerator = jnp.sum(gradient * gradient)
    probe_real, probe_imag = coil_spectra(gradient, sens_real, sens_imag, cosine_table, sine_table)
    denominator = jnp.sum(weight * (probe_real * probe_real + probe_imag * probe_imag))
    return (gradient, numerator, denominator)


def shrink(casorati):
    highest = lax.Precision.HIGHEST
    gram = jnp.einsum("bfv,bgv->bfg", casorati, casorati, precision=highest)
    frames = gram.shape[1]
    identity = jnp.eye(frames, dtype=jnp.float32)
    shrink_level = shrink_ratio * jnp.trace(gram, axis1=1, axis2=2) / frames + epsilon
    system = gram + shrink_level[:, None, None] * identity
    row_bound = jnp.max(jnp.sum(jnp.abs(system), axis=2), axis=1)
    approx = identity[None] / row_bound[:, None, None]
    for newton in range(NEWTON):
        product = jnp.einsum("bfg,bgh->bfh", system, approx, precision=highest)
        approx = jnp.einsum("bfg,bgh->bfh", approx, 2.0 * identity - product, precision=highest)
    return casorati - shrink_level[:, None, None] * jnp.einsum(
        "bfg,bgv->bfv", approx, casorati, precision=highest
    )


def to_blocks(field):
    frames, parts, width, length = field.shape
    blocks = field.reshape(frames, parts, width // BS, BS, length // BS, BS)
    blocks = blocks.transpose(2, 4, 0, 1, 3, 5)
    return blocks.reshape(width // BS * (length // BS), frames, parts * BS * BS)


def from_blocks(blocks, width, length):
    frames = blocks.shape[1]
    field = blocks.reshape(width // BS, length // BS, frames, 2, BS, BS)
    field = field.transpose(2, 3, 0, 4, 1, 5)
    return field.reshape(frames, 2, width, length)


def whole_body(start_image, sensitivity, kspace, sampled, offsets):
    width, length = (start_image.shape[2], start_image.shape[3])
    cosine_table, sine_table = dft_tables(length)
    estimate = start_image

    def per_frame(frame_items):
        field, data, lines = frame_items
        return frame_terms(field, sensitivity, data, lines, cosine_table, sine_table)

    for iteration in range(ITERS):
        gradient, numerator, denominator = lax.map(per_frame, (estimate, kspace, sampled))
        offset_pair = offsets[iteration]
        totals = lax.psum((jnp.sum(numerator), jnp.sum(denominator)), "tm")
        step_length = totals[0] / (totals[1] + epsilon)
        moved = estimate - step_length * gradient
        rolled = jnp.roll(moved, (offset_pair[0], offset_pair[1]), axis=(2, 3))
        casorati = lax.all_to_all(to_blocks(rolled), "tm", split_axis=0, concat_axis=1, tiled=True)
        shrunk = shrink(casorati)
        returned = lax.all_to_all(shrunk, "tm", split_axis=1, concat_axis=0, tiled=True)
        placed = from_blocks(returned, width, length)
        estimate = jnp.roll(placed, (-offset_pair[0], -offset_pair[1]), axis=(2, 3))
    return estimate


def block_of(column, shift, length):
    return lax.rem(column + shift, length) // BS


def iota(shape, dim):
    return lax.broadcasted_iota(jnp.int32, shape, dim)


def wide_tables(length):
    indices = np.arange(length, dtype=np.int32)
    phases = indices[:, None] * indices[None, :] % length
    angles = phases.astype(np.float32) * np.float32(2.0 * math.pi / length)
    norm_scale = np.float32(1.0 / math.sqrt(length))
    cosine = (np.cos(angles) * norm_scale).astype(ml_dtypes.bfloat16)
    sine = (np.sin(angles) * norm_scale).astype(ml_dtypes.bfloat16)
    ahead = np.block([[cosine, -sine], [sine, cosine]])
    back = np.block([[cosine, sine], [-sine, cosine]])
    return ahead, back


def pair_list(frames):
    return [(f, g) for f in range(frames) for g in range(f, frames)]


def pair_select(frames, lanes):
    table = np.zeros((frames * frames, lanes), np.float32)
    for place, (f, g) in enumerate(pair_list(frames)):
        table[f * frames + g, place] = 1.0
        table[g * frames + f, place] = 1.0
    return table


def exact_dot(a, b, dims=(((1,), (0,)), ((), ()))):
    return lax.dot_general(a, b, dims, precision=lax.Precision.HIGHEST, preferred_element_type=jnp.float32)


def mxu(a, b):
    return jnp.dot(a, b, preferred_element_type=jnp.float32)


def fold(x):
    rows, length = x.shape
    return jnp.sum(x.reshape(rows // 8, 8, length), axis=0)


def pack_kernel(offsets_ref, start_ref, lines_ref, out_ref):
    shift = offsets_ref[0, 0]
    strips = out_ref.shape[0]
    for part in range(2):
        rolled = pltpu.roll(start_ref[0, part], shift, 0)
        out_ref[:, part * BS : (part + 1) * BS, :] = rolled.reshape(strips, BS, rolled.shape[1])
    lines = lines_ref[0].astype(jnp.float32)
    coils = lines.shape[0]
    for strip in range(strips):
        out_ref[strip, 2 * BS : 2 * BS + coils, :] = lines


def frame_kernel(offsets_ref, start_ref, sens_ref, data_ref, lines_ref, ahead_ref, back_ref, out_ref, grad, num, den, left, right):
    step = pl.program_id(0)
    coils, _, rows, length = sens_ref.shape
    weight = lines_ref[0].astype(jnp.float32)

    @pl.when(step == 0)
    def _():
        num[...] = jnp.zeros_like(num)
        den[...] = jnp.zeros_like(den)

    def coil_image(a, b):
        for c in range(coils):
            sr = sens_ref[c, 0].astype(jnp.float32)
            si = sens_ref[c, 1].astype(jnp.float32)
            at = slice(c * rows, (c + 1) * rows)
            left[at, :length] = (sr * a - si * b).astype(jnp.bfloat16)
            left[at, length:] = (sr * b + si * a).astype(jnp.bfloat16)

    coil_image(start_ref[0, 0], start_ref[0, 1])
    spec = mxu(left[...], ahead_ref[...])
    for c in range(coils):
        at = slice(c * rows, (c + 1) * rows)
        w = weight[c : c + 1]
        right[at, :length] = (w * (spec[at, :length] - data_ref[0, c, 0].astype(jnp.float32))).astype(jnp.bfloat16)
        right[at, length:] = (w * (spec[at, length:] - data_ref[0, c, 1].astype(jnp.float32))).astype(jnp.bfloat16)
    home = mxu(right[...], back_ref[...])
    gr = jnp.zeros((rows, length), jnp.float32)
    gi = jnp.zeros((rows, length), jnp.float32)
    for c in range(coils):
        sr = sens_ref[c, 0].astype(jnp.float32)
        si = sens_ref[c, 1].astype(jnp.float32)
        at = slice(c * rows, (c + 1) * rows)
        br, bi = home[at, :length], home[at, length:]
        gr = gr + (sr * br + si * bi)
        gi = gi + (sr * bi - si * br)
    where = pl.ds(pl.multiple_of(step * rows, rows), rows)
    grad[0, where, :] = gr
    grad[1, where, :] = gi
    num[...] += fold(gr * gr + gi * gi)
    coil_image(gr, gi)
    probe = mxu(left[...], ahead_ref[...])
    total = jnp.zeros((8, length), jnp.float32)
    for c in range(coils):
        at = slice(c * rows, (c + 1) * rows)
        pr, pi = probe[at, :length], probe[at, length:]
        total = total + weight[c : c + 1] * fold(pr * pr + pi * pi)
    den[...] += total

    @pl.when(step == pl.num_programs(0) - 1)
    def _():
        shift = offsets_ref[0, 0]
        strips = out_ref.shape[0]
        for part in range(2):
            rolled = pltpu.roll(grad[part], shift, 0)
            out_ref[:, part * BS : (part + 1) * BS, :] = rolled.reshape(strips, BS, length)
        sums = jnp.where(
            iota((8, length), 0) == 0,
            jnp.sum(num[...], axis=0, keepdims=True),
            jnp.sum(den[...], axis=0, keepdims=True),
        )
        for strip in range(strips):
            out_ref[strip, 2 * BS : 2 * BS + 8, :] = sums


def strip_kernel(offsets_ref, sens_ref, out_ref, both, sems):
    axis = out_ref.shape
    coils, _, width, length = sens_ref.shape
    strips = width // BS
    me = lax.axis_index("tm")
    before = lax.rem(me + strips - 1, strips)
    first = pltpu.make_async_copy(
        sens_ref.at[:, :, pl.ds(pl.multiple_of(before * BS, BS), BS), :], both.at[0], sems.at[0]
    )
    second = pltpu.make_async_copy(
        sens_ref.at[:, :, pl.ds(pl.multiple_of(me * BS, BS), BS), :], both.at[1], sems.at[1]
    )
    first.start()
    second.start()
    first.wait()
    second.wait()
    shift = offsets_ref[0, 0]
    for c in range(coils):
        for part in range(2):
            rows = jnp.concatenate([both[0, c, part], both[1, c, part]], axis=0).astype(jnp.float32)
            out_ref[c, part] = pltpu.roll(rows, shift, 0)[BS:]


def newton_inverse(system, held, other, frames):
    lanes = system[0].shape[1]
    place = iota((frames, lanes), 0)
    unit = [(place == f).astype(jnp.float32) for f in range(frames)]
    sums = sum(jnp.abs(tile) for tile in system)
    bound = jnp.max(sums, axis=0, keepdims=True)
    for f in range(frames):
        held[f * frames : (f + 1) * frames, :] = system[f]
    approx = [unit[f] / bound for f in range(frames)]

    def times(ref, tiles):
        out = []
        for f in range(frames):
            terms = [ref[f * frames + g : f * frames + g + 1, :] * tiles[g] for g in range(frames)]
            while len(terms) > 1:
                terms = [a + b for a, b in zip(terms[::2], terms[1::2])]
            out.append(terms[0])
        return out

    for newton in range(NEWTON):
        for f in range(frames):
            other[f * frames : (f + 1) * frames, :] = approx[f]
        product = times(held, approx)
        approx = times(other, [2.0 * unit[f] - product[f] for f in range(frames)])
    return approx


def shrink_factors(gram, held, other, frames):
    lanes = gram.shape[1]
    place = iota((frames, lanes), 0)
    tiles = [gram[f * frames : (f + 1) * frames, :] for f in range(frames)]
    trace = sum(gram[f * frames + f : f * frames + f + 1, :] for f in range(frames))
    level = shrink_ratio * trace / frames + epsilon
    system = [tiles[f] + jnp.where(place == f, level, 0.0) for f in range(frames)]
    approx = newton_inverse(system, held, other, frames)
    return jnp.concatenate([level * tile for tile in approx], axis=0)


def middle_kernel(
    offsets_ref, image_ref, first_ref, sens_ref, ahead_ref, back_ref,
    out_ref, own_ref, est_ref, grad_ref,
    terms, held, other, spread, left, right,
):
    frames = image_ref.shape[0]
    coils, _, _, length = sens_ref.shape
    pairs = pair_list(frames)
    strip = 2 * BS
    numer = jnp.zeros((1, length), jnp.float32)
    denom = jnp.zeros((1, length), jnp.float32)
    for f in range(frames):
        numer = numer + first_ref[f, strip : strip + 1, :]
        denom = denom + first_ref[f, strip + 1 : strip + 2, :]
    numer = jnp.sum(numer, axis=1, keepdims=True)
    denom = jnp.sum(denom, axis=1, keepdims=True)
    step = numer / (denom + epsilon)
    for f in range(frames):
        est_ref[f] = image_ref[f, :strip, :] - step * first_ref[f, :strip, :]
    for f, g in pairs:
        tile = fold(est_ref[f] * est_ref[g])
        for place in {f * frames + g, g * frames + f}:
            for half in range(length // LANES):
                terms[half, place * 8 : place * 8 + 8, :] = tile[:, half * LANES : (half + 1) * LANES]
    count = frames * frames
    sums = jnp.concatenate(
        [sum(terms[half, pl.ds(s, count, stride=8), :] for s in range(8)) for half in range(length // LANES)], axis=1
    )
    shift = offsets_ref[0, 1]
    tall = (block_of(iota((length, LANES), 0), shift, length) == iota((length, LANES), 1)).astype(jnp.float32)
    broad = (block_of(iota((LANES, length), 1), shift, length) == iota((LANES, length), 0)).astype(jnp.float32)
    factors = shrink_factors(exact_dot(sums, tall), held, other, frames)
    spread[...] = exact_dot(factors, broad)
    moved = [est_ref[f] for f in range(frames)]
    for f in range(frames):
        total = spread[f * frames : f * frames + 1, :] * moved[0]
        for g in range(1, frames):
            total = total + spread[f * frames + g : f * frames + g + 1, :] * moved[g]
        grad_ref[f] = moved[f] - total
    for f in range(frames):
        est_ref[f] = grad_ref[f]

    num = jnp.zeros((8, length), jnp.float32)
    den = jnp.zeros((8, length), jnp.float32)
    group = left.shape[0] // (coils * BS)

    def coil_image(values):
        for k, (a, b) in enumerate(values):
            for c in range(coils):
                sr, si = sens_ref[c, 0], sens_ref[c, 1]
                at = slice((k * coils + c) * BS, (k * coils + c + 1) * BS)
                left[at, :length] = (sr * a - si * b).astype(jnp.bfloat16)
                left[at, length:] = (sr * b + si * a).astype(jnp.bfloat16)

    def passes(index, carry):
        num, den = carry
        at_frame = [index * group + k for k in range(group)]
        coil_image(
            [
                (
                    est_ref[f, :BS, :] - image_ref[f, :BS, :],
                    est_ref[f, BS:strip, :] - image_ref[f, BS:strip, :],
                )
                for f in at_frame
            ]
        )
        weights = [image_ref[f, strip : strip + coils, :] for f in at_frame]
        spec = mxu(left[...], ahead_ref[...])
        for k in range(group):
            for c in range(coils):
                at = slice((k * coils + c) * BS, (k * coils + c + 1) * BS)
                w = weights[k][c : c + 1]
                right[at, :length] = (w * spec[at, :length]).astype(jnp.bfloat16)
                right[at, length:] = (w * spec[at, length:]).astype(jnp.bfloat16)
        home = mxu(right[...], back_ref[...])
        values = []
        for k, f in enumerate(at_frame):
            gr = first_ref[f, :BS, :]
            gi = first_ref[f, BS:strip, :]
            for c in range(coils):
                at = slice((k * coils + c) * BS, (k * coils + c + 1) * BS)
                sr, si = sens_ref[c, 0], sens_ref[c, 1]
                br, bi = home[at, :length], home[at, length:]
                gr = gr + (sr * br + si * bi)
                gi = gi + (sr * bi - si * br)
            grad_ref[f, :BS, :] = gr
            grad_ref[f, BS:strip, :] = gi
            num = num + fold(gr * gr + gi * gi)
            values.append((gr, gi))
        coil_image(values)
        probe = mxu(left[...], ahead_ref[...])
        for k in range(group):
            for c in range(coils):
                at = slice((k * coils + c) * BS, (k * coils + c + 1) * BS)
                pr, pi = probe[at, :length], probe[at, length:]
                den = den + weights[k][c : c + 1] * fold(pr * pr + pi * pi)
        return num, den

    num, den = lax.fori_loop(0, frames // group, passes, (num, den))
    numer = jnp.sum(jnp.sum(num, axis=0, keepdims=True), axis=1, keepdims=True)
    denom = jnp.sum(jnp.sum(den, axis=0, keepdims=True), axis=1, keepdims=True)

    edge = lax.rem(offsets_ref[0, 0] - offsets_ref[1, 0] + BS, BS)
    low = [(iota((8, length), 0) + 8 * t >= edge) for t in range(BS // 8)]
    block = len(pairs)
    span = out_ref.shape[2]

    def rows_of(product):
        return [
            sum(product[p * BS + 8 * t : p * BS + 8 * t + 8] for p in range(2)) for t in range(BS // 8)
        ]

    def put(part, place, tile):
        for half in range(length // LANES):
            terms[half, (part * span + place) * 8 : (part * span + place) * 8 + 8, :] = tile[
                :, half * LANES : (half + 1) * LANES
            ]

    for part in range(2):
        for place in range(3 * block, span):
            put(part, place, jnp.zeros((8, length), jnp.float32))
    for place, (f, g) in enumerate(pairs):
        ef, eg, gf, gg = est_ref[f], est_ref[g], grad_ref[f], grad_ref[g]
        for kind, product in enumerate((ef * eg, ef * gg + eg * gf, gf * gg)):
            rows = rows_of(product)
            put(0, kind * block + place, sum(jnp.where(low[t], rows[t], 0.0) for t in range(BS // 8)))
            put(1, kind * block + place, sum(jnp.where(low[t], 0.0, rows[t]) for t in range(BS // 8)))
    shift = offsets_ref[1, 1]
    blocks = length // BS
    member = (block_of(iota((blocks, length), 1), shift, length) == iota((blocks, length), 0)).astype(jnp.float32)
    lane = iota((blocks, span), 1)
    packs = []
    for part in range(2):
        sums = jnp.concatenate(
            [
                sum(terms[half, pl.ds(part * span * 8 + s, span, stride=8), :] for s in range(8))
                for half in range(length // LANES)
            ],
            axis=1,
        )
        pack = exact_dot(member, sums, (((1,), (1,)), ((), ())))
        pack = jnp.where(lane == 3 * block, numer, jnp.where(lane == 3 * block + 1, denom, pack))
        own_ref[part * blocks : (part + 1) * blocks, :] = pack
        packs.append(pack)
    me = lax.axis_index("tm")
    strips = out_ref.shape[0]
    before = lax.rem(me + strips - 1, strips)
    for target in range(strips):
        out_ref[target] = jnp.where(before == target, packs[1], packs[0])


def last_kernel(offsets_ref, own_ref, heard_ref, est_ref, grad_ref, select_ref, out_ref, held, other, spread_low, spread_up):
    frames, strip, length = est_ref.shape
    strips, blocks, span = heard_ref.shape
    block = len(pair_list(frames))
    me = lax.axis_index("tm")
    numer = jnp.zeros((1, 1), jnp.float32)
    denom = jnp.zeros((1, 1), jnp.float32)
    for k in range(strips):
        numer = numer + heard_ref[k, 0:1, 3 * block : 3 * block + 1]
        denom = denom + heard_ref[k, 0:1, 3 * block + 1 : 3 * block + 2]
    step = numer / (denom + epsilon)
    after = lax.rem(me + 1, strips)
    before = lax.rem(me + strips - 1, strips)
    total = own_ref[...] + jnp.concatenate([heard_ref[after], heard_ref[before]], axis=0)
    cross = pltpu.roll(total, span - block, 1)
    square = pltpu.roll(total, span - 2 * block, 1)
    gram = total - step * cross + step * step * square
    gram = jnp.concatenate([gram, jnp.zeros((LANES - 2 * blocks, span), jnp.float32)], axis=0)
    gram = jnp.where(iota(gram.shape, 1) < block, gram, 0.0)
    gram = exact_dot(select_ref[...], gram, (((1,), (1,)), ((), ())))
    factors = shrink_factors(gram, held, other, frames)
    shift = offsets_ref[1, 1]
    column = block_of(iota((LANES, length), 1), shift, length)
    row = iota((LANES, length), 0)
    spread_low[...] = exact_dot(factors, (column == row).astype(jnp.float32))
    spread_up[...] = exact_dot(factors, (column + blocks == row).astype(jnp.float32))
    edge = lax.rem(offsets_ref[0, 0] - offsets_ref[1, 0] + BS, BS)
    moved = [est_ref[f] - step * grad_ref[f] for f in range(frames)]
    for t in range(BS // 8):
        low = iota((8, length), 0) + 8 * t >= edge
        for f in range(frames):
            total = [jnp.zeros((8, length), jnp.float32)] * 2
            for g in range(frames):
                at = f * frames + g
                factor = jnp.where(low, spread_low[at : at + 1, :], spread_up[at : at + 1, :])
                total = [total[p] + factor * moved[g][p * BS + 8 * t : p * BS + 8 * t + 8] for p in range(2)]
            for p in range(2):
                rows = slice(p * BS + 8 * t, p * BS + 8 * t + 8)
                out_ref[f, rows, :] = moved[f][rows] - total[p]


def place_kernel(offsets_ref, strips_ref, out_ref):
    strips, strip, length = strips_ref.shape
    width = strips * BS
    shift = lax.rem(width - offsets_ref[0, 0], width)
    for part in range(2):
        whole = strips_ref[:, part * BS : (part + 1) * BS, :].reshape(width, length)
        out_ref[0, part] = pltpu.roll(whole, shift, 0)


def vmem():
    return pl.BlockSpec(memory_space=pltpu.VMEM)


def smem():
    return pl.BlockSpec(memory_space=pltpu.SMEM)


def f32(*shape):
    return jax.ShapeDtypeStruct(shape, jnp.float32)


def exchange(blocks):
    return lax.all_to_all(blocks, "tm", split_axis=0, concat_axis=0, tiled=True)


def params():
    return pltpu.CompilerParams(vmem_limit_bytes=32 * 1024 * 1024)


def strips_body(start_image, sensitivity, kspace, sampled, offsets):
    _, _, width, length = start_image.shape
    coils = sensitivity.shape[0]
    strips = width // BS
    frames = strips
    ahead, back = (jnp.asarray(table) for table in wide_tables(length))
    strip = 2 * BS
    span = LANES
    blocks = length // BS

    packed = pl.pallas_call(
        pack_kernel,
        out_shape=f32(strips, strip + coils, length),
        in_specs=[smem(), vmem(), vmem()],
        out_specs=vmem(),
        compiler_params=params(),
        cost_estimate=pl.CostEstimate(flops=10**6, bytes_accessed=10**6, transcendentals=0),
    )(offsets, start_image, sampled)
    image = exchange(packed)

    rows = 2 * BS
    first = pl.pallas_call(
        frame_kernel,
        grid=(width // rows,),
        out_shape=f32(strips, strip + 8, length),
        in_specs=[
            smem(),
            pl.BlockSpec((1, 2, rows, length), lambda i: (0, 0, i, 0)),
            pl.BlockSpec((coils, 2, rows, length), lambda i: (0, 0, i, 0)),
            pl.BlockSpec((1, coils, 2, rows, length), lambda i: (0, 0, 0, i, 0)),
            pl.BlockSpec((1, coils, length), lambda i: (0, 0, 0)),
            vmem(),
            vmem(),
        ],
        out_specs=pl.BlockSpec((strips, strip + 8, length), lambda i: (0, 0, 0)),
        scratch_shapes=[
            pltpu.VMEM((2, width, length), jnp.float32),
            pltpu.VMEM((8, length), jnp.float32),
            pltpu.VMEM((8, length), jnp.float32),
            pltpu.VMEM((coils * rows, 2 * length), jnp.bfloat16),
            pltpu.VMEM((coils * rows, 2 * length), jnp.bfloat16),
        ],
        compiler_params=params(),
        cost_estimate=pl.CostEstimate(flops=24 * coils * width * length * length, bytes_accessed=4 * 10**6, transcendentals=0),
    )(offsets, start_image, sensitivity, kspace, sampled, ahead, back)
    first = exchange(first)

    sens = pl.pallas_call(
        strip_kernel,
        out_shape=f32(coils, 2, BS, length),
        in_specs=[smem(), pl.BlockSpec(memory_space=pl.ANY)],
        out_specs=vmem(),
        scratch_shapes=[pltpu.VMEM((2, coils, 2, BS, length), jnp.bfloat16), pltpu.SemaphoreType.DMA((2,))],
        compiler_params=params(),
        cost_estimate=pl.CostEstimate(flops=10**6, bytes_accessed=10**6, transcendentals=0),
    )(offsets, sensitivity)

    count = frames * frames
    group = 2
    sent, own, estimate, gradient = pl.pallas_call(
        middle_kernel,
        out_shape=(
            f32(strips, blocks, span),
            f32(2 * blocks, span),
            f32(frames, strip, length),
            f32(frames, strip, length),
        ),
        in_specs=[smem()] + [vmem()] * 5,
        out_specs=(vmem(),) * 4,
        scratch_shapes=[
            pltpu.VMEM((length // LANES, 2 * span * 8, LANES), jnp.float32),
            pltpu.VMEM((count, LANES), jnp.float32),
            pltpu.VMEM((count, LANES), jnp.float32),
            pltpu.VMEM((count, length), jnp.float32),
            pltpu.VMEM((group * coils * BS, 2 * length), jnp.bfloat16),
            pltpu.VMEM((group * coils * BS, 2 * length), jnp.bfloat16),
        ],
        compiler_params=params(),
        cost_estimate=pl.CostEstimate(flops=24 * coils * width * length * length, bytes_accessed=4 * 10**6, transcendentals=0),
    )(offsets, image, first, sens, ahead, back)
    heard = exchange(sent)

    returned = pl.pallas_call(
        last_kernel,
        out_shape=f32(frames, strip, length),
        in_specs=[smem()] + [vmem()] * 5,
        out_specs=vmem(),
        scratch_shapes=[
            pltpu.VMEM((count, LANES), jnp.float32),
            pltpu.VMEM((count, LANES), jnp.float32),
            pltpu.VMEM((count, length), jnp.float32),
            pltpu.VMEM((count, length), jnp.float32),
        ],
        compiler_params=params(),
    )(offsets, own, heard, estimate, gradient, jnp.asarray(pair_select(frames, span)))
    returned = exchange(returned)

    return pl.pallas_call(
        place_kernel,
        out_shape=f32(1, 2, width, length),
        in_specs=[smem(), vmem()],
        out_specs=vmem(),
        compiler_params=params(),
    )(offsets, returned)


def fits_strips(start_image, sensitivity, kspace, sampled, offsets):
    strips = lax.axis_size("tm")
    frames, _, width, length = start_image.shape
    coils = sensitivity.shape[0]
    kinds = 3 * len(pair_list(strips))
    return (
        frames == 1
        and width == strips * BS
        and strips == SUBLANES
        and coils % SUBLANES == 0
        and ITERS == 2
        and length % LANES == 0
        and 2 * (length // BS) <= LANES
        and kinds + 2 <= LANES
    )


def body(*args):
    return (strips_body if fits_strips(*args) else whole_body)(*args)


def solution(mesh):
    placed = (
        P(("cuts", "tm"), None, None, None),
        P("cuts", None, None, None),
        P(("cuts", "tm"), None, None, None, None),
        P(("cuts", "tm"), None, None),
        P("cuts", None),
    )
    return jax.shard_map(
        body,
        mesh=mesh,
        in_specs=placed,
        out_specs=P(("cuts", "tm"), None, None, None),
        check_vma=False,
    )
```

```python
import math

import jax
import jax.numpy as jnp
import ml_dtypes
import numpy as np
from jax import lax
from jax.experimental import pallas as pl
from jax.experimental.pallas import tpu as pltpu
from jax.sharding import PartitionSpec as P

BS = 16
ITERS = 2
NEWTON = 4
LANES = 128
SUBLANES = 8


shrink_ratio = 0.5
epsilon = 1e-06


def dft_tables(length):
    indices = jnp.arange(length, dtype=jnp.int32)
    phases = indices[:, None] * indices[None, :] % length
    angles = phases.astype(jnp.float32) * (2.0 * math.pi / length)
    norm_scale = 1.0 / math.sqrt(length)
    return (
        (jnp.cos(angles) * norm_scale).astype(jnp.bfloat16),
        (jnp.sin(angles) * norm_scale).astype(jnp.bfloat16),
    )


def forward(real_part, imag_part, cosine_table, sine_table):
    out_real = jnp.dot(real_part, cosine_table, preferred_element_type=jnp.float32) + jnp.dot(
        imag_part, sine_table, preferred_element_type=jnp.float32
    )
    out_imag = jnp.dot(imag_part, cosine_table, preferred_element_type=jnp.float32) - jnp.dot(
        real_part, sine_table, preferred_element_type=jnp.float32
    )
    return (out_real, out_imag)


def inverse(real_part, imag_part, cosine_table, sine_table):
    out_real = jnp.dot(real_part, cosine_table, preferred_element_type=jnp.float32) - jnp.dot(
        imag_part, sine_table, preferred_element_type=jnp.float32
    )
    out_imag = jnp.dot(imag_part, cosine_table, preferred_element_type=jnp.float32) + jnp.dot(
        real_part, sine_table, preferred_element_type=jnp.float32
    )
    return (out_real, out_imag)


def coil_spectra(field, sens_real, sens_imag, cosine_table, sine_table):
    coils, width, length = sens_real.shape
    coil_real = (
        (sens_real * field[0] - sens_imag * field[1])
        .astype(jnp.bfloat16)
        .reshape(coils * width, length)
    )
    coil_imag = (
        (sens_real * field[1] + sens_imag * field[0])
        .astype(jnp.bfloat16)
        .reshape(coils * width, length)
    )
    spec_real, spec_imag = forward(coil_real, coil_imag, cosine_table, sine_table)
    return (spec_real.reshape(coils, width, length), spec_imag.reshape(coils, width, length))


def frame_terms(field, sensitivity, data, lines, cosine_table, sine_table):
    sens_real = sensitivity[:, 0].astype(jnp.float32)
    sens_imag = sensitivity[:, 1].astype(jnp.float32)
    coils, width, length = sens_real.shape
    weight = lines.astype(jnp.float32)[:, None, :]
    spec_real, spec_imag = coil_spectra(field, sens_real, sens_imag, cosine_table, sine_table)
    misfit_real = (weight * (spec_real - data[:, 0].astype(jnp.float32))).astype(jnp.bfloat16)
    misfit_imag = (weight * (spec_imag - data[:, 1].astype(jnp.float32))).astype(jnp.bfloat16)
    back_real, back_imag = inverse(
        misfit_real.reshape(coils * width, length),
        misfit_imag.reshape(coils * width, length),
        cosine_table,
        sine_table,
    )
    back_real = back_real.reshape(coils, width, length)
    back_imag = back_imag.reshape(coils, width, length)
    grad_real = jnp.sum(sens_real * back_real + sens_imag * back_imag, axis=0)
    grad_imag = jnp.sum(sens_real * back_imag - sens_imag * back_real, axis=0)
    gradient = jnp.stack([grad_real, grad_imag])
    numerator = jnp.sum(gradient * gradient)
    probe_real, probe_imag = coil_spectra(gradient, sens_real, sens_imag, cosine_table, sine_table)
    denominator = jnp.sum(weight * (probe_real * probe_real + probe_imag * probe_imag))
    return (gradient, numerator, denominator)


def shrink(casorati):
    highest = lax.Precision.HIGHEST
    gram = jnp.einsum("bfv,bgv->bfg", casorati, casorati, precision=highest)
    frames = gram.shape[1]
    identity = jnp.eye(frames, dtype=jnp.float32)
    shrink_level = shrink_ratio * jnp.trace(gram, axis1=1, axis2=2) / frames + epsilon
    system = gram + shrink_level[:, None, None] * identity
    row_bound = jnp.max(jnp.sum(jnp.abs(system), axis=2), axis=1)
    approx = identity[None] / row_bound[:, None, None]
    for newton in range(NEWTON):
        product = jnp.einsum("bfg,bgh->bfh", system, approx, precision=highest)
        approx = jnp.einsum("bfg,bgh->bfh", approx, 2.0 * identity - product, precision=highest)
    return casorati - shrink_level[:, None, None] * jnp.einsum(
        "bfg,bgv->bfv", approx, casorati, precision=highest
    )


def to_blocks(field):
    frames, parts, width, length = field.shape
    blocks = field.reshape(frames, parts, width // BS, BS, length // BS, BS)
    blocks = blocks.transpose(2, 4, 0, 1, 3, 5)
    return blocks.reshape(width // BS * (length // BS), frames, parts * BS * BS)


def from_blocks(blocks, width, length):
    frames = blocks.shape[1]
    field = blocks.reshape(width // BS, length // BS, frames, 2, BS, BS)
    field = field.transpose(2, 3, 0, 4, 1, 5)
    return field.reshape(frames, 2, width, length)


def whole_body(start_image, sensitivity, kspace, sampled, offsets):
    width, length = (start_image.shape[2], start_image.shape[3])
    cosine_table, sine_table = dft_tables(length)
    estimate = start_image

    def per_frame(frame_items):
        field, data, lines = frame_items
        return frame_terms(field, sensitivity, data, lines, cosine_table, sine_table)

    for iteration in range(ITERS):
        gradient, numerator, denominator = lax.map(per_frame, (estimate, kspace, sampled))
        offset_pair = offsets[iteration]
        totals = lax.psum((jnp.sum(numerator), jnp.sum(denominator)), "tm")
        step_length = totals[0] / (totals[1] + epsilon)
        moved = estimate - step_length * gradient
        rolled = jnp.roll(moved, (offset_pair[0], offset_pair[1]), axis=(2, 3))
        casorati = lax.all_to_all(to_blocks(rolled), "tm", split_axis=0, concat_axis=1, tiled=True)
        shrunk = shrink(casorati)
        returned = lax.all_to_all(shrunk, "tm", split_axis=1, concat_axis=0, tiled=True)
        placed = from_blocks(returned, width, length)
        estimate = jnp.roll(placed, (-offset_pair[0], -offset_pair[1]), axis=(2, 3))
    return estimate


def block_of(column, shift, length):
    return lax.rem(column + shift, length) // BS


def iota(shape, dim):
    return lax.broadcasted_iota(jnp.int32, shape, dim)


def wide_table(length):
    indices = np.arange(length, dtype=np.int32)
    phases = indices[:, None] * indices[None, :] % length
    angles = phases.astype(np.float32) * np.float32(2.0 * math.pi / length)
    norm_scale = np.float32(1.0 / math.sqrt(length))
    cosine = (np.cos(angles) * norm_scale).astype(ml_dtypes.bfloat16)
    sine = (np.sin(angles) * norm_scale).astype(ml_dtypes.bfloat16)
    return np.block([[cosine, -sine], [sine, cosine]])


def pair_list(frames):
    return [(f, g) for f in range(frames) for g in range(f, frames)]


def pair_select(frames, lanes):
    table = np.zeros((frames * frames, lanes), np.float32)
    for place, (f, g) in enumerate(pair_list(frames)):
        table[f * frames + g, place] = 1.0
        table[g * frames + f, place] = 1.0
    return table


def exact_dot(a, b, dims=(((1,), (0,)), ((), ()))):
    return lax.dot_general(a, b, dims, precision=lax.Precision.HIGHEST, preferred_element_type=jnp.float32)


def mxu(a, b):
    return jnp.dot(a, b, preferred_element_type=jnp.float32)


def fold(x):
    rows, length = x.shape
    return jnp.sum(x.reshape(rows // 8, 8, length), axis=0)


def frame_kernel(
    offsets_hbm, start_hbm, sens_hbm, data_hbm, lines_hbm, table_hbm, out_ref,
    offsets_ref, start_ref, sens_ref, data_ref, lines_ref, table_ref, grad, left, right, sems, chunk_sems,
):
    chunks, coils, _, rows, length = sens_ref.shape
    start_copy, lines_copy, table_copy, offsets_copy = (
        pltpu.make_async_copy(source, target, sems.at[k])
        for k, (source, target) in enumerate(
            ((start_hbm, start_ref), (lines_hbm, lines_ref), (table_hbm, table_ref), (offsets_hbm, offsets_ref))
        )
    )
    sens_copy = [
        pltpu.make_async_copy(sens_hbm.at[:, :, pl.ds(i * rows, rows), :], sens_ref.at[i], chunk_sems.at[0, i])
        for i in range(chunks)
    ]
    data_copy = [
        pltpu.make_async_copy(data_hbm.at[0, :, :, pl.ds(i * rows, rows), :], data_ref.at[i], chunk_sems.at[1, i])
        for i in range(chunks)
    ]
    start_copy.start()
    sens_copy[0].start()
    table_copy.start()
    data_copy[0].start()
    lines_copy.start()
    offsets_copy.start()
    for i in range(1, chunks):
        sens_copy[i].start()
        data_copy[i].start()
    num = jnp.zeros((8, length), jnp.float32)
    den = jnp.zeros((8, length), jnp.float32)

    def coil_image(i, a, b):
        for c in range(coils):
            sr = sens_ref[i, c, 0].astype(jnp.float32)
            si = sens_ref[i, c, 1].astype(jnp.float32)
            at = slice(c * rows, (c + 1) * rows)
            left[i, at, :length] = (sr * a - si * b).astype(jnp.bfloat16)
            left[i, at, length:] = (sr * b + si * a).astype(jnp.bfloat16)

    start_copy.wait()
    for i in range(chunks):
        place = slice(i * rows, (i + 1) * rows)
        sens_copy[i].wait()
        coil_image(i, start_ref[0, 0, place], start_ref[0, 1, place])
        if i == 0:
            table_copy.wait()
        spec = mxu(left[i], table_ref[...])
        if i == 0:
            lines_copy.wait()
        weight = lines_ref[0].astype(jnp.float32)
        data_copy[i].wait()
        for c in range(coils):
            at = slice(c * rows, (c + 1) * rows)
            w = weight[c : c + 1]
            right[i, at, :length] = (w * (spec[at, :length] - data_ref[i, c, 0].astype(jnp.float32))).astype(jnp.bfloat16)
            right[i, at, length:] = (w * (data_ref[i, c, 1].astype(jnp.float32) - spec[at, length:])).astype(jnp.bfloat16)
        home = mxu(right[i], table_ref[...])
        gr = jnp.zeros((rows, length), jnp.float32)
        gi = jnp.zeros((rows, length), jnp.float32)
        for c in range(coils):
            sr = sens_ref[i, c, 0].astype(jnp.float32)
            si = sens_ref[i, c, 1].astype(jnp.float32)
            at = slice(c * rows, (c + 1) * rows)
            br, bi = home[at, :length], home[at, length:]
            gr = gr + (sr * br - si * bi)
            gi = gi - (sr * bi + si * br)
        grad[0, place, :] = gr
        grad[1, place, :] = gi
        num = num + fold(gr * gr + gi * gi)
        coil_image(i, gr, gi)
        probe = mxu(left[i], table_ref[...])
        for c in range(coils):
            at = slice(c * rows, (c + 1) * rows)
            pr, pi = probe[at, :length], probe[at, length:]
            den = den + weight[c : c + 1] * fold(pr * pr + pi * pi)

    strips = out_ref.shape[0]
    halves = length // LANES
    strip = 2 * BS
    weight = lines_ref[0].astype(jnp.float32)
    numer = jnp.sum(jnp.sum(num, axis=0, keepdims=True), axis=1, keepdims=True)
    denom = jnp.sum(jnp.sum(den, axis=0, keepdims=True), axis=1, keepdims=True)
    sums = jnp.where(iota((8, LANES), 0) == 0, numer, denom)
    offsets_copy.wait()
    shift = offsets_ref[0, 0]
    for kind, image in enumerate((start_ref.at[0], grad)):
        for part in range(2):
            rolled = pltpu.roll(image[part], shift, 0)
            for half in range(halves):
                base = (kind * halves + half) * strip + part * BS
                out_ref[:, base : base + BS, :] = rolled[:, half * LANES : (half + 1) * LANES].reshape(strips, BS, LANES)
    for target in range(strips):
        for half in range(halves):
            base = 2 * halves * strip + half * coils
            out_ref[target, base : base + coils, :] = weight[:, half * LANES : (half + 1) * LANES]
        base = 2 * halves * strip + halves * coils
        out_ref[target, base : base + 8, :] = sums


def strip_kernel(offsets_ref, sens_ref, out_ref, both, sems):
    coils, _, width, length = sens_ref.shape
    strips = width // BS
    me = lax.axis_index("tm")
    before = lax.rem(me + strips - 1, strips)
    first = pltpu.make_async_copy(
        sens_ref.at[:, :, pl.ds(pl.multiple_of(before * BS, BS), BS), :], both.at[0], sems.at[0]
    )
    second = pltpu.make_async_copy(
        sens_ref.at[:, :, pl.ds(pl.multiple_of(me * BS, BS), BS), :], both.at[1], sems.at[1]
    )
    first.start()
    second.start()
    first.wait()
    second.wait()
    shift = offsets_ref[0, 0]
    for c in range(coils):
        for part in range(2):
            rows = jnp.concatenate([both[0, c, part], both[1, c, part]], axis=0).astype(jnp.float32)
            out_ref[c, part] = pltpu.roll(rows, shift, 0)[BS:]


def newton_inverse(system, held, other, frames):
    lanes = system[0].shape[1]
    place = iota((frames, lanes), 0)
    unit = [(place == f).astype(jnp.float32) for f in range(frames)]
    sums = sum(jnp.abs(tile) for tile in system)
    bound = jnp.max(sums, axis=0, keepdims=True)
    for f in range(frames):
        held[f * frames : (f + 1) * frames, :] = system[f]
    approx = [unit[f] / bound for f in range(frames)]

    def times(ref, tiles):
        out = []
        for f in range(frames):
            terms = [ref[f * frames + g : f * frames + g + 1, :] * tiles[g] for g in range(frames)]
            while len(terms) > 1:
                terms = [a + b for a, b in zip(terms[::2], terms[1::2])]
            out.append(terms[0])
        return out

    for newton in range(NEWTON):
        for f in range(frames):
            other[f * frames : (f + 1) * frames, :] = approx[f]
        product = times(held, approx)
        approx = times(other, [2.0 * unit[f] - product[f] for f in range(frames)])
    return approx


def shrink_factors(gram, held, other, frames):
    lanes = gram.shape[1]
    place = iota((frames, lanes), 0)
    tiles = [gram[f * frames : (f + 1) * frames, :] for f in range(frames)]
    trace = sum(gram[f * frames + f : f * frames + f + 1, :] for f in range(frames))
    level = shrink_ratio * trace / frames + epsilon
    system = [tiles[f] + jnp.where(place == f, level, 0.0) for f in range(frames)]
    approx = newton_inverse(system, held, other, frames)
    return jnp.concatenate([level * tile for tile in approx], axis=0)


def middle_kernel(
    offsets_ref, mail_ref, sens_ref, table_ref,
    out_ref, own_ref, est_ref, grad_ref,
    terms, held, other, spread, left, right,
):
    frames = mail_ref.shape[0]
    coils, _, _, length = sens_ref.shape
    pairs = pair_list(frames)
    strip = 2 * BS
    halves = length // LANES

    def mail(f, kind, first, rows):
        return jnp.concatenate(
            [
                mail_ref[f, (kind * halves + half) * strip + first : (kind * halves + half) * strip + first + rows, :]
                for half in range(halves)
            ],
            axis=1,
        )

    def mask(f):
        base = 2 * halves * strip
        return jnp.concatenate(
            [mail_ref[f, base + half * coils : base + (half + 1) * coils, :] for half in range(halves)], axis=1
        )

    place = 2 * halves * strip + halves * coils
    numer = sum(mail_ref[f, place : place + 1, :1] for f in range(frames))
    denom = sum(mail_ref[f, place + 1 : place + 2, :1] for f in range(frames))
    step = numer / (denom + epsilon)
    for f in range(frames):
        est_ref[f] = mail(f, 0, 0, strip) - step * mail(f, 1, 0, strip)
    for f, g in pairs:
        tile = fold(est_ref[f] * est_ref[g])
        for place in {f * frames + g, g * frames + f}:
            for half in range(length // LANES):
                terms[half, place * 8 : place * 8 + 8, :] = tile[:, half * LANES : (half + 1) * LANES]
    count = frames * frames
    sums = jnp.concatenate(
        [sum(terms[half, pl.ds(s, count, stride=8), :] for s in range(8)) for half in range(length // LANES)], axis=1
    )
    shift = offsets_ref[0, 1]
    tall = (block_of(iota((length, LANES), 0), shift, length) == iota((length, LANES), 1)).astype(jnp.float32)
    broad = (block_of(iota((LANES, length), 1), shift, length) == iota((LANES, length), 0)).astype(jnp.float32)
    factors = shrink_factors(exact_dot(sums, tall), held, other, frames)
    spread[...] = exact_dot(factors, broad)
    moved = [est_ref[f] for f in range(frames)]
    for f in range(frames):
        total = spread[f * frames : f * frames + 1, :] * moved[0]
        for g in range(1, frames):
            total = total + spread[f * frames + g : f * frames + g + 1, :] * moved[g]
        grad_ref[f] = moved[f] - total
    for f in range(frames):
        est_ref[f] = grad_ref[f]

    num = jnp.zeros((8, length), jnp.float32)
    den = jnp.zeros((8, length), jnp.float32)
    group = left.shape[1] // (coils * BS)

    def coil_image(index, values):
        for k, (a, b) in enumerate(values):
            for c in range(coils):
                sr, si = sens_ref[c, 0], sens_ref[c, 1]
                at = slice((k * coils + c) * BS, (k * coils + c + 1) * BS)
                left[index, at, :length] = (sr * a - si * b).astype(jnp.bfloat16)
                left[index, at, length:] = (sr * b + si * a).astype(jnp.bfloat16)

    def passes(index, carry):
        num, den = carry
        at_frame = [index * group + k for k in range(group)]
        coil_image(
            index,
            [
                (est_ref[f, :BS, :] - mail(f, 0, 0, BS), est_ref[f, BS:strip, :] - mail(f, 0, BS, BS))
                for f in at_frame
            ],
        )
        weights = [mask(f) for f in at_frame]
        spec = mxu(left[index], table_ref[...])
        for k in range(group):
            for c in range(coils):
                at = slice((k * coils + c) * BS, (k * coils + c + 1) * BS)
                w = weights[k][c : c + 1]
                right[index, at, :length] = (w * spec[at, :length]).astype(jnp.bfloat16)
                right[index, at, length:] = (-w * spec[at, length:]).astype(jnp.bfloat16)
        home = mxu(right[index], table_ref[...])
        values = []
        for k, f in enumerate(at_frame):
            gr = mail(f, 1, 0, BS)
            gi = mail(f, 1, BS, BS)
            for c in range(coils):
                at = slice((k * coils + c) * BS, (k * coils + c + 1) * BS)
                sr, si = sens_ref[c, 0], sens_ref[c, 1]
                br, bi = home[at, :length], home[at, length:]
                gr = gr + (sr * br - si * bi)
                gi = gi - (sr * bi + si * br)
            grad_ref[f, :BS, :] = gr
            grad_ref[f, BS:strip, :] = gi
            num = num + fold(gr * gr + gi * gi)
            values.append((gr, gi))
        coil_image(index, values)
        probe = mxu(left[index], table_ref[...])
        for k in range(group):
            for c in range(coils):
                at = slice((k * coils + c) * BS, (k * coils + c + 1) * BS)
                pr, pi = probe[at, :length], probe[at, length:]
                den = den + weights[k][c : c + 1] * fold(pr * pr + pi * pi)
        return num, den

    for index in range(frames // group):
        num, den = passes(index, (num, den))
    numer = jnp.sum(jnp.sum(num, axis=0, keepdims=True), axis=1, keepdims=True)
    denom = jnp.sum(jnp.sum(den, axis=0, keepdims=True), axis=1, keepdims=True)

    edge = lax.rem(offsets_ref[0, 0] - offsets_ref[1, 0] + BS, BS)
    low = [(iota((8, length), 0) + 8 * t >= edge) for t in range(BS // 8)]
    block = len(pairs)
    span = out_ref.shape[2]

    def rows_of(product):
        return [
            sum(product[p * BS + 8 * t : p * BS + 8 * t + 8] for p in range(2)) for t in range(BS // 8)
        ]

    def put(part, place, tile):
        for half in range(length // LANES):
            terms[half, (part * span + place) * 8 : (part * span + place) * 8 + 8, :] = tile[
                :, half * LANES : (half + 1) * LANES
            ]

    for part in range(2):
        for place in range(3 * block, span):
            put(part, place, jnp.zeros((8, length), jnp.float32))
    for place, (f, g) in enumerate(pairs):
        ef, eg, gf, gg = est_ref[f], est_ref[g], grad_ref[f], grad_ref[g]
        for kind, product in enumerate((ef * eg, ef * gg + eg * gf, gf * gg)):
            rows = rows_of(product)
            put(0, kind * block + place, sum(jnp.where(low[t], rows[t], 0.0) for t in range(BS // 8)))
            put(1, kind * block + place, sum(jnp.where(low[t], 0.0, rows[t]) for t in range(BS // 8)))
    shift = offsets_ref[1, 1]
    blocks = length // BS
    member = (block_of(iota((blocks, length), 1), shift, length) == iota((blocks, length), 0)).astype(jnp.float32)
    lane = iota((blocks, span), 1)
    packs = []
    for part in range(2):
        sums = jnp.concatenate(
            [
                sum(terms[half, pl.ds(part * span * 8 + s, span, stride=8), :] for s in range(8))
                for half in range(length // LANES)
            ],
            axis=1,
        )
        pack = exact_dot(member, sums, (((1,), (1,)), ((), ())))
        pack = jnp.where(lane == 3 * block, numer, jnp.where(lane == 3 * block + 1, denom, pack))
        own_ref[part * blocks : (part + 1) * blocks, :] = pack
        packs.append(pack)
    me = lax.axis_index("tm")
    strips = out_ref.shape[0]
    before = lax.rem(me + strips - 1, strips)
    for target in range(strips):
        out_ref[target] = jnp.where(before == target, packs[1], packs[0])


def last_kernel(offsets_ref, own_ref, heard_ref, est_ref, grad_ref, select_ref, out_ref, held, other, spread_low, spread_up):
    frames, strip, length = est_ref.shape
    strips, blocks, span = heard_ref.shape
    block = len(pair_list(frames))
    me = lax.axis_index("tm")
    numer = jnp.zeros((1, 1), jnp.float32)
    denom = jnp.zeros((1, 1), jnp.float32)
    for k in range(strips):
        numer = numer + heard_ref[k, 0:1, 3 * block : 3 * block + 1]
        denom = denom + heard_ref[k, 0:1, 3 * block + 1 : 3 * block + 2]
    step = numer / (denom + epsilon)
    after = lax.rem(me + 1, strips)
    before = lax.rem(me + strips - 1, strips)
    total = own_ref[...] + jnp.concatenate([heard_ref[after], heard_ref[before]], axis=0)
    cross = pltpu.roll(total, span - block, 1)
    square = pltpu.roll(total, span - 2 * block, 1)
    gram = total - step * cross + step * step * square
    gram = jnp.concatenate([gram, jnp.zeros((LANES - 2 * blocks, span), jnp.float32)], axis=0)
    gram = jnp.where(iota(gram.shape, 1) < block, gram, 0.0)
    gram = exact_dot(select_ref[...], gram, (((1,), (1,)), ((), ())))
    factors = shrink_factors(gram, held, other, frames)
    shift = offsets_ref[1, 1]
    column = block_of(iota((LANES, length), 1), shift, length)
    row = iota((LANES, length), 0)
    spread_low[...] = exact_dot(factors, (column == row).astype(jnp.float32))
    spread_up[...] = exact_dot(factors, (column + blocks == row).astype(jnp.float32))
    edge = lax.rem(offsets_ref[0, 0] - offsets_ref[1, 0] + BS, BS)
    moved = [est_ref[f] - step * grad_ref[f] for f in range(frames)]
    for t in range(BS // 8):
        low = iota((8, length), 0) + 8 * t >= edge
        for f in range(frames):
            total = [jnp.zeros((8, length), jnp.float32)] * 2
            for g in range(frames):
                at = f * frames + g
                factor = jnp.where(low, spread_low[at : at + 1, :], spread_up[at : at + 1, :])
                total = [total[p] + factor * moved[g][p * BS + 8 * t : p * BS + 8 * t + 8] for p in range(2)]
            for p in range(2):
                rows = slice(p * BS + 8 * t, p * BS + 8 * t + 8)
                out_ref[f, rows, :] = moved[f][rows] - total[p]


def place_kernel(offsets_ref, strips_ref, out_ref):
    strips, strip, length = strips_ref.shape
    width = strips * BS
    shift = lax.rem(width - offsets_ref[0, 0], width)
    for part in range(2):
        whole = strips_ref[:, part * BS : (part + 1) * BS, :].reshape(width, length)
        out_ref[0, part] = pltpu.roll(whole, shift, 0)


def vmem():
    return pl.BlockSpec(memory_space=pltpu.VMEM)


def hbm():
    return pl.BlockSpec(memory_space=pltpu.HBM)


def smem():
    return pl.BlockSpec(memory_space=pltpu.SMEM)


def f32(*shape):
    return jax.ShapeDtypeStruct(shape, jnp.float32)


def exchange(blocks):
    return lax.all_to_all(blocks, "tm", split_axis=0, concat_axis=0, tiled=True)


def params(mebibytes=16):
    return pltpu.CompilerParams(vmem_limit_bytes=mebibytes * 1024 * 1024)


def strips_body(start_image, sensitivity, kspace, sampled, offsets):
    _, _, width, length = start_image.shape
    coils = sensitivity.shape[0]
    strips = width // BS
    frames = strips
    table = jnp.asarray(wide_table(length))
    strip = 2 * BS
    span = LANES
    blocks = length // BS
    halves = length // LANES

    rows = 2 * BS
    chunks = width // rows
    mail = pl.pallas_call(
        frame_kernel,
        out_shape=f32(strips, halves * (2 * strip + coils) + 8, LANES),
        in_specs=[hbm()] * 6,
        out_specs=vmem(),
        scratch_shapes=[
            pltpu.SMEM(offsets.shape, jnp.int32),
            pltpu.VMEM(start_image.shape, jnp.float32),
            pltpu.VMEM((chunks, coils, 2, rows, length), jnp.bfloat16),
            pltpu.VMEM((chunks, coils, 2, rows, length), jnp.bfloat16),
            pltpu.VMEM(sampled.shape, jnp.int32),
            pltpu.VMEM(table.shape, jnp.bfloat16),
            pltpu.VMEM((2, width, length), jnp.float32),
            pltpu.VMEM((chunks, coils * rows, 2 * length), jnp.bfloat16),
            pltpu.VMEM((chunks, coils * rows, 2 * length), jnp.bfloat16),
            pltpu.SemaphoreType.DMA((4,)),
            pltpu.SemaphoreType.DMA((2, chunks)),
        ],
        compiler_params=params(60),
        cost_estimate=pl.CostEstimate(flops=24 * coils * width * length * length, bytes_accessed=4 * 10**6, transcendentals=0),
    )(offsets, start_image, sensitivity, kspace, sampled, table)
    mail = exchange(mail)

    sens = pl.pallas_call(
        strip_kernel,
        out_shape=f32(coils, 2, BS, length),
        in_specs=[smem(), hbm()],
        out_specs=vmem(),
        scratch_shapes=[pltpu.VMEM((2, coils, 2, BS, length), jnp.bfloat16), pltpu.SemaphoreType.DMA((2,))],
        compiler_params=params(),
        cost_estimate=pl.CostEstimate(flops=10**6, bytes_accessed=10**6, transcendentals=0),
    )(offsets, sensitivity)

    count = frames * frames
    group = 2
    sent, own, estimate, gradient = pl.pallas_call(
        middle_kernel,
        out_shape=(
            f32(strips, blocks, span),
            f32(2 * blocks, span),
            f32(frames, strip, length),
            f32(frames, strip, length),
        ),
        in_specs=[smem()] + [vmem()] * 3,
        out_specs=(vmem(),) * 4,
        scratch_shapes=[
            pltpu.VMEM((length // LANES, 2 * span * 8, LANES), jnp.float32),
            pltpu.VMEM((count, LANES), jnp.float32),
            pltpu.VMEM((count, LANES), jnp.float32),
            pltpu.VMEM((count, length), jnp.float32),
            pltpu.VMEM((frames // group, group * coils * BS, 2 * length), jnp.bfloat16),
            pltpu.VMEM((frames // group, group * coils * BS, 2 * length), jnp.bfloat16),
        ],
        compiler_params=params(),
        cost_estimate=pl.CostEstimate(flops=24 * coils * width * length * length, bytes_accessed=4 * 10**6, transcendentals=0),
    )(offsets, mail, sens, table)
    heard = exchange(sent)

    returned = pl.pallas_call(
        last_kernel,
        out_shape=f32(frames, strip, length),
        in_specs=[smem()] + [vmem()] * 5,
        out_specs=vmem(),
        scratch_shapes=[
            pltpu.VMEM((count, LANES), jnp.float32),
            pltpu.VMEM((count, LANES), jnp.float32),
            pltpu.VMEM((count, length), jnp.float32),
            pltpu.VMEM((count, length), jnp.float32),
        ],
        compiler_params=params(),
    )(offsets, own, heard, estimate, gradient, jnp.asarray(pair_select(frames, span)))
    returned = exchange(returned)

    return pl.pallas_call(
        place_kernel,
        out_shape=f32(1, 2, width, length),
        in_specs=[smem(), vmem()],
        out_specs=vmem(),
        compiler_params=params(),
    )(offsets, returned)


def fits_strips(start_image, sensitivity, kspace, sampled, offsets):
    strips = lax.axis_size("tm")
    frames, _, width, length = start_image.shape
    coils = sensitivity.shape[0]
    kinds = 3 * len(pair_list(strips))
    return (
        frames == 1
        and width == strips * BS
        and strips == SUBLANES
        and coils % SUBLANES == 0
        and ITERS == 2
        and length % LANES == 0
        and 2 * (length // BS) <= LANES
        and kinds + 2 <= LANES
    )


def body(*args):
    return (strips_body if fits_strips(*args) else whole_body)(*args)


def solution(mesh):
    placed = (
        P(("cuts", "tm"), None, None, None),
        P("cuts", None, None, None),
        P(("cuts", "tm"), None, None, None, None),
        P(("cuts", "tm"), None, None),
        P("cuts", None),
    )
    return jax.shard_map(
        body,
        mesh=mesh,
        in_specs=placed,
        out_specs=P(("cuts", "tm"), None, None, None),
        check_vma=False,
    )
```

```python
import math

import jax
import jax.numpy as jnp
import ml_dtypes
import numpy as np
from jax import lax
from jax.experimental import pallas as pl
from jax.experimental.pallas import tpu as pltpu
from jax.sharding import PartitionSpec as P

BS = 16
ITERS = 2
NEWTON = 4
LANES = 128
SUBLANES = 8


shrink_ratio = 0.5
epsilon = 1e-06


def dft_tables(length):
    indices = jnp.arange(length, dtype=jnp.int32)
    phases = indices[:, None] * indices[None, :] % length
    angles = phases.astype(jnp.float32) * (2.0 * math.pi / length)
    norm_scale = 1.0 / math.sqrt(length)
    return (
        (jnp.cos(angles) * norm_scale).astype(jnp.bfloat16),
        (jnp.sin(angles) * norm_scale).astype(jnp.bfloat16),
    )


def forward(real_part, imag_part, cosine_table, sine_table):
    out_real = jnp.dot(real_part, cosine_table, preferred_element_type=jnp.float32) + jnp.dot(
        imag_part, sine_table, preferred_element_type=jnp.float32
    )
    out_imag = jnp.dot(imag_part, cosine_table, preferred_element_type=jnp.float32) - jnp.dot(
        real_part, sine_table, preferred_element_type=jnp.float32
    )
    return (out_real, out_imag)


def inverse(real_part, imag_part, cosine_table, sine_table):
    out_real = jnp.dot(real_part, cosine_table, preferred_element_type=jnp.float32) - jnp.dot(
        imag_part, sine_table, preferred_element_type=jnp.float32
    )
    out_imag = jnp.dot(imag_part, cosine_table, preferred_element_type=jnp.float32) + jnp.dot(
        real_part, sine_table, preferred_element_type=jnp.float32
    )
    return (out_real, out_imag)


def coil_spectra(field, sens_real, sens_imag, cosine_table, sine_table):
    coils, width, length = sens_real.shape
    coil_real = (
        (sens_real * field[0] - sens_imag * field[1])
        .astype(jnp.bfloat16)
        .reshape(coils * width, length)
    )
    coil_imag = (
        (sens_real * field[1] + sens_imag * field[0])
        .astype(jnp.bfloat16)
        .reshape(coils * width, length)
    )
    spec_real, spec_imag = forward(coil_real, coil_imag, cosine_table, sine_table)
    return (spec_real.reshape(coils, width, length), spec_imag.reshape(coils, width, length))


def frame_terms(field, sensitivity, data, lines, cosine_table, sine_table):
    sens_real = sensitivity[:, 0].astype(jnp.float32)
    sens_imag = sensitivity[:, 1].astype(jnp.float32)
    coils, width, length = sens_real.shape
    weight = lines.astype(jnp.float32)[:, None, :]
    spec_real, spec_imag = coil_spectra(field, sens_real, sens_imag, cosine_table, sine_table)
    misfit_real = (weight * (spec_real - data[:, 0].astype(jnp.float32))).astype(jnp.bfloat16)
    misfit_imag = (weight * (spec_imag - data[:, 1].astype(jnp.float32))).astype(jnp.bfloat16)
    back_real, back_imag = inverse(
        misfit_real.reshape(coils * width, length),
        misfit_imag.reshape(coils * width, length),
        cosine_table,
        sine_table,
    )
    back_real = back_real.reshape(coils, width, length)
    back_imag = back_imag.reshape(coils, width, length)
    grad_real = jnp.sum(sens_real * back_real + sens_imag * back_imag, axis=0)
    grad_imag = jnp.sum(sens_real * back_imag - sens_imag * back_real, axis=0)
    gradient = jnp.stack([grad_real, grad_imag])
    numerator = jnp.sum(gradient * gradient)
    probe_real, probe_imag = coil_spectra(gradient, sens_real, sens_imag, cosine_table, sine_table)
    denominator = jnp.sum(weight * (probe_real * probe_real + probe_imag * probe_imag))
    return (gradient, numerator, denominator)


def shrink(casorati):
    highest = lax.Precision.HIGHEST
    gram = jnp.einsum("bfv,bgv->bfg", casorati, casorati, precision=highest)
    frames = gram.shape[1]
    identity = jnp.eye(frames, dtype=jnp.float32)
    shrink_level = shrink_ratio * jnp.trace(gram, axis1=1, axis2=2) / frames + epsilon
    system = gram + shrink_level[:, None, None] * identity
    row_bound = jnp.max(jnp.sum(jnp.abs(system), axis=2), axis=1)
    approx = identity[None] / row_bound[:, None, None]
    for newton in range(NEWTON):
        product = jnp.einsum("bfg,bgh->bfh", system, approx, precision=highest)
        approx = jnp.einsum("bfg,bgh->bfh", approx, 2.0 * identity - product, precision=highest)
    return casorati - shrink_level[:, None, None] * jnp.einsum(
        "bfg,bgv->bfv", approx, casorati, precision=highest
    )


def to_blocks(field):
    frames, parts, width, length = field.shape
    blocks = field.reshape(frames, parts, width // BS, BS, length // BS, BS)
    blocks = blocks.transpose(2, 4, 0, 1, 3, 5)
    return blocks.reshape(width // BS * (length // BS), frames, parts * BS * BS)


def from_blocks(blocks, width, length):
    frames = blocks.shape[1]
    field = blocks.reshape(width // BS, length // BS, frames, 2, BS, BS)
    field = field.transpose(2, 3, 0, 4, 1, 5)
    return field.reshape(frames, 2, width, length)


def whole_body(start_image, sensitivity, kspace, sampled, offsets):
    width, length = (start_image.shape[2], start_image.shape[3])
    cosine_table, sine_table = dft_tables(length)
    estimate = start_image

    def per_frame(frame_items):
        field, data, lines = frame_items
        return frame_terms(field, sensitivity, data, lines, cosine_table, sine_table)

    for iteration in range(ITERS):
        gradient, numerator, denominator = lax.map(per_frame, (estimate, kspace, sampled))
        offset_pair = offsets[iteration]
        totals = lax.psum((jnp.sum(numerator), jnp.sum(denominator)), "tm")
        step_length = totals[0] / (totals[1] + epsilon)
        moved = estimate - step_length * gradient
        rolled = jnp.roll(moved, (offset_pair[0], offset_pair[1]), axis=(2, 3))
        casorati = lax.all_to_all(to_blocks(rolled), "tm", split_axis=0, concat_axis=1, tiled=True)
        shrunk = shrink(casorati)
        returned = lax.all_to_all(shrunk, "tm", split_axis=1, concat_axis=0, tiled=True)
        placed = from_blocks(returned, width, length)
        estimate = jnp.roll(placed, (-offset_pair[0], -offset_pair[1]), axis=(2, 3))
    return estimate


def block_of(column, shift, length):
    return lax.rem(column + shift, length) // BS


def iota(shape, dim):
    return lax.broadcasted_iota(jnp.int32, shape, dim)


def wide_table(length):
    indices = np.arange(length, dtype=np.int32)
    phases = indices[:, None] * indices[None, :] % length
    angles = phases.astype(np.float32) * np.float32(2.0 * math.pi / length)
    norm_scale = np.float32(1.0 / math.sqrt(length))
    cosine = (np.cos(angles) * norm_scale).astype(ml_dtypes.bfloat16)
    sine = (np.sin(angles) * norm_scale).astype(ml_dtypes.bfloat16)
    return np.block([[cosine, -sine], [sine, cosine]])


def pair_list(frames):
    return [(f, g) for f in range(frames) for g in range(f, frames)]


def pair_select(frames, lanes):
    table = np.zeros((frames * frames, lanes), np.float32)
    for place, (f, g) in enumerate(pair_list(frames)):
        table[f * frames + g, place] = 1.0
        table[g * frames + f, place] = 1.0
    return table


def pieces(x):
    first = x.astype(jnp.bfloat16)
    rest = x - first.astype(jnp.float32)
    second = rest.astype(jnp.bfloat16)
    third = (rest - second.astype(jnp.float32)).astype(jnp.bfloat16)
    return jnp.concatenate([first, second, third], axis=0)


def pick(x, ones):
    rows = x.shape[0]
    out = mxu(pieces(x), ones.astype(jnp.bfloat16))
    return out[:rows] + out[rows : 2 * rows] + out[2 * rows :]


def pick_rows(ones, x):
    rows = x.shape[0]
    out = lax.dot_general(
        ones.astype(jnp.bfloat16), pieces(x), (((1,), (1,)), ((), ())), preferred_element_type=jnp.float32
    )
    return out[:, :rows] + out[:, rows : 2 * rows] + out[:, 2 * rows :]


def mxu(a, b):
    return jnp.dot(a, b, preferred_element_type=jnp.float32)


def fold(x):
    rows, length = x.shape
    return jnp.sum(x.reshape(rows // 8, 8, length), axis=0)


def frame_kernel(
    offsets_hbm, start_hbm, sens_hbm, data_hbm, lines_hbm, table_hbm, out_ref, strip_ref, copied_ref,
    offsets_ref, start_ref, sens_ref, data_ref, lines_ref, table_ref, grad, left, right, sems, chunk_sems,
):
    chunks, coils, _, rows, length = sens_ref.shape
    start_copy, lines_copy, table_copy, offsets_copy = (
        pltpu.make_async_copy(source, target, sems.at[k])
        for k, (source, target) in enumerate(
            ((start_hbm, start_ref), (lines_hbm, lines_ref), (table_hbm, table_ref), (offsets_hbm, offsets_ref))
        )
    )
    sens_copy = [
        pltpu.make_async_copy(sens_hbm.at[:, :, pl.ds(i * rows, rows), :], sens_ref.at[i], chunk_sems.at[0, i])
        for i in range(chunks)
    ]
    data_copy = [
        pltpu.make_async_copy(data_hbm.at[0, :, :, pl.ds(i * rows, rows), :], data_ref.at[i], chunk_sems.at[1, i])
        for i in range(chunks)
    ]
    offsets_copy.start()
    start_copy.start()
    lines_copy.start()
    sens_copy[0].start()
    table_copy.start()
    for copy in sens_copy[1:] + data_copy:
        copy.start()
    strips = out_ref.shape[0]
    halves = length // LANES
    strip = 2 * BS

    def coil_image(i, a, b):
        for c in range(coils):
            sr = sens_ref[i, c, 0].astype(jnp.float32)
            si = sens_ref[i, c, 1].astype(jnp.float32)
            at = slice(c * rows, (c + 1) * rows)
            left[i, at, :length] = (sr * a - si * b).astype(jnp.bfloat16)
            left[i, at, length:] = (sr * b + si * a).astype(jnp.bfloat16)

    def post(kind, image):
        shift = offsets_ref[0, 0]
        for part in range(2):
            rolled = pltpu.roll(image[part], shift, 0)
            for half in range(halves):
                base = (kind * halves + half) * strip + part * BS
                out_ref[:, base : base + BS, :] = rolled[:, half * LANES : (half + 1) * LANES].reshape(strips, BS, LANES)

    offsets_copy.wait()
    start_copy.wait()
    lines_copy.wait()
    copied = jnp.zeros(copied_ref.shape, jnp.int32)
    for k in range(copied.shape[0]):
        for axis in range(copied.shape[1]):
            here = (iota(copied.shape, 0) == k) & (iota(copied.shape, 1) == axis)
            copied = jnp.where(here, offsets_ref[k, axis], copied)
    copied_ref[...] = copied
    weight = lines_ref[0].astype(jnp.float32)
    post(0, start_ref.at[0])
    for target in range(strips):
        for half in range(halves):
            base = 2 * halves * strip + half * coils
            out_ref[target, base : base + coils, :] = weight[:, half * LANES : (half + 1) * LANES]
    spec = []
    for i in range(chunks):
        sens_copy[i].wait()
        coil_image(i, start_ref[0, 0, i * rows : (i + 1) * rows], start_ref[0, 1, i * rows : (i + 1) * rows])
        if i == 0:
            table_copy.wait()
        spec.append(mxu(left[i], table_ref[...]))
    me = lax.axis_index("tm")
    each = rows // BS
    pair = []
    for place in (lax.rem(me + strips - 1, strips), me):
        pair.append((place // each, pl.ds(pl.multiple_of(lax.rem(place, each) * BS, BS), BS)))
    shift = offsets_ref[0, 0]
    for c in range(coils):
        for part in range(2):
            two = jnp.concatenate([sens_ref[i, c, part, at, :] for i, at in pair], axis=0).astype(jnp.float32)
            strip_ref[c, part] = pltpu.roll(two, shift, 0)[BS:]
    home = []
    for i in range(chunks):
        data_copy[i].wait()
        for c in range(coils):
            at = slice(c * rows, (c + 1) * rows)
            w = weight[c : c + 1]
            right[i, at, :length] = (w * (spec[i][at, :length] - data_ref[i, c, 0].astype(jnp.float32))).astype(jnp.bfloat16)
            right[i, at, length:] = (w * (data_ref[i, c, 1].astype(jnp.float32) - spec[i][at, length:])).astype(jnp.bfloat16)
        home.append(mxu(right[i], table_ref[...]))
    num = jnp.zeros((8, length), jnp.float32)
    probe = []
    for i in range(chunks):
        gr = jnp.zeros((rows, length), jnp.float32)
        gi = jnp.zeros((rows, length), jnp.float32)
        for c in range(coils):
            sr = sens_ref[i, c, 0].astype(jnp.float32)
            si = sens_ref[i, c, 1].astype(jnp.float32)
            at = slice(c * rows, (c + 1) * rows)
            br, bi = home[i][at, :length], home[i][at, length:]
            gr = gr + (sr * br - si * bi)
            gi = gi - (sr * bi + si * br)
        grad[0, i * rows : (i + 1) * rows, :] = gr
        grad[1, i * rows : (i + 1) * rows, :] = gi
        num = num + fold(gr * gr + gi * gi)
        coil_image(i, gr, gi)
        probe.append(mxu(left[i], table_ref[...]))
    post(1, grad)
    den = jnp.zeros((8, length), jnp.float32)
    for i in range(chunks):
        for c in range(coils):
            at = slice(c * rows, (c + 1) * rows)
            pr, pi = probe[i][at, :length], probe[i][at, length:]
            den = den + weight[c : c + 1] * fold(pr * pr + pi * pi)
    numer = jnp.sum(jnp.sum(num, axis=0, keepdims=True), axis=1, keepdims=True)
    denom = jnp.sum(jnp.sum(den, axis=0, keepdims=True), axis=1, keepdims=True)
    sums = jnp.where(iota((8, LANES), 0) == 0, numer, denom)
    base = 2 * halves * strip + halves * coils
    for target in range(strips):
        out_ref[target, base : base + 8, :] = sums


def newton_inverse(system, held, other, frames):
    lanes = system[0].shape[1]
    place = iota((frames, lanes), 0)
    unit = [(place == f).astype(jnp.float32) for f in range(frames)]
    sums = sum(jnp.abs(tile) for tile in system)
    bound = jnp.max(sums, axis=0, keepdims=True)
    for f in range(frames):
        held[f * frames : (f + 1) * frames, :] = system[f]
    approx = [unit[f] / bound for f in range(frames)]

    def times(ref, tiles):
        out = []
        for f in range(frames):
            terms = [ref[f * frames + g : f * frames + g + 1, :] * tiles[g] for g in range(frames)]
            while len(terms) > 1:
                terms = [a + b for a, b in zip(terms[::2], terms[1::2])]
            out.append(terms[0])
        return out

    for newton in range(NEWTON):
        for f in range(frames):
            other[f * frames : (f + 1) * frames, :] = approx[f]
        product = times(held, approx)
        approx = times(other, [2.0 * unit[f] - product[f] for f in range(frames)])
    return approx


def shrink_factors(gram, held, other, frames):
    lanes = gram.shape[1]
    place = iota((frames, lanes), 0)
    tiles = [gram[f * frames : (f + 1) * frames, :] for f in range(frames)]
    trace = sum(gram[f * frames + f : f * frames + f + 1, :] for f in range(frames))
    level = shrink_ratio * trace / frames + epsilon
    system = [tiles[f] + jnp.where(place == f, level, 0.0) for f in range(frames)]
    approx = newton_inverse(system, held, other, frames)
    return jnp.concatenate([level * tile for tile in approx], axis=0)


def middle_kernel(
    offsets_ref, mail_ref, sens_ref, table_ref,
    out_ref, own_ref, est_ref, grad_ref,
    terms, held, other, spread, left, right,
):
    frames = mail_ref.shape[0]
    coils, _, _, length = sens_ref.shape
    pairs = pair_list(frames)
    strip = 2 * BS
    halves = length // LANES

    def mail(f, kind, first, rows):
        return jnp.concatenate(
            [
                mail_ref[f, (kind * halves + half) * strip + first : (kind * halves + half) * strip + first + rows, :]
                for half in range(halves)
            ],
            axis=1,
        )

    def mask(f):
        base = 2 * halves * strip
        return jnp.concatenate(
            [mail_ref[f, base + half * coils : base + (half + 1) * coils, :] for half in range(halves)], axis=1
        )

    place = 2 * halves * strip + halves * coils
    totals = sum(mail_ref[f, place : place + 8, :] for f in range(frames))
    step = totals[:1] / (totals[1:2] + epsilon)
    step = jnp.concatenate([step] * halves, axis=1)
    for f in range(frames):
        est_ref[f] = mail(f, 0, 0, strip) - step * mail(f, 1, 0, strip)
    for f, g in pairs:
        tile = fold(est_ref[f] * est_ref[g])
        for place in {f * frames + g, g * frames + f}:
            for half in range(length // LANES):
                terms[half, place * 8 : place * 8 + 8, :] = tile[:, half * LANES : (half + 1) * LANES]
    count = frames * frames
    sums = jnp.concatenate(
        [sum(terms[half, pl.ds(s, count, stride=8), :] for s in range(8)) for half in range(length // LANES)], axis=1
    )
    shift = offsets_ref[0, 1]
    tall = (block_of(iota((length, LANES), 0), shift, length) == iota((length, LANES), 1)).astype(jnp.float32)
    broad = (block_of(iota((LANES, length), 1), shift, length) == iota((LANES, length), 0)).astype(jnp.float32)
    factors = shrink_factors(pick(sums, tall), held, other, frames)
    spread[...] = pick(factors, broad)
    moved = [est_ref[f] for f in range(frames)]
    for f in range(frames):
        total = spread[f * frames : f * frames + 1, :] * moved[0]
        for g in range(1, frames):
            total = total + spread[f * frames + g : f * frames + g + 1, :] * moved[g]
        grad_ref[f] = moved[f] - total
    for f in range(frames):
        est_ref[f] = grad_ref[f]

    num = jnp.zeros((8, length), jnp.float32)
    den = jnp.zeros((8, length), jnp.float32)
    group = left.shape[1] // (coils * BS)

    def coil_image(index, values):
        for k, (a, b) in enumerate(values):
            for c in range(coils):
                sr, si = sens_ref[c, 0], sens_ref[c, 1]
                at = slice((k * coils + c) * BS, (k * coils + c + 1) * BS)
                left[index, at, :length] = (sr * a - si * b).astype(jnp.bfloat16)
                left[index, at, length:] = (sr * b + si * a).astype(jnp.bfloat16)

    edge = lax.rem(offsets_ref[0, 0] - offsets_ref[1, 0] + BS, BS)
    low = [(iota((8, length), 0) + 8 * t >= edge) for t in range(BS // 8)]
    block = len(pairs)
    span = out_ref.shape[2]

    def rows_of(product):
        return [
            sum(product[p * BS + 8 * t : p * BS + 8 * t + 8] for p in range(2)) for t in range(BS // 8)
        ]

    def put(part, place, tile):
        for half in range(length // LANES):
            terms[half, (part * span + place) * 8 : (part * span + place) * 8 + 8, :] = tile[
                :, half * LANES : (half + 1) * LANES
            ]

    def put_kind(kind, product_of):
        for place, pair in enumerate(pairs):
            rows = rows_of(product_of(*pair))
            put(0, kind * block + place, sum(jnp.where(low[t], rows[t], 0.0) for t in range(BS // 8)))
            put(1, kind * block + place, sum(jnp.where(low[t], 0.0, rows[t]) for t in range(BS // 8)))

    groups = [range(at, at + group) for at in range(0, frames, group)]
    weights = [mask(f) for f in range(frames)]
    spec = []
    for index, members in enumerate(groups):
        coil_image(
            index,
            [(est_ref[f, :BS, :] - mail(f, 0, 0, BS), est_ref[f, BS:strip, :] - mail(f, 0, BS, BS)) for f in members],
        )
        spec.append(mxu(left[index], table_ref[...]))
    for part in range(2):
        for place in range(3 * block, span):
            put(part, place, jnp.zeros((8, length), jnp.float32))
    put_kind(0, lambda f, g: est_ref[f] * est_ref[g])
    home = []
    for index, members in enumerate(groups):
        for k, f in enumerate(members):
            for c in range(coils):
                at = slice((k * coils + c) * BS, (k * coils + c + 1) * BS)
                w = weights[f][c : c + 1]
                right[index, at, :length] = (w * spec[index][at, :length]).astype(jnp.bfloat16)
                right[index, at, length:] = (-w * spec[index][at, length:]).astype(jnp.bfloat16)
        home.append(mxu(right[index], table_ref[...]))
    probe = []
    for index, members in enumerate(groups):
        values = []
        for k, f in enumerate(members):
            gr = mail(f, 1, 0, BS)
            gi = mail(f, 1, BS, BS)
            for c in range(coils):
                at = slice((k * coils + c) * BS, (k * coils + c + 1) * BS)
                sr, si = sens_ref[c, 0], sens_ref[c, 1]
                br, bi = home[index][at, :length], home[index][at, length:]
                gr = gr + (sr * br - si * bi)
                gi = gi - (sr * bi + si * br)
            grad_ref[f, :BS, :] = gr
            grad_ref[f, BS:strip, :] = gi
            num = num + fold(gr * gr + gi * gi)
            values.append((gr, gi))
        coil_image(index, values)
        probe.append(mxu(left[index], table_ref[...]))
    put_kind(1, lambda f, g: est_ref[f] * grad_ref[g] + est_ref[g] * grad_ref[f])
    put_kind(2, lambda f, g: grad_ref[f] * grad_ref[g])
    for index, members in enumerate(groups):
        for k, f in enumerate(members):
            for c in range(coils):
                at = slice((k * coils + c) * BS, (k * coils + c + 1) * BS)
                pr, pi = probe[index][at, :length], probe[index][at, length:]
                den = den + weights[f][c : c + 1] * fold(pr * pr + pi * pi)
    numer = jnp.sum(jnp.sum(num, axis=0, keepdims=True), axis=1, keepdims=True)
    denom = jnp.sum(jnp.sum(den, axis=0, keepdims=True), axis=1, keepdims=True)

    shift = offsets_ref[1, 1]
    blocks = length // BS
    member = (block_of(iota((blocks, length), 1), shift, length) == iota((blocks, length), 0)).astype(jnp.float32)
    lane = iota((blocks, span), 1)
    packs = []
    for part in range(2):
        sums = jnp.concatenate(
            [
                sum(terms[half, pl.ds(part * span * 8 + s, span, stride=8), :] for s in range(8))
                for half in range(length // LANES)
            ],
            axis=1,
        )
        pack = pick_rows(member, sums)
        pack = jnp.where(lane == 3 * block, numer, jnp.where(lane == 3 * block + 1, denom, pack))
        own_ref[part * blocks : (part + 1) * blocks, :] = pack
        packs.append(pack)
    me = lax.axis_index("tm")
    strips = out_ref.shape[0]
    before = lax.rem(me + strips - 1, strips)
    for target in range(strips):
        out_ref[target] = jnp.where(before == target, packs[1], packs[0])


def last_kernel(offsets_ref, own_ref, heard_ref, est_ref, grad_ref, select_ref, out_ref, held, other, spread_low, spread_up):
    frames, strip, length = est_ref.shape
    strips, blocks, span = heard_ref.shape
    block = len(pair_list(frames))
    me = lax.axis_index("tm")
    numer = jnp.zeros((1, 1), jnp.float32)
    denom = jnp.zeros((1, 1), jnp.float32)
    for k in range(strips):
        numer = numer + heard_ref[k, 0:1, 3 * block : 3 * block + 1]
        denom = denom + heard_ref[k, 0:1, 3 * block + 1 : 3 * block + 2]
    step = numer / (denom + epsilon)
    after = lax.rem(me + 1, strips)
    before = lax.rem(me + strips - 1, strips)
    total = own_ref[...] + jnp.concatenate([heard_ref[after], heard_ref[before]], axis=0)
    cross = pltpu.roll(total, span - block, 1)
    square = pltpu.roll(total, span - 2 * block, 1)
    gram = total - step * cross + step * step * square
    gram = jnp.concatenate([gram, jnp.zeros((LANES - 2 * blocks, span), jnp.float32)], axis=0)
    gram = jnp.where(iota(gram.shape, 1) < block, gram, 0.0)
    gram = pick_rows(select_ref[...], gram)
    factors = shrink_factors(gram, held, other, frames)
    shift = offsets_ref[1, 1]
    column = block_of(iota((LANES, length), 1), shift, length)
    row = iota((LANES, length), 0)
    spread_low[...] = pick(factors, (column == row).astype(jnp.float32))
    spread_up[...] = pick(factors, (column + blocks == row).astype(jnp.float32))
    edge = lax.rem(offsets_ref[0, 0] - offsets_ref[1, 0] + BS, BS)
    moved = [est_ref[f] - step * grad_ref[f] for f in range(frames)]
    for t in range(BS // 8):
        low = iota((8, length), 0) + 8 * t >= edge
        for f in range(frames):
            total = [jnp.zeros((8, length), jnp.float32)] * 2
            for g in range(frames):
                at = f * frames + g
                factor = jnp.where(low, spread_low[at : at + 1, :], spread_up[at : at + 1, :])
                total = [total[p] + factor * moved[g][p * BS + 8 * t : p * BS + 8 * t + 8] for p in range(2)]
            for p in range(2):
                rows = slice(p * BS + 8 * t, p * BS + 8 * t + 8)
                out_ref[f, rows, :] = moved[f][rows] - total[p]


def place_kernel(offsets_ref, strips_ref, out_hbm, whole, sems):
    strips, _, length = strips_ref.shape
    width = strips * BS
    shift = lax.rem(width - offsets_ref[0, 0], width)
    copies = []
    for part in range(2):
        whole[part] = pltpu.roll(strips_ref[:, part * BS : (part + 1) * BS, :].reshape(width, length), shift, 0)
        copies.append(pltpu.make_async_copy(whole.at[part], out_hbm.at[0, part], sems.at[part]))
        copies[-1].start()
    for copy in copies:
        copy.wait()


def vmem():
    return pl.BlockSpec(memory_space=pltpu.VMEM)


def hbm():
    return pl.BlockSpec(memory_space=pltpu.HBM)


def smem():
    return pl.BlockSpec(memory_space=pltpu.SMEM)


def f32(*shape):
    return jax.ShapeDtypeStruct(shape, jnp.float32)


def exchange(blocks):
    return lax.all_to_all(blocks, "tm", split_axis=0, concat_axis=0, tiled=True)


def params(mebibytes=16):
    return pltpu.CompilerParams(vmem_limit_bytes=mebibytes * 1024 * 1024)


def frame_call(start_image, sensitivity, kspace, sampled, offsets, table):
    _, _, width, length = start_image.shape
    coils = sensitivity.shape[0]
    rows = 2 * BS
    chunks = width // rows
    return pl.pallas_call(
        frame_kernel,
        out_shape=(
            pltpu.VMEM((width // BS, length // LANES * (4 * BS + coils) + 8, LANES), jnp.float32),
            pltpu.VMEM((coils, 2, BS, length), jnp.float32),
            pltpu.VMEM(offsets.shape, jnp.int32),
        ),
        in_specs=[hbm()] * 6,
        out_specs=(vmem(),) * 3,
        scratch_shapes=[
            pltpu.SMEM(offsets.shape, jnp.int32),
            pltpu.VMEM(start_image.shape, jnp.float32),
            pltpu.VMEM((chunks, coils, 2, rows, length), jnp.bfloat16),
            pltpu.VMEM((chunks, coils, 2, rows, length), jnp.bfloat16),
            pltpu.VMEM(sampled.shape, jnp.int32),
            pltpu.VMEM(table.shape, jnp.bfloat16),
            pltpu.VMEM((2, width, length), jnp.float32),
            pltpu.VMEM((chunks, coils * rows, 2 * length), jnp.bfloat16),
            pltpu.VMEM((chunks, coils * rows, 2 * length), jnp.bfloat16),
            pltpu.SemaphoreType.DMA((4,)),
            pltpu.SemaphoreType.DMA((2, chunks)),
        ],
        compiler_params=params(60),
        name="frame_gradient",
    )(offsets, start_image, sensitivity, kspace, sampled, table)


def middle_call(mail, sens, offsets, table):
    frames = mail.shape[0]
    coils, _, _, length = sens.shape
    count = frames * frames
    blocks = length // BS
    group = 2
    return pl.pallas_call(
        middle_kernel,
        out_shape=(
            f32(frames, blocks, LANES),
            f32(2 * blocks, LANES),
            f32(frames, 2 * BS, length),
            f32(frames, 2 * BS, length),
        ),
        in_specs=[smem()] + [vmem()] * 3,
        out_specs=(vmem(),) * 4,
        scratch_shapes=[
            pltpu.VMEM((length // LANES, 2 * LANES * 8, LANES), jnp.float32),
            pltpu.VMEM((count, LANES), jnp.float32),
            pltpu.VMEM((count, LANES), jnp.float32),
            pltpu.VMEM((count, length), jnp.float32),
            pltpu.VMEM((frames // group, group * coils * BS, 2 * length), jnp.bfloat16),
            pltpu.VMEM((frames // group, group * coils * BS, 2 * length), jnp.bfloat16),
        ],
        compiler_params=params(),
        name="strip_shrink_gradient",
    )(offsets, mail, sens, table)


def last_call(own, heard, estimate, gradient, offsets):
    frames, strip, length = estimate.shape
    count = frames * frames
    return pl.pallas_call(
        last_kernel,
        out_shape=f32(frames, strip, length),
        in_specs=[smem()] + [vmem()] * 5,
        out_specs=vmem(),
        scratch_shapes=[
            pltpu.VMEM((count, LANES), jnp.float32),
            pltpu.VMEM((count, LANES), jnp.float32),
            pltpu.VMEM((count, length), jnp.float32),
            pltpu.VMEM((count, length), jnp.float32),
        ],
        compiler_params=params(),
        name="strip_shrink",
    )(offsets, own, heard, estimate, gradient, jnp.asarray(pair_select(frames, LANES)))


def place_call(strips, offsets):
    count, strip, length = strips.shape
    width = count * strip // 2
    return pl.pallas_call(
        place_kernel,
        out_shape=f32(1, 2, width, length),
        in_specs=[smem(), vmem()],
        out_specs=hbm(),
        scratch_shapes=[pltpu.VMEM((2, width, length), jnp.float32), pltpu.SemaphoreType.DMA((2,))],
        compiler_params=params(),
        name="frame_place",
    )(offsets, strips)


def strips_body(start_image, sensitivity, kspace, sampled, offsets):
    table = jnp.asarray(wide_table(start_image.shape[3]))
    mail, sens, offsets = frame_call(start_image, sensitivity, kspace, sampled, offsets, table)
    mail = exchange(mail)
    sent, own, estimate, gradient = middle_call(mail, sens, offsets, table)
    returned = exchange(last_call(own, exchange(sent), estimate, gradient, offsets))
    return place_call(returned, offsets)


def fits_strips(start_image, sensitivity, kspace, sampled, offsets):
    strips = lax.axis_size("tm")
    frames, _, width, length = start_image.shape
    coils = sensitivity.shape[0]
    kinds = 3 * len(pair_list(strips))
    return (
        frames == 1
        and width == strips * BS
        and strips == SUBLANES
        and coils % SUBLANES == 0
        and ITERS == 2
        and length % LANES == 0
        and 2 * (length // BS) <= LANES
        and kinds + 2 <= LANES
    )


def body(*args):
    return (strips_body if fits_strips(*args) else whole_body)(*args)


def solution(mesh):
    placed = (
        P(("cuts", "tm"), None, None, None),
        P("cuts", None, None, None),
        P(("cuts", "tm"), None, None, None, None),
        P(("cuts", "tm"), None, None),
        P("cuts", None),
    )
    return jax.shard_map(
        body,
        mesh=mesh,
        in_specs=placed,
        out_specs=P(("cuts", "tm"), None, None, None),
        check_vma=False,
    )
```

```python
import math

import jax
import jax.numpy as jnp
import ml_dtypes
import numpy as np
from jax import lax
from jax.experimental import pallas as pl
from jax.experimental.pallas import tpu as pltpu
from jax.sharding import PartitionSpec as P

BS = 16
ITERS = 2
NEWTON = 4
LANES = 128
SUBLANES = 8


shrink_ratio = 0.5
epsilon = 1e-06


def dft_tables(length):
    indices = jnp.arange(length, dtype=jnp.int32)
    phases = indices[:, None] * indices[None, :] % length
    angles = phases.astype(jnp.float32) * (2.0 * math.pi / length)
    norm_scale = 1.0 / math.sqrt(length)
    return (
        (jnp.cos(angles) * norm_scale).astype(jnp.bfloat16),
        (jnp.sin(angles) * norm_scale).astype(jnp.bfloat16),
    )


def forward(real_part, imag_part, cosine_table, sine_table):
    out_real = jnp.dot(real_part, cosine_table, preferred_element_type=jnp.float32) + jnp.dot(
        imag_part, sine_table, preferred_element_type=jnp.float32
    )
    out_imag = jnp.dot(imag_part, cosine_table, preferred_element_type=jnp.float32) - jnp.dot(
        real_part, sine_table, preferred_element_type=jnp.float32
    )
    return (out_real, out_imag)


def inverse(real_part, imag_part, cosine_table, sine_table):
    out_real = jnp.dot(real_part, cosine_table, preferred_element_type=jnp.float32) - jnp.dot(
        imag_part, sine_table, preferred_element_type=jnp.float32
    )
    out_imag = jnp.dot(imag_part, cosine_table, preferred_element_type=jnp.float32) + jnp.dot(
        real_part, sine_table, preferred_element_type=jnp.float32
    )
    return (out_real, out_imag)


def coil_spectra(field, sens_real, sens_imag, cosine_table, sine_table):
    coils, width, length = sens_real.shape
    coil_real = (
        (sens_real * field[0] - sens_imag * field[1])
        .astype(jnp.bfloat16)
        .reshape(coils * width, length)
    )
    coil_imag = (
        (sens_real * field[1] + sens_imag * field[0])
        .astype(jnp.bfloat16)
        .reshape(coils * width, length)
    )
    spec_real, spec_imag = forward(coil_real, coil_imag, cosine_table, sine_table)
    return (spec_real.reshape(coils, width, length), spec_imag.reshape(coils, width, length))


def frame_terms(field, sensitivity, data, lines, cosine_table, sine_table):
    sens_real = sensitivity[:, 0].astype(jnp.float32)
    sens_imag = sensitivity[:, 1].astype(jnp.float32)
    coils, width, length = sens_real.shape
    weight = lines.astype(jnp.float32)[:, None, :]
    spec_real, spec_imag = coil_spectra(field, sens_real, sens_imag, cosine_table, sine_table)
    misfit_real = (weight * (spec_real - data[:, 0].astype(jnp.float32))).astype(jnp.bfloat16)
    misfit_imag = (weight * (spec_imag - data[:, 1].astype(jnp.float32))).astype(jnp.bfloat16)
    back_real, back_imag = inverse(
        misfit_real.reshape(coils * width, length),
        misfit_imag.reshape(coils * width, length),
        cosine_table,
        sine_table,
    )
    back_real = back_real.reshape(coils, width, length)
    back_imag = back_imag.reshape(coils, width, length)
    grad_real = jnp.sum(sens_real * back_real + sens_imag * back_imag, axis=0)
    grad_imag = jnp.sum(sens_real * back_imag - sens_imag * back_real, axis=0)
    gradient = jnp.stack([grad_real, grad_imag])
    numerator = jnp.sum(gradient * gradient)
    probe_real, probe_imag = coil_spectra(gradient, sens_real, sens_imag, cosine_table, sine_table)
    denominator = jnp.sum(weight * (probe_real * probe_real + probe_imag * probe_imag))
    return (gradient, numerator, denominator)


def shrink(casorati):
    highest = lax.Precision.HIGHEST
    gram = jnp.einsum("bfv,bgv->bfg", casorati, casorati, precision=highest)
    frames = gram.shape[1]
    identity = jnp.eye(frames, dtype=jnp.float32)
    shrink_level = shrink_ratio * jnp.trace(gram, axis1=1, axis2=2) / frames + epsilon
    system = gram + shrink_level[:, None, None] * identity
    row_bound = jnp.max(jnp.sum(jnp.abs(system), axis=2), axis=1)
    approx = identity[None] / row_bound[:, None, None]
    for newton in range(NEWTON):
        product = jnp.einsum("bfg,bgh->bfh", system, approx, precision=highest)
        approx = jnp.einsum("bfg,bgh->bfh", approx, 2.0 * identity - product, precision=highest)
    return casorati - shrink_level[:, None, None] * jnp.einsum(
        "bfg,bgv->bfv", approx, casorati, precision=highest
    )


def to_blocks(field):
    frames, parts, width, length = field.shape
    blocks = field.reshape(frames, parts, width // BS, BS, length // BS, BS)
    blocks = blocks.transpose(2, 4, 0, 1, 3, 5)
    return blocks.reshape(width // BS * (length // BS), frames, parts * BS * BS)


def from_blocks(blocks, width, length):
    frames = blocks.shape[1]
    field = blocks.reshape(width // BS, length // BS, frames, 2, BS, BS)
    field = field.transpose(2, 3, 0, 4, 1, 5)
    return field.reshape(frames, 2, width, length)


def whole_body(start_image, sensitivity, kspace, sampled, offsets):
    width, length = (start_image.shape[2], start_image.shape[3])
    cosine_table, sine_table = dft_tables(length)
    estimate = start_image

    def per_frame(frame_items):
        field, data, lines = frame_items
        return frame_terms(field, sensitivity, data, lines, cosine_table, sine_table)

    for iteration in range(ITERS):
        gradient, numerator, denominator = lax.map(per_frame, (estimate, kspace, sampled))
        offset_pair = offsets[iteration]
        totals = lax.psum((jnp.sum(numerator), jnp.sum(denominator)), "tm")
        step_length = totals[0] / (totals[1] + epsilon)
        moved = estimate - step_length * gradient
        rolled = jnp.roll(moved, (offset_pair[0], offset_pair[1]), axis=(2, 3))
        casorati = lax.all_to_all(to_blocks(rolled), "tm", split_axis=0, concat_axis=1, tiled=True)
        shrunk = shrink(casorati)
        returned = lax.all_to_all(shrunk, "tm", split_axis=1, concat_axis=0, tiled=True)
        placed = from_blocks(returned, width, length)
        estimate = jnp.roll(placed, (-offset_pair[0], -offset_pair[1]), axis=(2, 3))
    return estimate


def iota(shape, dim):
    return lax.broadcasted_iota(jnp.int32, shape, dim)


def in_block(column, shift, block, length):
    moved = column + shift
    moved = jnp.where(moved >= length, moved - length, moved)
    return (moved >= block * BS) & (moved < block * BS + BS)


def offset_row(offsets_ref, iteration, axis, lanes):
    at = 2 * iteration + axis
    return jnp.concatenate([offsets_ref[at : at + 1, :]] * (lanes // LANES), axis=1)


def upper_rows(offsets_ref, length):
    edge = offset_row(offsets_ref, 0, 0, length) - offset_row(offsets_ref, 1, 0, length)
    return jnp.where(edge < 0, edge + BS, edge)


def wide_table(length):
    indices = np.arange(length, dtype=np.int32)
    phases = indices[:, None] * indices[None, :] % length
    angles = phases.astype(np.float32) * np.float32(2.0 * math.pi / length)
    norm_scale = np.float32(1.0 / math.sqrt(length))
    cosine = (np.cos(angles) * norm_scale).astype(ml_dtypes.bfloat16)
    sine = (np.sin(angles) * norm_scale).astype(ml_dtypes.bfloat16)
    return np.block([[cosine, -sine], [sine, cosine]])


def pair_list(frames):
    return [(f, g) for f in range(frames) for g in range(f, frames)]


def pair_select(frames, lanes):
    table = np.zeros((frames * frames, lanes), np.float32)
    for place, (f, g) in enumerate(pair_list(frames)):
        table[f * frames + g, place] = 1.0
        table[g * frames + f, place] = 1.0
    return table


def pieces(x):
    first = x.astype(jnp.bfloat16)
    rest = x - first.astype(jnp.float32)
    second = rest.astype(jnp.bfloat16)
    third = (rest - second.astype(jnp.float32)).astype(jnp.bfloat16)
    return jnp.concatenate([first, second, third], axis=0)


def pick(x, ones):
    rows = x.shape[0]
    out = mxu(pieces(x), ones.astype(jnp.float32).astype(jnp.bfloat16))
    return out[:rows] + out[rows : 2 * rows] + out[2 * rows :]


def pick_rows(ones, x):
    rows = x.shape[0]
    out = lax.dot_general(
        ones.astype(jnp.float32).astype(jnp.bfloat16), pieces(x), (((1,), (1,)), ((), ())), preferred_element_type=jnp.float32
    )
    return out[:, :rows] + out[:, rows : 2 * rows] + out[:, 2 * rows :]


def mxu(a, b):
    return jnp.dot(a, b, preferred_element_type=jnp.float32)


def fold(x):
    rows, length = x.shape
    return jnp.sum(x.reshape(rows // 8, 8, length), axis=0)


def frame_kernel(
    offsets_hbm, start_hbm, sens_hbm, data_hbm, lines_hbm, table_hbm, out_ref, strip_ref, copied_ref,
    offsets_ref, start_ref, sens_ref, data_ref, lines_ref, table_ref, grad, left, right, sems, chunk_sems,
):
    chunks, coils, _, rows, length = sens_ref.shape
    start_copy, lines_copy, table_copy, offsets_copy = (
        pltpu.make_async_copy(source, target, sems.at[k])
        for k, (source, target) in enumerate(
            ((start_hbm, start_ref), (lines_hbm, lines_ref), (table_hbm, table_ref), (offsets_hbm, offsets_ref))
        )
    )
    sens_copy = [
        pltpu.make_async_copy(sens_hbm.at[:, :, pl.ds(i * rows, rows), :], sens_ref.at[i], chunk_sems.at[0, i])
        for i in range(chunks)
    ]
    data_copy = [
        pltpu.make_async_copy(data_hbm.at[0, :, :, pl.ds(i * rows, rows), :], data_ref.at[i], chunk_sems.at[1, i])
        for i in range(chunks)
    ]
    offsets_copy.start()
    start_copy.start()
    lines_copy.start()
    sens_copy[0].start()
    table_copy.start()
    for copy in sens_copy[1:] + data_copy:
        copy.start()
    strips = out_ref.shape[0]
    halves = length // LANES
    strip = 2 * BS

    def coil_image(i, a, b):
        for c in range(coils):
            sr = sens_ref[i, c, 0].astype(jnp.float32)
            si = sens_ref[i, c, 1].astype(jnp.float32)
            at = slice(c * rows, (c + 1) * rows)
            left[i, at, :length] = (sr * a - si * b).astype(jnp.bfloat16)
            left[i, at, length:] = (sr * b + si * a).astype(jnp.bfloat16)

    def post(kind, image):
        shift = offsets_ref[0, 0]
        for part in range(2):
            rolled = pltpu.roll(image[part], shift, 0)
            for half in range(halves):
                base = (kind * halves + half) * strip + part * BS
                out_ref[:, base : base + BS, :] = rolled[:, half * LANES : (half + 1) * LANES].reshape(strips, BS, LANES)

    offsets_copy.wait()
    start_copy.wait()
    lines_copy.wait()
    copied = jnp.zeros(copied_ref.shape, jnp.int32)
    for k in range(ITERS):
        for axis in range(2):
            copied = jnp.where(iota(copied.shape, 0) == 2 * k + axis, offsets_ref[k, axis], copied)
    copied_ref[...] = copied
    weight = lines_ref[0].astype(jnp.float32)
    post(0, start_ref.at[0])
    for target in range(strips):
        for half in range(halves):
            base = 2 * halves * strip + half * coils
            out_ref[target, base : base + coils, :] = weight[:, half * LANES : (half + 1) * LANES]
    spec = []
    for i in range(chunks):
        sens_copy[i].wait()
        coil_image(i, start_ref[0, 0, i * rows : (i + 1) * rows], start_ref[0, 1, i * rows : (i + 1) * rows])
        if i == 0:
            table_copy.wait()
        spec.append(mxu(left[i], table_ref[...]))
    me = lax.axis_index("tm")
    each = rows // BS
    pair = []
    for place in (lax.rem(me + strips - 1, strips), me):
        pair.append((place // each, pl.ds(pl.multiple_of(lax.rem(place, each) * BS, BS), BS)))
    shift = offsets_ref[0, 0]
    for c in range(coils):
        for part in range(2):
            two = jnp.concatenate([sens_ref[i, c, part, at, :] for i, at in pair], axis=0).astype(jnp.float32)
            strip_ref[c, part] = pltpu.roll(two, shift, 0)[BS:]
    home = []
    for i in range(chunks):
        data_copy[i].wait()
        for c in range(coils):
            at = slice(c * rows, (c + 1) * rows)
            w = weight[c : c + 1]
            right[i, at, :length] = (w * (spec[i][at, :length] - data_ref[i, c, 0].astype(jnp.float32))).astype(jnp.bfloat16)
            right[i, at, length:] = (w * (data_ref[i, c, 1].astype(jnp.float32) - spec[i][at, length:])).astype(jnp.bfloat16)
        home.append(mxu(right[i], table_ref[...]))
    num = jnp.zeros((8, length), jnp.float32)
    probe = []
    for i in range(chunks):
        gr = jnp.zeros((rows, length), jnp.float32)
        gi = jnp.zeros((rows, length), jnp.float32)
        for c in range(coils):
            sr = sens_ref[i, c, 0].astype(jnp.float32)
            si = sens_ref[i, c, 1].astype(jnp.float32)
            at = slice(c * rows, (c + 1) * rows)
            br, bi = home[i][at, :length], home[i][at, length:]
            gr = gr + (sr * br - si * bi)
            gi = gi - (sr * bi + si * br)
        grad[0, i * rows : (i + 1) * rows, :] = gr
        grad[1, i * rows : (i + 1) * rows, :] = gi
        num = num + fold(gr * gr + gi * gi)
        coil_image(i, gr, gi)
        probe.append(mxu(left[i], table_ref[...]))
    post(1, grad)
    den = jnp.zeros((8, length), jnp.float32)
    for i in range(chunks):
        for c in range(coils):
            at = slice(c * rows, (c + 1) * rows)
            pr, pi = probe[i][at, :length], probe[i][at, length:]
            den = den + weight[c : c + 1] * fold(pr * pr + pi * pi)
    numer = jnp.sum(jnp.sum(num, axis=0, keepdims=True), axis=1, keepdims=True)
    denom = jnp.sum(jnp.sum(den, axis=0, keepdims=True), axis=1, keepdims=True)
    sums = jnp.where(iota((8, LANES), 0) == 0, numer, denom)
    base = 2 * halves * strip + halves * coils
    for target in range(strips):
        out_ref[target, base : base + 8, :] = sums


def newton_inverse(system, held, frames):
    place = iota(system[0].shape, 0)
    unit = [(place == f).astype(jnp.float32) for f in range(frames)]
    bound = jnp.max(sum(jnp.abs(tile) for tile in system), axis=0, keepdims=True)
    scale = 1.0 / bound

    def times(ref, tiles):
        out = []
        for f in range(frames):
            terms = [ref[f * frames + g : f * frames + g + 1, :] * tiles[g] for g in range(frames)]
            while len(terms) > 1:
                terms = [a + b for a, b in zip(terms[::2], terms[1::2])]
            out.append(terms[0])
        return out

    power = [unit[f] - scale * system[f] for f in range(frames)]
    total = [unit[f] + power[f] for f in range(frames)]
    for newton in range(1, NEWTON):
        for f in range(frames):
            held[newton, f * frames : (f + 1) * frames, :] = power[f]
        power = times(held.at[newton], power)
        for f in range(frames):
            held[0, f * frames : (f + 1) * frames, :] = power[f]
        added = times(held.at[0], total)
        total = [total[f] + added[f] for f in range(frames)]
    return [scale * tile for tile in total]


def shrink_factors(gram, held, frames):
    lanes = gram.shape[1]
    place = iota((frames, lanes), 0)
    tiles = [gram[f * frames : (f + 1) * frames, :] for f in range(frames)]
    trace = sum(gram[f * frames + f : f * frames + f + 1, :] for f in range(frames))
    level = shrink_ratio * trace / frames + epsilon
    system = [tiles[f] + jnp.where(place == f, level, 0.0) for f in range(frames)]
    approx = newton_inverse(system, held, frames)
    return jnp.concatenate([level * tile for tile in approx], axis=0)


def middle_kernel(
    offsets_ref, mail_ref, sens_ref, table_ref,
    out_ref, own_ref, est_ref, grad_ref,
    terms, held, spread, left, right,
):
    frames = mail_ref.shape[0]
    coils, _, _, length = sens_ref.shape
    pairs = pair_list(frames)
    strip = 2 * BS
    halves = length // LANES

    def mail(f, kind, first, rows):
        return jnp.concatenate(
            [
                mail_ref[f, (kind * halves + half) * strip + first : (kind * halves + half) * strip + first + rows, :]
                for half in range(halves)
            ],
            axis=1,
        )

    def mask(f):
        base = 2 * halves * strip
        return jnp.concatenate(
            [mail_ref[f, base + half * coils : base + (half + 1) * coils, :] for half in range(halves)], axis=1
        )

    place = 2 * halves * strip + halves * coils
    totals = sum(mail_ref[f, place : place + 8, :] for f in range(frames))
    step = totals[:1] / (totals[1:2] + epsilon)
    step = jnp.concatenate([step] * halves, axis=1)
    for f in range(frames):
        est_ref[f] = mail(f, 0, 0, strip) - step * mail(f, 1, 0, strip)
    for f, g in pairs:
        tile = fold(est_ref[f] * est_ref[g])
        for place in {f * frames + g, g * frames + f}:
            for half in range(length // LANES):
                terms[half, place * 8 : place * 8 + 8, :] = tile[:, half * LANES : (half + 1) * LANES]
    count = frames * frames
    sums = jnp.concatenate(
        [sum(terms[half, pl.ds(s, count, stride=8), :] for s in range(8)) for half in range(length // LANES)], axis=1
    )
    tall = in_block(iota((length, LANES), 0), offset_row(offsets_ref, 0, 1, LANES), iota((length, LANES), 1), length)
    broad = in_block(iota((LANES, length), 1), offset_row(offsets_ref, 0, 1, length), iota((LANES, length), 0), length)
    factors = shrink_factors(pick(sums, tall), held, frames)
    spread[...] = pick(factors, broad)
    moved = [est_ref[f] for f in range(frames)]
    for f in range(frames):
        total = spread[f * frames : f * frames + 1, :] * moved[0]
        for g in range(1, frames):
            total = total + spread[f * frames + g : f * frames + g + 1, :] * moved[g]
        grad_ref[f] = moved[f] - total
    for f in range(frames):
        est_ref[f] = grad_ref[f]

    num = jnp.zeros((8, length), jnp.float32)
    den = jnp.zeros((8, length), jnp.float32)
    group = left.shape[1] // (coils * BS)

    def coil_image(index, values):
        for k, (a, b) in enumerate(values):
            for c in range(coils):
                sr, si = sens_ref[c, 0], sens_ref[c, 1]
                at = slice((k * coils + c) * BS, (k * coils + c + 1) * BS)
                left[index, at, :length] = (sr * a - si * b).astype(jnp.bfloat16)
                left[index, at, length:] = (sr * b + si * a).astype(jnp.bfloat16)

    edge = upper_rows(offsets_ref, length)
    low = [(iota((8, length), 0) + 8 * t >= edge) for t in range(BS // 8)]
    block = len(pairs)
    span = out_ref.shape[2]

    def rows_of(product):
        return [
            sum(product[p * BS + 8 * t : p * BS + 8 * t + 8] for p in range(2)) for t in range(BS // 8)
        ]

    def put(part, place, tile):
        for half in range(length // LANES):
            terms[half, (part * span + place) * 8 : (part * span + place) * 8 + 8, :] = tile[
                :, half * LANES : (half + 1) * LANES
            ]

    def put_kind(kind, product_of):
        for place, pair in enumerate(pairs):
            rows = rows_of(product_of(*pair))
            put(0, kind * block + place, sum(jnp.where(low[t], rows[t], 0.0) for t in range(BS // 8)))
            put(1, kind * block + place, sum(jnp.where(low[t], 0.0, rows[t]) for t in range(BS // 8)))

    groups = [range(at, at + group) for at in range(0, frames, group)]
    weights = [mask(f) for f in range(frames)]
    spec = []
    for index, members in enumerate(groups):
        coil_image(
            index,
            [(est_ref[f, :BS, :] - mail(f, 0, 0, BS), est_ref[f, BS:strip, :] - mail(f, 0, BS, BS)) for f in members],
        )
        spec.append(mxu(left[index], table_ref[...]))
    for part in range(2):
        for place in range(3 * block, span):
            put(part, place, jnp.zeros((8, length), jnp.float32))
    put_kind(0, lambda f, g: est_ref[f] * est_ref[g])
    home = []
    for index, members in enumerate(groups):
        for k, f in enumerate(members):
            for c in range(coils):
                at = slice((k * coils + c) * BS, (k * coils + c + 1) * BS)
                w = weights[f][c : c + 1]
                right[index, at, :length] = (w * spec[index][at, :length]).astype(jnp.bfloat16)
                right[index, at, length:] = (-w * spec[index][at, length:]).astype(jnp.bfloat16)
        home.append(mxu(right[index], table_ref[...]))
    probe = []
    for index, members in enumerate(groups):
        values = []
        for k, f in enumerate(members):
            gr = mail(f, 1, 0, BS)
            gi = mail(f, 1, BS, BS)
            for c in range(coils):
                at = slice((k * coils + c) * BS, (k * coils + c + 1) * BS)
                sr, si = sens_ref[c, 0], sens_ref[c, 1]
                br, bi = home[index][at, :length], home[index][at, length:]
                gr = gr + (sr * br - si * bi)
                gi = gi - (sr * bi + si * br)
            grad_ref[f, :BS, :] = gr
            grad_ref[f, BS:strip, :] = gi
            num = num + fold(gr * gr + gi * gi)
            values.append((gr, gi))
        coil_image(index, values)
        probe.append(mxu(left[index], table_ref[...]))
    put_kind(1, lambda f, g: est_ref[f] * grad_ref[g] + est_ref[g] * grad_ref[f])
    put_kind(2, lambda f, g: grad_ref[f] * grad_ref[g])
    for index, members in enumerate(groups):
        for k, f in enumerate(members):
            for c in range(coils):
                at = slice((k * coils + c) * BS, (k * coils + c + 1) * BS)
                pr, pi = probe[index][at, :length], probe[index][at, length:]
                den = den + weights[f][c : c + 1] * fold(pr * pr + pi * pi)
    numer = jnp.sum(jnp.sum(num, axis=0, keepdims=True), axis=1, keepdims=True)
    denom = jnp.sum(jnp.sum(den, axis=0, keepdims=True), axis=1, keepdims=True)

    blocks = length // BS
    shift = offset_row(offsets_ref, 1, 1, length)
    member = in_block(iota((blocks, length), 1), shift, iota((blocks, length), 0), length)
    lane = iota((blocks, span), 1)
    packs = []
    for part in range(2):
        sums = jnp.concatenate(
            [
                sum(terms[half, pl.ds(part * span * 8 + s, span, stride=8), :] for s in range(8))
                for half in range(length // LANES)
            ],
            axis=1,
        )
        pack = pick_rows(member, sums)
        pack = jnp.where(lane == 3 * block, numer, jnp.where(lane == 3 * block + 1, denom, pack))
        own_ref[part * blocks : (part + 1) * blocks, :] = pack
        packs.append(pack)
    me = lax.axis_index("tm")
    strips = out_ref.shape[0]
    before = lax.rem(me + strips - 1, strips)
    for target in range(strips):
        out_ref[target] = jnp.where(before == target, packs[1], packs[0])


def last_kernel(offsets_ref, own_ref, heard_ref, est_ref, grad_ref, select_ref, out_ref, held, spread):
    frames, strip, length = est_ref.shape
    strips, blocks, span = heard_ref.shape
    block = len(pair_list(frames))
    me = lax.axis_index("tm")
    numer = jnp.zeros((1, 1), jnp.float32)
    denom = jnp.zeros((1, 1), jnp.float32)
    for k in range(strips):
        numer = numer + heard_ref[k, 0:1, 3 * block : 3 * block + 1]
        denom = denom + heard_ref[k, 0:1, 3 * block + 1 : 3 * block + 2]
    step = numer / (denom + epsilon)
    after = lax.rem(me + 1, strips)
    before = lax.rem(me + strips - 1, strips)
    total = own_ref[...] + jnp.concatenate([heard_ref[after], heard_ref[before]], axis=0)
    cross = pltpu.roll(total, span - block, 1)
    square = pltpu.roll(total, span - 2 * block, 1)
    gram = total - step * cross + step * step * square
    gram = jnp.concatenate([gram, jnp.zeros((LANES - 2 * blocks, span), jnp.float32)], axis=0)
    gram = jnp.where(iota(gram.shape, 1) < block, gram, 0.0)
    gram = pick_rows(select_ref[...], gram)
    factors = shrink_factors(gram, held, frames)
    shift = offset_row(offsets_ref, 1, 1, length)
    column = iota((LANES, length), 1)
    row = iota((LANES, length), 0)
    broad = [in_block(column, shift, row - part * blocks, length).astype(jnp.float32) for part in range(2)]
    spread[...] = pick(factors, jnp.concatenate(broad, axis=1))
    edge = upper_rows(offsets_ref, length)
    moved = [est_ref[f] - step * grad_ref[f] for f in range(frames)]
    for t in range(BS // 8):
        low = iota((8, length), 0) + 8 * t >= edge
        for f in range(frames):
            total = [jnp.zeros((8, length), jnp.float32)] * 2
            for g in range(frames):
                at = f * frames + g
                factor = jnp.where(low, spread[at : at + 1, :length], spread[at : at + 1, length:])
                total = [total[p] + factor * moved[g][p * BS + 8 * t : p * BS + 8 * t + 8] for p in range(2)]
            for p in range(2):
                rows = slice(p * BS + 8 * t, p * BS + 8 * t + 8)
                out_ref[f, rows, :] = moved[f][rows] - total[p]


def place_kernel(offsets_ref, strips_ref, out_hbm, whole, sems):
    strips, _, length = strips_ref.shape
    width = strips * BS
    shift = offset_row(offsets_ref, 0, 0, length)
    copies = []
    for part in range(2):
        image = strips_ref[:, part * BS : (part + 1) * BS, :].reshape(width, length)
        step = 1
        while step < BS:
            image = jnp.where((shift & step) != 0, pltpu.roll(image, width - step, 0), image)
            step *= 2
        whole[part] = image
        copies.append(pltpu.make_async_copy(whole.at[part], out_hbm.at[0, part], sems.at[part]))
        copies[-1].start()
    for copy in copies:
        copy.wait()


def vmem():
    return pl.BlockSpec(memory_space=pltpu.VMEM)


def hbm():
    return pl.BlockSpec(memory_space=pltpu.HBM)


def f32(*shape):
    return jax.ShapeDtypeStruct(shape, jnp.float32)


def exchange(blocks):
    return lax.all_to_all(blocks, "tm", split_axis=0, concat_axis=0, tiled=True)


def params(mebibytes=16):
    return pltpu.CompilerParams(vmem_limit_bytes=mebibytes * 1024 * 1024)


def frame_call(start_image, sensitivity, kspace, sampled, offsets, table):
    _, _, width, length = start_image.shape
    coils = sensitivity.shape[0]
    rows = 4 * BS
    chunks = width // rows
    return pl.pallas_call(
        frame_kernel,
        out_shape=(
            pltpu.VMEM((width // BS, length // LANES * (4 * BS + coils) + 8, LANES), jnp.float32),
            pltpu.VMEM((coils, 2, BS, length), jnp.float32),
            pltpu.VMEM((SUBLANES, LANES), jnp.int32),
        ),
        in_specs=[hbm()] * 6,
        out_specs=(vmem(),) * 3,
        scratch_shapes=[
            pltpu.SMEM(offsets.shape, jnp.int32),
            pltpu.VMEM(start_image.shape, jnp.float32),
            pltpu.VMEM((chunks, coils, 2, rows, length), jnp.bfloat16),
            pltpu.VMEM((chunks, coils, 2, rows, length), jnp.bfloat16),
            pltpu.VMEM(sampled.shape, jnp.int32),
            pltpu.VMEM(table.shape, jnp.bfloat16),
            pltpu.VMEM((2, width, length), jnp.float32),
            pltpu.VMEM((chunks, coils * rows, 2 * length), jnp.bfloat16),
            pltpu.VMEM((chunks, coils * rows, 2 * length), jnp.bfloat16),
            pltpu.SemaphoreType.DMA((4,)),
            pltpu.SemaphoreType.DMA((2, chunks)),
        ],
        compiler_params=params(60),
        name="frame_gradient",
    )(offsets, start_image, sensitivity, kspace, sampled, table)


def middle_call(mail, sens, offsets, table):
    frames = mail.shape[0]
    coils, _, _, length = sens.shape
    count = frames * frames
    blocks = length // BS
    group = 4
    return pl.pallas_call(
        middle_kernel,
        out_shape=(
            f32(frames, blocks, LANES),
            f32(2 * blocks, LANES),
            f32(frames, 2 * BS, length),
            f32(frames, 2 * BS, length),
        ),
        in_specs=[vmem()] * 4,
        out_specs=(vmem(),) * 4,
        scratch_shapes=[
            pltpu.VMEM((length // LANES, 2 * LANES * 8, LANES), jnp.float32),
            pltpu.VMEM((NEWTON, count, LANES), jnp.float32),
            pltpu.VMEM((count, length), jnp.float32),
            pltpu.VMEM((frames // group, group * coils * BS, 2 * length), jnp.bfloat16),
            pltpu.VMEM((frames // group, group * coils * BS, 2 * length), jnp.bfloat16),
        ],
        compiler_params=params(),
        name="strip_shrink_gradient",
    )(offsets, mail, sens, table)


def last_call(own, heard, estimate, gradient, offsets):
    frames, strip, length = estimate.shape
    count = frames * frames
    return pl.pallas_call(
        last_kernel,
        out_shape=f32(frames, strip, length),
        in_specs=[vmem()] * 6,
        out_specs=vmem(),
        scratch_shapes=[
            pltpu.VMEM((NEWTON, count, LANES), jnp.float32),
            pltpu.VMEM((count, 2 * length), jnp.float32),
        ],
        compiler_params=params(),
        name="strip_shrink",
    )(offsets, own, heard, estimate, gradient, jnp.asarray(pair_select(frames, LANES)))


def place_call(strips, offsets):
    count, strip, length = strips.shape
    width = count * strip // 2
    return pl.pallas_call(
        place_kernel,
        out_shape=f32(1, 2, width, length),
        in_specs=[vmem()] * 2,
        out_specs=hbm(),
        scratch_shapes=[pltpu.VMEM((2, width, length), jnp.float32), pltpu.SemaphoreType.DMA((2,))],
        compiler_params=params(),
        name="frame_place",
    )(offsets, strips)


def strips_body(start_image, sensitivity, kspace, sampled, offsets):
    table = jnp.asarray(wide_table(start_image.shape[3]))
    mail, sens, offsets = frame_call(start_image, sensitivity, kspace, sampled, offsets, table)
    mail = exchange(mail)
    sent, own, estimate, gradient = middle_call(mail, sens, offsets, table)
    returned = exchange(last_call(own, exchange(sent), estimate, gradient, offsets))
    return place_call(returned, offsets)


def fits_strips(start_image, sensitivity, kspace, sampled, offsets):
    strips = lax.axis_size("tm")
    frames, _, width, length = start_image.shape
    coils = sensitivity.shape[0]
    kinds = 3 * len(pair_list(strips))
    return (
        frames == 1
        and width == strips * BS
        and strips == SUBLANES
        and coils % SUBLANES == 0
        and ITERS == 2
        and length % LANES == 0
        and 2 * (length // BS) <= LANES
        and kinds + 2 <= LANES
    )


def body(*args):
    return (strips_body if fits_strips(*args) else whole_body)(*args)


def solution(mesh):
    placed = (
        P(("cuts", "tm"), None, None, None),
        P("cuts", None, None, None),
        P(("cuts", "tm"), None, None, None, None),
        P(("cuts", "tm"), None, None),
        P("cuts", None),
    )
    return jax.shard_map(
        body,
        mesh=mesh,
        in_specs=placed,
        out_specs=P(("cuts", "tm"), None, None, None),
        check_vma=False,
    )
```

```python
import math

import jax
import jax.numpy as jnp
import ml_dtypes
import numpy as np
from jax import lax
from jax.experimental import pallas as pl
from jax.experimental.pallas import tpu as pltpu
from jax.sharding import PartitionSpec as P

BS = 16
ITERS = 2
NEWTON = 4
LANES = 128
SUBLANES = 8


shrink_ratio = 0.5
epsilon = 1e-06


def dft_tables(length):
    indices = jnp.arange(length, dtype=jnp.int32)
    phases = indices[:, None] * indices[None, :] % length
    angles = phases.astype(jnp.float32) * (2.0 * math.pi / length)
    norm_scale = 1.0 / math.sqrt(length)
    return (
        (jnp.cos(angles) * norm_scale).astype(jnp.bfloat16),
        (jnp.sin(angles) * norm_scale).astype(jnp.bfloat16),
    )


def forward(real_part, imag_part, cosine_table, sine_table):
    out_real = jnp.dot(real_part, cosine_table, preferred_element_type=jnp.float32) + jnp.dot(
        imag_part, sine_table, preferred_element_type=jnp.float32
    )
    out_imag = jnp.dot(imag_part, cosine_table, preferred_element_type=jnp.float32) - jnp.dot(
        real_part, sine_table, preferred_element_type=jnp.float32
    )
    return (out_real, out_imag)


def inverse(real_part, imag_part, cosine_table, sine_table):
    out_real = jnp.dot(real_part, cosine_table, preferred_element_type=jnp.float32) - jnp.dot(
        imag_part, sine_table, preferred_element_type=jnp.float32
    )
    out_imag = jnp.dot(imag_part, cosine_table, preferred_element_type=jnp.float32) + jnp.dot(
        real_part, sine_table, preferred_element_type=jnp.float32
    )
    return (out_real, out_imag)


def coil_spectra(field, sens_real, sens_imag, cosine_table, sine_table):
    coils, width, length = sens_real.shape
    coil_real = (
        (sens_real * field[0] - sens_imag * field[1])
        .astype(jnp.bfloat16)
        .reshape(coils * width, length)
    )
    coil_imag = (
        (sens_real * field[1] + sens_imag * field[0])
        .astype(jnp.bfloat16)
        .reshape(coils * width, length)
    )
    spec_real, spec_imag = forward(coil_real, coil_imag, cosine_table, sine_table)
    return (spec_real.reshape(coils, width, length), spec_imag.reshape(coils, width, length))


def frame_terms(field, sensitivity, data, lines, cosine_table, sine_table):
    sens_real = sensitivity[:, 0].astype(jnp.float32)
    sens_imag = sensitivity[:, 1].astype(jnp.float32)
    coils, width, length = sens_real.shape
    weight = lines.astype(jnp.float32)[:, None, :]
    spec_real, spec_imag = coil_spectra(field, sens_real, sens_imag, cosine_table, sine_table)
    misfit_real = (weight * (spec_real - data[:, 0].astype(jnp.float32))).astype(jnp.bfloat16)
    misfit_imag = (weight * (spec_imag - data[:, 1].astype(jnp.float32))).astype(jnp.bfloat16)
    back_real, back_imag = inverse(
        misfit_real.reshape(coils * width, length),
        misfit_imag.reshape(coils * width, length),
        cosine_table,
        sine_table,
    )
    back_real = back_real.reshape(coils, width, length)
    back_imag = back_imag.reshape(coils, width, length)
    grad_real = jnp.sum(sens_real * back_real + sens_imag * back_imag, axis=0)
    grad_imag = jnp.sum(sens_real * back_imag - sens_imag * back_real, axis=0)
    gradient = jnp.stack([grad_real, grad_imag])
    numerator = jnp.sum(gradient * gradient)
    probe_real, probe_imag = coil_spectra(gradient, sens_real, sens_imag, cosine_table, sine_table)
    denominator = jnp.sum(weight * (probe_real * probe_real + probe_imag * probe_imag))
    return (gradient, numerator, denominator)


def shrink(casorati):
    highest = lax.Precision.HIGHEST
    gram = jnp.einsum("bfv,bgv->bfg", casorati, casorati, precision=highest)
    frames = gram.shape[1]
    identity = jnp.eye(frames, dtype=jnp.float32)
    shrink_level = shrink_ratio * jnp.trace(gram, axis1=1, axis2=2) / frames + epsilon
    system = gram + shrink_level[:, None, None] * identity
    row_bound = jnp.max(jnp.sum(jnp.abs(system), axis=2), axis=1)
    approx = identity[None] / row_bound[:, None, None]
    for newton in range(NEWTON):
        product = jnp.einsum("bfg,bgh->bfh", system, approx, precision=highest)
        approx = jnp.einsum("bfg,bgh->bfh", approx, 2.0 * identity - product, precision=highest)
    return casorati - shrink_level[:, None, None] * jnp.einsum(
        "bfg,bgv->bfv", approx, casorati, precision=highest
    )


def to_blocks(field):
    frames, parts, width, length = field.shape
    blocks = field.reshape(frames, parts, width // BS, BS, length // BS, BS)
    blocks = blocks.transpose(2, 4, 0, 1, 3, 5)
    return blocks.reshape(width // BS * (length // BS), frames, parts * BS * BS)


def from_blocks(blocks, width, length):
    frames = blocks.shape[1]
    field = blocks.reshape(width // BS, length // BS, frames, 2, BS, BS)
    field = field.transpose(2, 3, 0, 4, 1, 5)
    return field.reshape(frames, 2, width, length)


def whole_body(start_image, sensitivity, kspace, sampled, offsets):
    width, length = (start_image.shape[2], start_image.shape[3])
    cosine_table, sine_table = dft_tables(length)
    estimate = start_image

    def per_frame(frame_items):
        field, data, lines = frame_items
        return frame_terms(field, sensitivity, data, lines, cosine_table, sine_table)

    for iteration in range(ITERS):
        gradient, numerator, denominator = lax.map(per_frame, (estimate, kspace, sampled))
        offset_pair = offsets[iteration]
        totals = lax.psum((jnp.sum(numerator), jnp.sum(denominator)), "tm")
        step_length = totals[0] / (totals[1] + epsilon)
        moved = estimate - step_length * gradient
        rolled = jnp.roll(moved, (offset_pair[0], offset_pair[1]), axis=(2, 3))
        casorati = lax.all_to_all(to_blocks(rolled), "tm", split_axis=0, concat_axis=1, tiled=True)
        shrunk = shrink(casorati)
        returned = lax.all_to_all(shrunk, "tm", split_axis=1, concat_axis=0, tiled=True)
        placed = from_blocks(returned, width, length)
        estimate = jnp.roll(placed, (-offset_pair[0], -offset_pair[1]), axis=(2, 3))
    return estimate


def iota(shape, dim):
    return lax.broadcasted_iota(jnp.int32, shape, dim)


def in_block(column, shift, block, length):
    moved = column + shift
    moved = jnp.where(moved >= length, moved - length, moved)
    return (moved >= block * BS) & (moved < block * BS + BS)


def offset_row(offsets_ref, iteration, axis, lanes):
    at = 2 * iteration + axis
    return jnp.concatenate([offsets_ref[at : at + 1, :]] * (lanes // LANES), axis=1)


def upper_rows(offsets_ref, length):
    edge = offset_row(offsets_ref, 0, 0, length) - offset_row(offsets_ref, 1, 0, length)
    return jnp.where(edge < 0, edge + BS, edge)


def wide_table(length):
    indices = np.arange(length, dtype=np.int32)
    phases = indices[:, None] * indices[None, :] % length
    angles = phases.astype(np.float32) * np.float32(2.0 * math.pi / length)
    norm_scale = np.float32(1.0 / math.sqrt(length))
    cosine = (np.cos(angles) * norm_scale).astype(ml_dtypes.bfloat16)
    sine = (np.sin(angles) * norm_scale).astype(ml_dtypes.bfloat16)
    return np.block([[cosine, -sine], [sine, cosine]])


def pair_list(frames):
    return [(f, g) for f in range(frames) for g in range(f, frames)]


def pair_select(frames, lanes):
    table = np.zeros((frames * frames, lanes), np.float32)
    for place, (f, g) in enumerate(pair_list(frames)):
        table[f * frames + g, place] = 1.0
        table[g * frames + f, place] = 1.0
    return table


def pieces(x):
    first = x.astype(jnp.bfloat16)
    rest = x - first.astype(jnp.float32)
    second = rest.astype(jnp.bfloat16)
    third = (rest - second.astype(jnp.float32)).astype(jnp.bfloat16)
    return jnp.concatenate([first, second, third], axis=0)


def pick(x, ones):
    rows = x.shape[0]
    out = mxu(pieces(x), ones.astype(jnp.float32).astype(jnp.bfloat16))
    return out[:rows] + out[rows : 2 * rows] + out[2 * rows :]


def pick_rows(ones, x):
    rows = x.shape[0]
    out = lax.dot_general(
        ones.astype(jnp.float32).astype(jnp.bfloat16), pieces(x), (((1,), (1,)), ((), ())), preferred_element_type=jnp.float32
    )
    return out[:, :rows] + out[:, rows : 2 * rows] + out[:, 2 * rows :]


def mxu(a, b):
    return jnp.dot(a, b, preferred_element_type=jnp.float32)


def fold(x):
    rows, length = x.shape
    return jnp.sum(x.reshape(rows // 8, 8, length), axis=0)


def frame_kernel(
    offsets_hbm, start_hbm, sens_hbm, data_hbm, lines_hbm, table_hbm, out_ref, strip_ref, copied_ref,
    offsets_ref, start_ref, sens_ref, data_ref, lines_ref, table_ref, grad, left, right, sems, chunk_sems,
):
    chunks, coils, _, rows, length = sens_ref.shape
    start_copy, lines_copy, table_copy, offsets_copy = (
        pltpu.make_async_copy(source, target, sems.at[k])
        for k, (source, target) in enumerate(
            ((start_hbm, start_ref), (lines_hbm, lines_ref), (table_hbm, table_ref), (offsets_hbm, offsets_ref))
        )
    )
    sens_copy = [
        pltpu.make_async_copy(sens_hbm.at[:, :, pl.ds(i * rows, rows), :], sens_ref.at[i], chunk_sems.at[0, i])
        for i in range(chunks)
    ]
    data_copy = [
        pltpu.make_async_copy(data_hbm.at[0, :, :, pl.ds(i * rows, rows), :], data_ref.at[i], chunk_sems.at[1, i])
        for i in range(chunks)
    ]
    offsets_copy.start()
    start_copy.start()
    lines_copy.start()
    sens_copy[0].start()
    table_copy.start()
    for copy in sens_copy[1:] + data_copy:
        copy.start()
    strips = out_ref.shape[0]
    halves = length // LANES
    strip = 2 * BS

    def coil_image(i, a, b):
        for c in range(coils):
            sr = sens_ref[i, c, 0].astype(jnp.float32)
            si = sens_ref[i, c, 1].astype(jnp.float32)
            at = slice(c * rows, (c + 1) * rows)
            left[i, at, :length] = (sr * a - si * b).astype(jnp.bfloat16)
            left[i, at, length:] = (sr * b + si * a).astype(jnp.bfloat16)

    def post(kind, image):
        shift = offsets_ref[0, 0]
        for part in range(2):
            rolled = pltpu.roll(image[part], shift, 0)
            for half in range(halves):
                base = (kind * halves + half) * strip + part * BS
                out_ref[:, base : base + BS, :] = rolled[:, half * LANES : (half + 1) * LANES].reshape(strips, BS, LANES)

    offsets_copy.wait()
    start_copy.wait()
    lines_copy.wait()
    copied = jnp.zeros(copied_ref.shape, jnp.int32)
    for k in range(ITERS):
        for axis in range(2):
            copied = jnp.where(iota(copied.shape, 0) == 2 * k + axis, offsets_ref[k, axis], copied)
    copied_ref[...] = copied
    weight = lines_ref[0].astype(jnp.float32)
    post(0, start_ref.at[0])
    for target in range(strips):
        for half in range(halves):
            base = 2 * halves * strip + half * coils
            out_ref[target, base : base + coils, :] = weight[:, half * LANES : (half + 1) * LANES]
    spec = []
    for i in range(chunks):
        sens_copy[i].wait()
        if i == 0:
            table_copy.wait()
        coil_image(i, start_ref[0, 0, i * rows : (i + 1) * rows], start_ref[0, 1, i * rows : (i + 1) * rows])
        spec.append(mxu(left[i], table_ref[...]))
    me = lax.axis_index("tm")
    each = rows // BS
    pair = []
    for place in (lax.rem(me + strips - 1, strips), me):
        pair.append((place // each, pl.ds(pl.multiple_of(lax.rem(place, each) * BS, BS), BS)))
    shift = offsets_ref[0, 0]
    for c in range(coils):
        for part in range(2):
            two = jnp.concatenate([sens_ref[i, c, part, at, :] for i, at in pair], axis=0).astype(jnp.float32)
            strip_ref[c, part] = pltpu.roll(two, shift, 0)[BS:]
    home = []
    for i in range(chunks):
        data_copy[i].wait()
        for c in range(coils):
            at = slice(c * rows, (c + 1) * rows)
            w = weight[c : c + 1]
            right[i, at, :length] = (w * (spec[i][at, :length] - data_ref[i, c, 0].astype(jnp.float32))).astype(jnp.bfloat16)
            right[i, at, length:] = (w * (data_ref[i, c, 1].astype(jnp.float32) - spec[i][at, length:])).astype(jnp.bfloat16)
        home.append(mxu(right[i], table_ref[...]))
    num = jnp.zeros((8, length), jnp.float32)
    probe = []
    for i in range(chunks):
        for first in range(0, rows, 2 * BS):
            some = slice(first, first + 2 * BS)
            gr = jnp.zeros((2 * BS, length), jnp.float32)
            gi = jnp.zeros((2 * BS, length), jnp.float32)
            for c in range(coils):
                sr = sens_ref[i, c, 0, some].astype(jnp.float32)
                si = sens_ref[i, c, 1, some].astype(jnp.float32)
                at = slice(c * rows + first, c * rows + first + 2 * BS)
                br, bi = home[i][at, :length], home[i][at, length:]
                gr = gr + (sr * br - si * bi)
                gi = gi - (sr * bi + si * br)
            grad[0, i * rows + first : i * rows + first + 2 * BS, :] = gr
            grad[1, i * rows + first : i * rows + first + 2 * BS, :] = gi
            num = num + fold(gr * gr + gi * gi)
        coil_image(i, grad[0, i * rows : (i + 1) * rows], grad[1, i * rows : (i + 1) * rows])
        probe.append(mxu(left[i], table_ref[...]))
    post(1, grad)
    den = jnp.zeros((8, length), jnp.float32)
    for i in range(chunks):
        for c in range(coils):
            at = slice(c * rows, (c + 1) * rows)
            pr, pi = probe[i][at, :length], probe[i][at, length:]
            den = den + weight[c : c + 1] * fold(pr * pr + pi * pi)
    numer = jnp.sum(jnp.sum(num, axis=0, keepdims=True), axis=1, keepdims=True)
    denom = jnp.sum(jnp.sum(den, axis=0, keepdims=True), axis=1, keepdims=True)
    sums = jnp.where(iota((8, LANES), 0) == 0, numer, denom)
    base = 2 * halves * strip + halves * coils
    for target in range(strips):
        out_ref[target, base : base + 8, :] = sums


def newton_inverse(system, held, frames):
    place = iota(system[0].shape, 0)
    unit = [(place == f).astype(jnp.float32) for f in range(frames)]
    bound = jnp.max(sum(jnp.abs(tile) for tile in system), axis=0, keepdims=True)
    scale = 1.0 / bound

    def times(ref, tiles):
        out = []
        for f in range(frames):
            terms = [ref[f * frames + g : f * frames + g + 1, :] * tiles[g] for g in range(frames)]
            while len(terms) > 1:
                terms = [a + b for a, b in zip(terms[::2], terms[1::2])]
            out.append(terms[0])
        return out

    power = [unit[f] - scale * system[f] for f in range(frames)]
    total = [unit[f] + power[f] for f in range(frames)]
    for newton in range(1, NEWTON):
        for f in range(frames):
            held[newton, f * frames : (f + 1) * frames, :] = power[f]
        power = times(held.at[newton], power)
        for f in range(frames):
            held[0, f * frames : (f + 1) * frames, :] = power[f]
        added = times(held.at[0], total)
        total = [total[f] + added[f] for f in range(frames)]
    return [scale * tile for tile in total]


def shrink_factors(gram, held, frames):
    lanes = gram.shape[1]
    place = iota((frames, lanes), 0)
    tiles = [gram[f * frames : (f + 1) * frames, :] for f in range(frames)]
    trace = sum(gram[f * frames + f : f * frames + f + 1, :] for f in range(frames))
    level = shrink_ratio * trace / frames + epsilon
    system = [tiles[f] + jnp.where(place == f, level, 0.0) for f in range(frames)]
    approx = newton_inverse(system, held, frames)
    return jnp.concatenate([level * tile for tile in approx], axis=0)


def middle_kernel(
    offsets_ref, mail_ref, sens_ref, table_ref,
    out_ref, own_ref, est_ref, grad_ref,
    terms, held, spread, left, right,
):
    frames = mail_ref.shape[0]
    coils, _, _, length = sens_ref.shape
    pairs = pair_list(frames)
    strip = 2 * BS
    halves = length // LANES

    def mail(f, kind, first, rows):
        return jnp.concatenate(
            [
                mail_ref[f, (kind * halves + half) * strip + first : (kind * halves + half) * strip + first + rows, :]
                for half in range(halves)
            ],
            axis=1,
        )

    def mask(f):
        base = 2 * halves * strip
        return jnp.concatenate(
            [mail_ref[f, base + half * coils : base + (half + 1) * coils, :] for half in range(halves)], axis=1
        )

    place = 2 * halves * strip + halves * coils
    totals = sum(mail_ref[f, place : place + 8, :] for f in range(frames))
    step = totals[:1] / (totals[1:2] + epsilon)
    step = jnp.concatenate([step] * halves, axis=1)
    for f in range(frames):
        est_ref[f] = mail(f, 0, 0, strip) - step * mail(f, 1, 0, strip)
    for f, g in pairs:
        tile = fold(est_ref[f] * est_ref[g])
        for place in {f * frames + g, g * frames + f}:
            for half in range(length // LANES):
                terms[half, place * 8 : place * 8 + 8, :] = tile[:, half * LANES : (half + 1) * LANES]
    count = frames * frames
    sums = jnp.concatenate(
        [sum(terms[half, pl.ds(s, count, stride=8), :] for s in range(8)) for half in range(length // LANES)], axis=1
    )
    tall = in_block(iota((length, LANES), 0), offset_row(offsets_ref, 0, 1, LANES), iota((length, LANES), 1), length)
    broad = in_block(iota((LANES, length), 1), offset_row(offsets_ref, 0, 1, length), iota((LANES, length), 0), length)
    factors = shrink_factors(pick(sums, tall), held, frames)
    spread[...] = pick(factors, broad)
    moved = [est_ref[f] for f in range(frames)]
    for f in range(frames):
        total = spread[f * frames : f * frames + 1, :] * moved[0]
        for g in range(1, frames):
            total = total + spread[f * frames + g : f * frames + g + 1, :] * moved[g]
        grad_ref[f] = moved[f] - total
    for f in range(frames):
        est_ref[f] = grad_ref[f]

    num = jnp.zeros((8, length), jnp.float32)
    den = jnp.zeros((8, length), jnp.float32)
    group = left.shape[1] // (coils * BS)

    def coil_image(index, values):
        for k, (a, b) in enumerate(values):
            for c in range(coils):
                sr, si = sens_ref[c, 0], sens_ref[c, 1]
                at = slice((k * coils + c) * BS, (k * coils + c + 1) * BS)
                left[index, at, :length] = (sr * a - si * b).astype(jnp.bfloat16)
                left[index, at, length:] = (sr * b + si * a).astype(jnp.bfloat16)

    edge = upper_rows(offsets_ref, length)
    low = [(iota((8, length), 0) + 8 * t >= edge) for t in range(BS // 8)]
    block = len(pairs)
    span = out_ref.shape[2]

    def rows_of(product):
        return [
            sum(product[p * BS + 8 * t : p * BS + 8 * t + 8] for p in range(2)) for t in range(BS // 8)
        ]

    def put(part, place, tile):
        for half in range(length // LANES):
            terms[half, (part * span + place) * 8 : (part * span + place) * 8 + 8, :] = tile[
                :, half * LANES : (half + 1) * LANES
            ]

    def put_kind(kind, product_of):
        for place, pair in enumerate(pairs):
            rows = rows_of(product_of(*pair))
            put(0, kind * block + place, sum(jnp.where(low[t], rows[t], 0.0) for t in range(BS // 8)))
            put(1, kind * block + place, sum(jnp.where(low[t], 0.0, rows[t]) for t in range(BS // 8)))

    groups = [range(at, at + group) for at in range(0, frames, group)]
    weights = [mask(f) for f in range(frames)]
    spec = []
    for index, members in enumerate(groups):
        coil_image(
            index,
            [(est_ref[f, :BS, :] - mail(f, 0, 0, BS), est_ref[f, BS:strip, :] - mail(f, 0, BS, BS)) for f in members],
        )
        spec.append(mxu(left[index], table_ref[...]))
    for part in range(2):
        for place in range(3 * block, span):
            put(part, place, jnp.zeros((8, length), jnp.float32))
    put_kind(0, lambda f, g: est_ref[f] * est_ref[g])
    home = []
    for index, members in enumerate(groups):
        for k, f in enumerate(members):
            for c in range(coils):
                at = slice((k * coils + c) * BS, (k * coils + c + 1) * BS)
                w = weights[f][c : c + 1]
                right[index, at, :length] = (w * spec[index][at, :length]).astype(jnp.bfloat16)
                right[index, at, length:] = (-w * spec[index][at, length:]).astype(jnp.bfloat16)
        home.append(mxu(right[index], table_ref[...]))
    probe = []
    for index, members in enumerate(groups):
        values = []
        for k, f in enumerate(members):
            gr = mail(f, 1, 0, BS)
            gi = mail(f, 1, BS, BS)
            for c in range(coils):
                at = slice((k * coils + c) * BS, (k * coils + c + 1) * BS)
                sr, si = sens_ref[c, 0], sens_ref[c, 1]
                br, bi = home[index][at, :length], home[index][at, length:]
                gr = gr + (sr * br - si * bi)
                gi = gi - (sr * bi + si * br)
            grad_ref[f, :BS, :] = gr
            grad_ref[f, BS:strip, :] = gi
            num = num + fold(gr * gr + gi * gi)
            values.append((gr, gi))
        coil_image(index, values)
        probe.append(mxu(left[index], table_ref[...]))
    put_kind(1, lambda f, g: est_ref[f] * grad_ref[g] + est_ref[g] * grad_ref[f])
    put_kind(2, lambda f, g: grad_ref[f] * grad_ref[g])
    for index, members in enumerate(groups):
        for k, f in enumerate(members):
            for c in range(coils):
                at = slice((k * coils + c) * BS, (k * coils + c + 1) * BS)
                pr, pi = probe[index][at, :length], probe[index][at, length:]
                den = den + weights[f][c : c + 1] * fold(pr * pr + pi * pi)
    numer = jnp.sum(jnp.sum(num, axis=0, keepdims=True), axis=1, keepdims=True)
    denom = jnp.sum(jnp.sum(den, axis=0, keepdims=True), axis=1, keepdims=True)

    blocks = length // BS
    shift = offset_row(offsets_ref, 1, 1, length)
    member = in_block(iota((blocks, length), 1), shift, iota((blocks, length), 0), length)
    lane = iota((blocks, span), 1)
    packs = []
    for part in range(2):
        sums = jnp.concatenate(
            [
                sum(terms[half, pl.ds(part * span * 8 + s, span, stride=8), :] for s in range(8))
                for half in range(length // LANES)
            ],
            axis=1,
        )
        pack = pick_rows(member, sums)
        pack = jnp.where(lane == 3 * block, numer, jnp.where(lane == 3 * block + 1, denom, pack))
        own_ref[part * blocks : (part + 1) * blocks, :] = pack
        packs.append(pack)
    me = lax.axis_index("tm")
    strips = out_ref.shape[0]
    before = lax.rem(me + strips - 1, strips)
    for target in range(strips):
        out_ref[target] = jnp.where(before == target, packs[1], packs[0])


def last_kernel(offsets_ref, own_ref, heard_ref, est_ref, grad_ref, select_ref, out_ref, held, spread):
    frames, strip, length = est_ref.shape
    strips, blocks, span = heard_ref.shape
    block = len(pair_list(frames))
    me = lax.axis_index("tm")
    numer = jnp.zeros((1, 1), jnp.float32)
    denom = jnp.zeros((1, 1), jnp.float32)
    for k in range(strips):
        numer = numer + heard_ref[k, 0:1, 3 * block : 3 * block + 1]
        denom = denom + heard_ref[k, 0:1, 3 * block + 1 : 3 * block + 2]
    step = numer / (denom + epsilon)
    after = lax.rem(me + 1, strips)
    before = lax.rem(me + strips - 1, strips)
    total = own_ref[...] + jnp.concatenate([heard_ref[after], heard_ref[before]], axis=0)
    cross = pltpu.roll(total, span - block, 1)
    square = pltpu.roll(total, span - 2 * block, 1)
    gram = total - step * cross + step * step * square
    gram = jnp.concatenate([gram, jnp.zeros((LANES - 2 * blocks, span), jnp.float32)], axis=0)
    gram = jnp.where(iota(gram.shape, 1) < block, gram, 0.0)
    gram = pick_rows(select_ref[...], gram)
    factors = shrink_factors(gram, held, frames)
    shift = offset_row(offsets_ref, 1, 1, length)
    column = iota((LANES, length), 1)
    row = iota((LANES, length), 0)
    broad = [in_block(column, shift, row - part * blocks, length).astype(jnp.float32) for part in range(2)]
    spread[...] = pick(factors, jnp.concatenate(broad, axis=1))
    edge = upper_rows(offsets_ref, length)
    moved = [est_ref[f] - step * grad_ref[f] for f in range(frames)]
    for t in range(BS // 8):
        low = iota((8, length), 0) + 8 * t >= edge
        for f in range(frames):
            total = [jnp.zeros((8, length), jnp.float32)] * 2
            for g in range(frames):
                at = f * frames + g
                factor = jnp.where(low, spread[at : at + 1, :length], spread[at : at + 1, length:])
                total = [total[p] + factor * moved[g][p * BS + 8 * t : p * BS + 8 * t + 8] for p in range(2)]
            for p in range(2):
                rows = slice(p * BS + 8 * t, p * BS + 8 * t + 8)
                out_ref[f, rows, :] = moved[f][rows] - total[p]


def place_kernel(offsets_ref, strips_ref, out_hbm, whole, sems):
    strips, _, length = strips_ref.shape
    width = strips * BS
    shift = offset_row(offsets_ref, 0, 0, length)
    copies = []
    for part in range(2):
        image = strips_ref[:, part * BS : (part + 1) * BS, :].reshape(width, length)
        step = 1
        while step < BS:
            image = jnp.where((shift & step) != 0, pltpu.roll(image, width - step, 0), image)
            step *= 2
        whole[part] = image
        copies.append(pltpu.make_async_copy(whole.at[part], out_hbm.at[0, part], sems.at[part]))
        copies[-1].start()
    for copy in copies:
        copy.wait()


def vmem():
    return pl.BlockSpec(memory_space=pltpu.VMEM)


def hbm():
    return pl.BlockSpec(memory_space=pltpu.HBM)


def f32(*shape):
    return jax.ShapeDtypeStruct(shape, jnp.float32)


def exchange(blocks):
    return lax.all_to_all(blocks, "tm", split_axis=0, concat_axis=0, tiled=True)


def params(mebibytes=16):
    return pltpu.CompilerParams(vmem_limit_bytes=mebibytes * 1024 * 1024)


def frame_call(start_image, sensitivity, kspace, sampled, offsets, table):
    _, _, width, length = start_image.shape
    coils = sensitivity.shape[0]
    rows = width
    chunks = width // rows
    return pl.pallas_call(
        frame_kernel,
        out_shape=(
            pltpu.VMEM((width // BS, length // LANES * (4 * BS + coils) + 8, LANES), jnp.float32),
            pltpu.VMEM((coils, 2, BS, length), jnp.float32),
            pltpu.VMEM((SUBLANES, LANES), jnp.int32),
        ),
        in_specs=[hbm()] * 6,
        out_specs=(vmem(),) * 3,
        scratch_shapes=[
            pltpu.SMEM(offsets.shape, jnp.int32),
            pltpu.VMEM(start_image.shape, jnp.float32),
            pltpu.VMEM((chunks, coils, 2, rows, length), jnp.bfloat16),
            pltpu.VMEM((chunks, coils, 2, rows, length), jnp.bfloat16),
            pltpu.VMEM(sampled.shape, jnp.int32),
            pltpu.VMEM(table.shape, jnp.bfloat16),
            pltpu.VMEM((2, width, length), jnp.float32),
            pltpu.VMEM((chunks, coils * rows, 2 * length), jnp.bfloat16),
            pltpu.VMEM((chunks, coils * rows, 2 * length), jnp.bfloat16),
            pltpu.SemaphoreType.DMA((4,)),
            pltpu.SemaphoreType.DMA((2, chunks)),
        ],
        compiler_params=params(60),
        name="frame_gradient",
    )(offsets, start_image, sensitivity, kspace, sampled, table)


def middle_call(mail, sens, offsets, table):
    frames = mail.shape[0]
    coils, _, _, length = sens.shape
    count = frames * frames
    blocks = length // BS
    group = frames
    return pl.pallas_call(
        middle_kernel,
        out_shape=(
            f32(frames, blocks, LANES),
            f32(2 * blocks, LANES),
            f32(frames, 2 * BS, length),
            f32(frames, 2 * BS, length),
        ),
        in_specs=[vmem()] * 4,
        out_specs=(vmem(),) * 4,
        scratch_shapes=[
            pltpu.VMEM((length // LANES, 2 * LANES * 8, LANES), jnp.float32),
            pltpu.VMEM((NEWTON, count, LANES), jnp.float32),
            pltpu.VMEM((count, length), jnp.float32),
            pltpu.VMEM((frames // group, group * coils * BS, 2 * length), jnp.bfloat16),
            pltpu.VMEM((frames // group, group * coils * BS, 2 * length), jnp.bfloat16),
        ],
        compiler_params=params(),
        name="strip_shrink_gradient",
    )(offsets, mail, sens, table)


def last_call(own, heard, estimate, gradient, offsets):
    frames, strip, length = estimate.shape
    count = frames * frames
    return pl.pallas_call(
        last_kernel,
        out_shape=f32(frames, strip, length),
        in_specs=[vmem()] * 6,
        out_specs=vmem(),
        scratch_shapes=[
            pltpu.VMEM((NEWTON, count, LANES), jnp.float32),
            pltpu.VMEM((count, 2 * length), jnp.float32),
        ],
        compiler_params=params(),
        name="strip_shrink",
    )(offsets, own, heard, estimate, gradient, jnp.asarray(pair_select(frames, LANES)))


def place_call(strips, offsets):
    count, strip, length = strips.shape
    width = count * strip // 2
    return pl.pallas_call(
        place_kernel,
        out_shape=f32(1, 2, width, length),
        in_specs=[vmem()] * 2,
        out_specs=hbm(),
        scratch_shapes=[pltpu.VMEM((2, width, length), jnp.float32), pltpu.SemaphoreType.DMA((2,))],
        compiler_params=params(),
        name="frame_place",
    )(offsets, strips)


def strips_body(start_image, sensitivity, kspace, sampled, offsets):
    table = jnp.asarray(wide_table(start_image.shape[3]))
    mail, sens, offsets = frame_call(start_image, sensitivity, kspace, sampled, offsets, table)
    mail = exchange(mail)
    sent, own, estimate, gradient = middle_call(mail, sens, offsets, table)
    returned = exchange(last_call(own, exchange(sent), estimate, gradient, offsets))
    return place_call(returned, offsets)


def fits_strips(start_image, sensitivity, kspace, sampled, offsets):
    strips = lax.axis_size("tm")
    frames, _, width, length = start_image.shape
    coils = sensitivity.shape[0]
    kinds = 3 * len(pair_list(strips))
    return (
        frames == 1
        and width == strips * BS
        and strips == SUBLANES
        and coils % SUBLANES == 0
        and ITERS == 2
        and length % LANES == 0
        and 2 * (length // BS) <= LANES
        and kinds + 2 <= LANES
    )


def body(*args):
    return (strips_body if fits_strips(*args) else whole_body)(*args)


def solution(mesh):
    placed = (
        P(("cuts", "tm"), None, None, None),
        P("cuts", None, None, None),
        P(("cuts", "tm"), None, None, None, None),
        P(("cuts", "tm"), None, None),
        P("cuts", None),
    )
    return jax.shard_map(
        body,
        mesh=mesh,
        in_specs=placed,
        out_specs=P(("cuts", "tm"), None, None, None),
        check_vma=False,
    )
```

```python
import math

import jax
import jax.numpy as jnp
import ml_dtypes
import numpy as np
from jax import lax
from jax.experimental import pallas as pl
from jax.experimental.pallas import tpu as pltpu
from jax.sharding import PartitionSpec as P

BS = 16
ITERS = 2
NEWTON = 4
LANES = 128
SUBLANES = 8


shrink_ratio = 0.5
epsilon = 1e-06


def dft_tables(length):
    indices = jnp.arange(length, dtype=jnp.int32)
    phases = indices[:, None] * indices[None, :] % length
    angles = phases.astype(jnp.float32) * (2.0 * math.pi / length)
    norm_scale = 1.0 / math.sqrt(length)
    return (
        (jnp.cos(angles) * norm_scale).astype(jnp.bfloat16),
        (jnp.sin(angles) * norm_scale).astype(jnp.bfloat16),
    )


def forward(real_part, imag_part, cosine_table, sine_table):
    out_real = jnp.dot(real_part, cosine_table, preferred_element_type=jnp.float32) + jnp.dot(
        imag_part, sine_table, preferred_element_type=jnp.float32
    )
    out_imag = jnp.dot(imag_part, cosine_table, preferred_element_type=jnp.float32) - jnp.dot(
        real_part, sine_table, preferred_element_type=jnp.float32
    )
    return (out_real, out_imag)


def inverse(real_part, imag_part, cosine_table, sine_table):
    out_real = jnp.dot(real_part, cosine_table, preferred_element_type=jnp.float32) - jnp.dot(
        imag_part, sine_table, preferred_element_type=jnp.float32
    )
    out_imag = jnp.dot(imag_part, cosine_table, preferred_element_type=jnp.float32) + jnp.dot(
        real_part, sine_table, preferred_element_type=jnp.float32
    )
    return (out_real, out_imag)


def coil_spectra(field, sens_real, sens_imag, cosine_table, sine_table):
    coils, width, length = sens_real.shape
    coil_real = (
        (sens_real * field[0] - sens_imag * field[1])
        .astype(jnp.bfloat16)
        .reshape(coils * width, length)
    )
    coil_imag = (
        (sens_real * field[1] + sens_imag * field[0])
        .astype(jnp.bfloat16)
        .reshape(coils * width, length)
    )
    spec_real, spec_imag = forward(coil_real, coil_imag, cosine_table, sine_table)
    return (spec_real.reshape(coils, width, length), spec_imag.reshape(coils, width, length))


def frame_terms(field, sensitivity, data, lines, cosine_table, sine_table):
    sens_real = sensitivity[:, 0].astype(jnp.float32)
    sens_imag = sensitivity[:, 1].astype(jnp.float32)
    coils, width, length = sens_real.shape
    weight = lines.astype(jnp.float32)[:, None, :]
    spec_real, spec_imag = coil_spectra(field, sens_real, sens_imag, cosine_table, sine_table)
    misfit_real = (weight * (spec_real - data[:, 0].astype(jnp.float32))).astype(jnp.bfloat16)
    misfit_imag = (weight * (spec_imag - data[:, 1].astype(jnp.float32))).astype(jnp.bfloat16)
    back_real, back_imag = inverse(
        misfit_real.reshape(coils * width, length),
        misfit_imag.reshape(coils * width, length),
        cosine_table,
        sine_table,
    )
    back_real = back_real.reshape(coils, width, length)
    back_imag = back_imag.reshape(coils, width, length)
    grad_real = jnp.sum(sens_real * back_real + sens_imag * back_imag, axis=0)
    grad_imag = jnp.sum(sens_real * back_imag - sens_imag * back_real, axis=0)
    gradient = jnp.stack([grad_real, grad_imag])
    numerator = jnp.sum(gradient * gradient)
    probe_real, probe_imag = coil_spectra(gradient, sens_real, sens_imag, cosine_table, sine_table)
    denominator = jnp.sum(weight * (probe_real * probe_real + probe_imag * probe_imag))
    return (gradient, numerator, denominator)


def shrink(casorati):
    highest = lax.Precision.HIGHEST
    gram = jnp.einsum("bfv,bgv->bfg", casorati, casorati, precision=highest)
    frames = gram.shape[1]
    identity = jnp.eye(frames, dtype=jnp.float32)
    shrink_level = shrink_ratio * jnp.trace(gram, axis1=1, axis2=2) / frames + epsilon
    system = gram + shrink_level[:, None, None] * identity
    row_bound = jnp.max(jnp.sum(jnp.abs(system), axis=2), axis=1)
    approx = identity[None] / row_bound[:, None, None]
    for newton in range(NEWTON):
        product = jnp.einsum("bfg,bgh->bfh", system, approx, precision=highest)
        approx = jnp.einsum("bfg,bgh->bfh", approx, 2.0 * identity - product, precision=highest)
    return casorati - shrink_level[:, None, None] * jnp.einsum(
        "bfg,bgv->bfv", approx, casorati, precision=highest
    )


def to_blocks(field):
    frames, parts, width, length = field.shape
    blocks = field.reshape(frames, parts, width // BS, BS, length // BS, BS)
    blocks = blocks.transpose(2, 4, 0, 1, 3, 5)
    return blocks.reshape(width // BS * (length // BS), frames, parts * BS * BS)


def from_blocks(blocks, width, length):
    frames = blocks.shape[1]
    field = blocks.reshape(width // BS, length // BS, frames, 2, BS, BS)
    field = field.transpose(2, 3, 0, 4, 1, 5)
    return field.reshape(frames, 2, width, length)


def whole_body(start_image, sensitivity, kspace, sampled, offsets):
    width, length = (start_image.shape[2], start_image.shape[3])
    cosine_table, sine_table = dft_tables(length)
    estimate = start_image

    def per_frame(frame_items):
        field, data, lines = frame_items
        return frame_terms(field, sensitivity, data, lines, cosine_table, sine_table)

    for iteration in range(ITERS):
        gradient, numerator, denominator = lax.map(per_frame, (estimate, kspace, sampled))
        offset_pair = offsets[iteration]
        totals = lax.psum((jnp.sum(numerator), jnp.sum(denominator)), "tm")
        step_length = totals[0] / (totals[1] + epsilon)
        moved = estimate - step_length * gradient
        rolled = jnp.roll(moved, (offset_pair[0], offset_pair[1]), axis=(2, 3))
        casorati = lax.all_to_all(to_blocks(rolled), "tm", split_axis=0, concat_axis=1, tiled=True)
        shrunk = shrink(casorati)
        returned = lax.all_to_all(shrunk, "tm", split_axis=1, concat_axis=0, tiled=True)
        placed = from_blocks(returned, width, length)
        estimate = jnp.roll(placed, (-offset_pair[0], -offset_pair[1]), axis=(2, 3))
    return estimate


def iota(shape, dim):
    return lax.broadcasted_iota(jnp.int32, shape, dim)


def in_block(column, shift, block, length):
    moved = column + shift
    moved = jnp.where(moved >= length, moved - length, moved)
    return (moved >= block * BS) & (moved < block * BS + BS)


def offset_row(offsets_ref, iteration, axis, lanes):
    at = 2 * iteration + axis
    return jnp.concatenate([offsets_ref[at : at + 1, :]] * (lanes // LANES), axis=1)


def upper_rows(offsets_ref, length):
    edge = offset_row(offsets_ref, 0, 0, length) - offset_row(offsets_ref, 1, 0, length)
    return jnp.where(edge < 0, edge + BS, edge)


def wide_table(length):
    indices = np.arange(length, dtype=np.int32)
    phases = indices[:, None] * indices[None, :] % length
    angles = phases.astype(np.float32) * np.float32(2.0 * math.pi / length)
    norm_scale = np.float32(1.0 / math.sqrt(length))
    cosine = (np.cos(angles) * norm_scale).astype(ml_dtypes.bfloat16)
    sine = (np.sin(angles) * norm_scale).astype(ml_dtypes.bfloat16)
    return np.block([[cosine, -sine], [sine, cosine]])


def pair_list(frames):
    return [(f, g) for f in range(frames) for g in range(f, frames)]


def pair_select(frames, lanes):
    table = np.zeros((frames * frames, lanes), np.float32)
    for place, (f, g) in enumerate(pair_list(frames)):
        table[f * frames + g, place] = 1.0
        table[g * frames + f, place] = 1.0
    return table


def pieces(x):
    first = x.astype(jnp.bfloat16)
    rest = x - first.astype(jnp.float32)
    second = rest.astype(jnp.bfloat16)
    third = (rest - second.astype(jnp.float32)).astype(jnp.bfloat16)
    return jnp.concatenate([first, second, third], axis=0)


def pick(x, ones):
    rows = x.shape[0]
    out = mxu(pieces(x), ones.astype(jnp.float32).astype(jnp.bfloat16))
    return out[:rows] + out[rows : 2 * rows] + out[2 * rows :]


def pick_rows(ones, x):
    rows = x.shape[0]
    out = lax.dot_general(
        ones.astype(jnp.float32).astype(jnp.bfloat16), pieces(x), (((1,), (1,)), ((), ())), preferred_element_type=jnp.float32
    )
    return out[:, :rows] + out[:, rows : 2 * rows] + out[:, 2 * rows :]


def mxu(a, b):
    return jnp.dot(a, b, preferred_element_type=jnp.float32)


def fold(x):
    rows, length = x.shape
    return jnp.sum(x.reshape(rows // 8, 8, length), axis=0)


def frame_kernel(
    offsets_hbm, start_hbm, sens_hbm, data_hbm, lines_hbm, table_hbm, out_ref, strip_ref, copied_ref,
    offsets_ref, start_ref, sens_ref, data_ref, lines_ref, table_ref, grad, left, right, sems, chunk_sems,
):
    chunks, coils, _, rows, length = sens_ref.shape
    start_copy, lines_copy, table_copy, offsets_copy, again_copy = (
        pltpu.make_async_copy(source, target, sems.at[k])
        for k, (source, target) in enumerate(
            (
                (start_hbm, start_ref),
                (lines_hbm, lines_ref),
                (table_hbm, table_ref.at[: 2 * length]),
                (offsets_hbm, offsets_ref),
                (table_hbm, table_ref.at[2 * length :]),
            )
        )
    )
    sens_copy = [
        pltpu.make_async_copy(sens_hbm.at[:, :, pl.ds(i * rows, rows), :], sens_ref.at[i], chunk_sems.at[0, i])
        for i in range(chunks)
    ]
    data_copy = [
        pltpu.make_async_copy(data_hbm.at[0, :, :, pl.ds(i * rows, rows), :], data_ref.at[i], chunk_sems.at[1, i])
        for i in range(chunks)
    ]
    offsets_copy.start()
    start_copy.start()
    lines_copy.start()
    sens_copy[0].start()
    table_copy.start()
    for copy in sens_copy[1:] + data_copy + [again_copy]:
        copy.start()
    strips = out_ref.shape[0]
    halves = length // LANES
    strip = 2 * BS

    def coil_image(i, a, b):
        for c in range(coils):
            sr = sens_ref[i, c, 0].astype(jnp.float32)
            si = sens_ref[i, c, 1].astype(jnp.float32)
            at = slice(c * rows, (c + 1) * rows)
            left[i, at, :length] = (sr * a - si * b).astype(jnp.bfloat16)
            left[i, at, length:] = (sr * b + si * a).astype(jnp.bfloat16)

    def post(kind, image):
        shift = offsets_ref[0, 0]
        for part in range(2):
            rolled = pltpu.roll(image[part], shift, 0)
            for half in range(halves):
                base = (kind * halves + half) * strip + part * BS
                out_ref[:, base : base + BS, :] = rolled[:, half * LANES : (half + 1) * LANES].reshape(strips, BS, LANES)

    offsets_copy.wait()
    start_copy.wait()
    lines_copy.wait()
    copied = jnp.zeros(copied_ref.shape, jnp.int32)
    for k in range(ITERS):
        for axis in range(2):
            copied = jnp.where(iota(copied.shape, 0) == 2 * k + axis, offsets_ref[k, axis], copied)
    copied_ref[...] = copied
    weight = lines_ref[0].astype(jnp.float32)
    post(0, start_ref.at[0])
    for target in range(strips):
        for half in range(halves):
            base = 2 * halves * strip + half * coils
            out_ref[target, base : base + coils, :] = weight[:, half * LANES : (half + 1) * LANES]
    spec = []
    for i in range(chunks):
        sens_copy[i].wait()
        if i == 0:
            table_copy.wait()
        coil_image(i, start_ref[0, 0, i * rows : (i + 1) * rows], start_ref[0, 1, i * rows : (i + 1) * rows])
        spec.append(mxu(left[i], table_ref[: 2 * length]))
    me = lax.axis_index("tm")
    each = rows // BS
    pair = []
    for place in (lax.rem(me + strips - 1, strips), me):
        pair.append((place // each, pl.ds(pl.multiple_of(lax.rem(place, each) * BS, BS), BS)))
    shift = offsets_ref[0, 0]
    for c in range(coils):
        for part in range(2):
            two = jnp.concatenate([sens_ref[i, c, part, at, :] for i, at in pair], axis=0).astype(jnp.float32)
            strip_ref[c, part] = pltpu.roll(two, shift, 0)[BS:]
    home = []
    for i in range(chunks):
        data_copy[i].wait()
        if i == 0:
            again_copy.wait()
        for c in range(coils):
            at = slice(c * rows, (c + 1) * rows)
            w = weight[c : c + 1]
            parts = (
                w * (spec[i][at, :length] - data_ref[i, c, 0].astype(jnp.float32)),
                w * (data_ref[i, c, 1].astype(jnp.float32) - spec[i][at, length:]),
            )
            for k, value in enumerate(parts):
                main = value.astype(jnp.bfloat16)
                right[i, at, k * length : (k + 1) * length] = main
                right[i, at, (k + 2) * length : (k + 3) * length] = (value - main.astype(jnp.float32)).astype(jnp.bfloat16)
        home.append(mxu(right[i], table_ref[...]))
    num = jnp.zeros((8, length), jnp.float32)
    probe = []
    for i in range(chunks):
        for first in range(0, rows, 2 * BS):
            some = slice(first, first + 2 * BS)
            gr = jnp.zeros((2 * BS, length), jnp.float32)
            gi = jnp.zeros((2 * BS, length), jnp.float32)
            for c in range(coils):
                sr = sens_ref[i, c, 0, some].astype(jnp.float32)
                si = sens_ref[i, c, 1, some].astype(jnp.float32)
                at = slice(c * rows + first, c * rows + first + 2 * BS)
                br, bi = home[i][at, :length], home[i][at, length:]
                gr = gr + (sr * br - si * bi)
                gi = gi - (sr * bi + si * br)
            grad[0, i * rows + first : i * rows + first + 2 * BS, :] = gr
            grad[1, i * rows + first : i * rows + first + 2 * BS, :] = gi
            num = num + fold(gr * gr + gi * gi)
        coil_image(i, grad[0, i * rows : (i + 1) * rows], grad[1, i * rows : (i + 1) * rows])
        probe.append(mxu(left[i], table_ref[: 2 * length]))
    post(1, grad)
    den = jnp.zeros((8, length), jnp.float32)
    for i in range(chunks):
        for c in range(coils):
            at = slice(c * rows, (c + 1) * rows)
            pr, pi = probe[i][at, :length], probe[i][at, length:]
            den = den + weight[c : c + 1] * fold(pr * pr + pi * pi)
    numer = jnp.sum(jnp.sum(num, axis=0, keepdims=True), axis=1, keepdims=True)
    denom = jnp.sum(jnp.sum(den, axis=0, keepdims=True), axis=1, keepdims=True)
    sums = jnp.where(iota((8, LANES), 0) == 0, numer, denom)
    base = 2 * halves * strip + halves * coils
    for target in range(strips):
        out_ref[target, base : base + 8, :] = sums


def newton_inverse(system, held, frames):
    place = iota(system[0].shape, 0)
    unit = [(place == f).astype(jnp.float32) for f in range(frames)]
    bound = jnp.max(sum(jnp.abs(tile) for tile in system), axis=0, keepdims=True)
    scale = 1.0 / bound

    def times(ref, tiles):
        out = []
        for f in range(frames):
            terms = [ref[f * frames + g : f * frames + g + 1, :] * tiles[g] for g in range(frames)]
            while len(terms) > 1:
                terms = [a + b for a, b in zip(terms[::2], terms[1::2])]
            out.append(terms[0])
        return out

    power = [unit[f] - scale * system[f] for f in range(frames)]
    total = [unit[f] + power[f] for f in range(frames)]
    for newton in range(1, NEWTON):
        for f in range(frames):
            held[newton, f * frames : (f + 1) * frames, :] = power[f]
        power = times(held.at[newton], power)
        for f in range(frames):
            held[0, f * frames : (f + 1) * frames, :] = power[f]
        added = times(held.at[0], total)
        total = [total[f] + added[f] for f in range(frames)]
    return [scale * tile for tile in total]


def shrink_factors(gram, held, frames):
    lanes = gram.shape[1]
    place = iota((frames, lanes), 0)
    tiles = [gram[f * frames : (f + 1) * frames, :] for f in range(frames)]
    trace = sum(gram[f * frames + f : f * frames + f + 1, :] for f in range(frames))
    level = shrink_ratio * trace / frames + epsilon
    system = [tiles[f] + jnp.where(place == f, level, 0.0) for f in range(frames)]
    approx = newton_inverse(system, held, frames)
    return jnp.concatenate([level * tile for tile in approx], axis=0)


def middle_kernel(
    offsets_ref, mail_ref, sens_ref, table_ref,
    out_ref, own_ref, est_ref, grad_ref,
    terms, held, spread, left, right,
):
    frames = mail_ref.shape[0]
    coils, _, _, length = sens_ref.shape
    pairs = pair_list(frames)
    strip = 2 * BS
    halves = length // LANES

    def mail(f, kind, first, rows):
        return jnp.concatenate(
            [
                mail_ref[f, (kind * halves + half) * strip + first : (kind * halves + half) * strip + first + rows, :]
                for half in range(halves)
            ],
            axis=1,
        )

    def mask(f):
        base = 2 * halves * strip
        return jnp.concatenate(
            [mail_ref[f, base + half * coils : base + (half + 1) * coils, :] for half in range(halves)], axis=1
        )

    place = 2 * halves * strip + halves * coils
    totals = sum(mail_ref[f, place : place + 8, :] for f in range(frames))
    step = totals[:1] / (totals[1:2] + epsilon)
    step = jnp.concatenate([step] * halves, axis=1)
    for f in range(frames):
        est_ref[f] = mail(f, 0, 0, strip) - step * mail(f, 1, 0, strip)
    for f, g in pairs:
        tile = fold(est_ref[f] * est_ref[g])
        for place in {f * frames + g, g * frames + f}:
            for half in range(length // LANES):
                terms[half, place * 8 : place * 8 + 8, :] = tile[:, half * LANES : (half + 1) * LANES]
    count = frames * frames
    sums = jnp.concatenate(
        [sum(terms[half, pl.ds(s, count, stride=8), :] for s in range(8)) for half in range(length // LANES)], axis=1
    )
    tall = in_block(iota((length, LANES), 0), offset_row(offsets_ref, 0, 1, LANES), iota((length, LANES), 1), length)
    broad = in_block(iota((LANES, length), 1), offset_row(offsets_ref, 0, 1, length), iota((LANES, length), 0), length)
    factors = shrink_factors(pick(sums, tall), held, frames)
    spread[...] = pick(factors, broad)
    moved = [est_ref[f] for f in range(frames)]
    for f in range(frames):
        total = spread[f * frames : f * frames + 1, :] * moved[0]
        for g in range(1, frames):
            total = total + spread[f * frames + g : f * frames + g + 1, :] * moved[g]
        grad_ref[f] = moved[f] - total
    for f in range(frames):
        est_ref[f] = grad_ref[f]

    num = jnp.zeros((8, length), jnp.float32)
    den = jnp.zeros((8, length), jnp.float32)
    group = left.shape[1] // (coils * BS)

    def coil_image(index, values):
        for k, (a, b) in enumerate(values):
            for c in range(coils):
                sr, si = sens_ref[c, 0], sens_ref[c, 1]
                at = slice((k * coils + c) * BS, (k * coils + c + 1) * BS)
                left[index, at, :length] = (sr * a - si * b).astype(jnp.bfloat16)
                left[index, at, length:] = (sr * b + si * a).astype(jnp.bfloat16)

    edge = upper_rows(offsets_ref, length)
    low = [(iota((8, length), 0) + 8 * t >= edge) for t in range(BS // 8)]
    block = len(pairs)
    span = out_ref.shape[2]

    def rows_of(product):
        return [
            sum(product[p * BS + 8 * t : p * BS + 8 * t + 8] for p in range(2)) for t in range(BS // 8)
        ]

    def put(part, place, tile):
        for half in range(length // LANES):
            terms[half, (part * span + place) * 8 : (part * span + place) * 8 + 8, :] = tile[
                :, half * LANES : (half + 1) * LANES
            ]

    def put_kind(kind, product_of):
        for place, pair in enumerate(pairs):
            rows = rows_of(product_of(*pair))
            put(0, kind * block + place, sum(jnp.where(low[t], rows[t], 0.0) for t in range(BS // 8)))
            put(1, kind * block + place, sum(jnp.where(low[t], 0.0, rows[t]) for t in range(BS // 8)))

    groups = [range(at, at + group) for at in range(0, frames, group)]
    weights = [mask(f) for f in range(frames)]
    spec = []
    for index, members in enumerate(groups):
        coil_image(
            index,
            [(est_ref[f, :BS, :] - mail(f, 0, 0, BS), est_ref[f, BS:strip, :] - mail(f, 0, BS, BS)) for f in members],
        )
        spec.append(mxu(left[index], table_ref[...]))
    for part in range(2):
        for place in range(3 * block, span):
            put(part, place, jnp.zeros((8, length), jnp.float32))
    put_kind(0, lambda f, g: est_ref[f] * est_ref[g])
    home = []
    for index, members in enumerate(groups):
        for k, f in enumerate(members):
            for c in range(coils):
                at = slice((k * coils + c) * BS, (k * coils + c + 1) * BS)
                w = weights[f][c : c + 1]
                right[index, at, :length] = (w * spec[index][at, :length]).astype(jnp.bfloat16)
                right[index, at, length:] = (-w * spec[index][at, length:]).astype(jnp.bfloat16)
        home.append(mxu(right[index], table_ref[...]))
    probe = []
    for index, members in enumerate(groups):
        values = []
        for k, f in enumerate(members):
            gr = mail(f, 1, 0, BS)
            gi = mail(f, 1, BS, BS)
            for c in range(coils):
                at = slice((k * coils + c) * BS, (k * coils + c + 1) * BS)
                sr, si = sens_ref[c, 0], sens_ref[c, 1]
                br, bi = home[index][at, :length], home[index][at, length:]
                gr = gr + (sr * br - si * bi)
                gi = gi - (sr * bi + si * br)
            grad_ref[f, :BS, :] = gr
            grad_ref[f, BS:strip, :] = gi
            num = num + fold(gr * gr + gi * gi)
            values.append((gr, gi))
        coil_image(index, values)
        probe.append(mxu(left[index], table_ref[...]))
    put_kind(1, lambda f, g: est_ref[f] * grad_ref[g] + est_ref[g] * grad_ref[f])
    put_kind(2, lambda f, g: grad_ref[f] * grad_ref[g])
    for index, members in enumerate(groups):
        for k, f in enumerate(members):
            for c in range(coils):
                at = slice((k * coils + c) * BS, (k * coils + c + 1) * BS)
                pr, pi = probe[index][at, :length], probe[index][at, length:]
                den = den + weights[f][c : c + 1] * fold(pr * pr + pi * pi)
    numer = jnp.sum(jnp.sum(num, axis=0, keepdims=True), axis=1, keepdims=True)
    denom = jnp.sum(jnp.sum(den, axis=0, keepdims=True), axis=1, keepdims=True)

    blocks = length // BS
    shift = offset_row(offsets_ref, 1, 1, length)
    member = in_block(iota((blocks, length), 1), shift, iota((blocks, length), 0), length)
    lane = iota((blocks, span), 1)
    packs = []
    for part in range(2):
        sums = jnp.concatenate(
            [
                sum(terms[half, pl.ds(part * span * 8 + s, span, stride=8), :] for s in range(8))
                for half in range(length // LANES)
            ],
            axis=1,
        )
        pack = pick_rows(member, sums)
        pack = jnp.where(lane == 3 * block, numer, jnp.where(lane == 3 * block + 1, denom, pack))
        own_ref[part * blocks : (part + 1) * blocks, :] = pack
        packs.append(pack)
    me = lax.axis_index("tm")
    strips = out_ref.shape[0]
    before = lax.rem(me + strips - 1, strips)
    for target in range(strips):
        out_ref[target] = jnp.where(before == target, packs[1], packs[0])


def last_kernel(offsets_ref, own_ref, heard_ref, est_ref, grad_ref, select_ref, out_ref, held, spread):
    frames, strip, length = est_ref.shape
    strips, blocks, span = heard_ref.shape
    block = len(pair_list(frames))
    me = lax.axis_index("tm")
    numer = jnp.zeros((1, 1), jnp.float32)
    denom = jnp.zeros((1, 1), jnp.float32)
    for k in range(strips):
        numer = numer + heard_ref[k, 0:1, 3 * block : 3 * block + 1]
        denom = denom + heard_ref[k, 0:1, 3 * block + 1 : 3 * block + 2]
    step = numer / (denom + epsilon)
    after = lax.rem(me + 1, strips)
    before = lax.rem(me + strips - 1, strips)
    total = own_ref[...] + jnp.concatenate([heard_ref[after], heard_ref[before]], axis=0)
    cross = pltpu.roll(total, span - block, 1)
    square = pltpu.roll(total, span - 2 * block, 1)
    gram = total - step * cross + step * step * square
    gram = jnp.concatenate([gram, jnp.zeros((LANES - 2 * blocks, span), jnp.float32)], axis=0)
    gram = jnp.where(iota(gram.shape, 1) < block, gram, 0.0)
    gram = pick_rows(select_ref[...], gram)
    factors = shrink_factors(gram, held, frames)
    shift = offset_row(offsets_ref, 1, 1, length)
    column = iota((LANES, length), 1)
    row = iota((LANES, length), 0)
    broad = [in_block(column, shift, row - part * blocks, length).astype(jnp.float32) for part in range(2)]
    spread[...] = pick(factors, jnp.concatenate(broad, axis=1))
    edge = upper_rows(offsets_ref, length)
    moved = [est_ref[f] - step * grad_ref[f] for f in range(frames)]
    for t in range(BS // 8):
        low = iota((8, length), 0) + 8 * t >= edge
        for f in range(frames):
            total = [jnp.zeros((8, length), jnp.float32)] * 2
            for g in range(frames):
                at = f * frames + g
                factor = jnp.where(low, spread[at : at + 1, :length], spread[at : at + 1, length:])
                total = [total[p] + factor * moved[g][p * BS + 8 * t : p * BS + 8 * t + 8] for p in range(2)]
            for p in range(2):
                rows = slice(p * BS + 8 * t, p * BS + 8 * t + 8)
                out_ref[f, rows, :] = moved[f][rows] - total[p]


def place_kernel(offsets_ref, strips_ref, out_hbm, whole, sems):
    strips, _, length = strips_ref.shape
    width = strips * BS
    shift = offset_row(offsets_ref, 0, 0, length)
    copies = []
    for part in range(2):
        image = strips_ref[:, part * BS : (part + 1) * BS, :].reshape(width, length)
        step = 1
        while step < BS:
            image = jnp.where((shift & step) != 0, pltpu.roll(image, width - step, 0), image)
            step *= 2
        whole[part] = image
        copies.append(pltpu.make_async_copy(whole.at[part], out_hbm.at[0, part], sems.at[part]))
        copies[-1].start()
    for copy in copies:
        copy.wait()


def vmem():
    return pl.BlockSpec(memory_space=pltpu.VMEM)


def hbm():
    return pl.BlockSpec(memory_space=pltpu.HBM)


def f32(*shape):
    return jax.ShapeDtypeStruct(shape, jnp.float32)


def exchange(blocks):
    return lax.all_to_all(blocks, "tm", split_axis=0, concat_axis=0, tiled=True)


def params(mebibytes=16):
    return pltpu.CompilerParams(vmem_limit_bytes=mebibytes * 1024 * 1024)


def frame_call(start_image, sensitivity, kspace, sampled, offsets, table):
    _, _, width, length = start_image.shape
    coils = sensitivity.shape[0]
    rows = width
    chunks = width // rows
    return pl.pallas_call(
        frame_kernel,
        out_shape=(
            pltpu.VMEM((width // BS, length // LANES * (4 * BS + coils) + 8, LANES), jnp.float32),
            pltpu.VMEM((coils, 2, BS, length), jnp.float32),
            pltpu.VMEM((SUBLANES, LANES), jnp.int32),
        ),
        in_specs=[hbm()] * 6,
        out_specs=(vmem(),) * 3,
        scratch_shapes=[
            pltpu.SMEM(offsets.shape, jnp.int32),
            pltpu.VMEM(start_image.shape, jnp.float32),
            pltpu.VMEM((chunks, coils, 2, rows, length), jnp.bfloat16),
            pltpu.VMEM((chunks, coils, 2, rows, length), jnp.bfloat16),
            pltpu.VMEM(sampled.shape, jnp.int32),
            pltpu.VMEM((4 * length, 2 * length), jnp.bfloat16),
            pltpu.VMEM((2, width, length), jnp.float32),
            pltpu.VMEM((chunks, coils * rows, 2 * length), jnp.bfloat16),
            pltpu.VMEM((chunks, coils * rows, 4 * length), jnp.bfloat16),
            pltpu.SemaphoreType.DMA((5,)),
            pltpu.SemaphoreType.DMA((2, chunks)),
        ],
        compiler_params=params(60),
        name="frame_gradient",
    )(offsets, start_image, sensitivity, kspace, sampled, table)


def middle_call(mail, sens, offsets, table):
    frames = mail.shape[0]
    coils, _, _, length = sens.shape
    count = frames * frames
    blocks = length // BS
    group = frames
    return pl.pallas_call(
        middle_kernel,
        out_shape=(
            f32(frames, blocks, LANES),
            f32(2 * blocks, LANES),
            f32(frames, 2 * BS, length),
            f32(frames, 2 * BS, length),
        ),
        in_specs=[vmem()] * 4,
        out_specs=(vmem(),) * 4,
        scratch_shapes=[
            pltpu.VMEM((length // LANES, 2 * LANES * 8, LANES), jnp.float32),
            pltpu.VMEM((NEWTON, count, LANES), jnp.float32),
            pltpu.VMEM((count, length), jnp.float32),
            pltpu.VMEM((frames // group, group * coils * BS, 2 * length), jnp.bfloat16),
            pltpu.VMEM((frames // group, group * coils * BS, 2 * length), jnp.bfloat16),
        ],
        compiler_params=params(),
        name="strip_shrink_gradient",
    )(offsets, mail, sens, table)


def last_call(own, heard, estimate, gradient, offsets):
    frames, strip, length = estimate.shape
    count = frames * frames
    return pl.pallas_call(
        last_kernel,
        out_shape=f32(frames, strip, length),
        in_specs=[vmem()] * 6,
        out_specs=vmem(),
        scratch_shapes=[
            pltpu.VMEM((NEWTON, count, LANES), jnp.float32),
            pltpu.VMEM((count, 2 * length), jnp.float32),
        ],
        compiler_params=params(),
        name="strip_shrink",
    )(offsets, own, heard, estimate, gradient, jnp.asarray(pair_select(frames, LANES)))


def place_call(strips, offsets):
    count, strip, length = strips.shape
    width = count * strip // 2
    return pl.pallas_call(
        place_kernel,
        out_shape=f32(1, 2, width, length),
        in_specs=[vmem()] * 2,
        out_specs=hbm(),
        scratch_shapes=[pltpu.VMEM((2, width, length), jnp.float32), pltpu.SemaphoreType.DMA((2,))],
        compiler_params=params(),
        name="frame_place",
    )(offsets, strips)


def strips_body(start_image, sensitivity, kspace, sampled, offsets):
    table = jnp.asarray(wide_table(start_image.shape[3]))
    mail, sens, offsets = frame_call(start_image, sensitivity, kspace, sampled, offsets, table)
    mail = exchange(mail)
    sent, own, estimate, gradient = middle_call(mail, sens, offsets, table)
    returned = exchange(last_call(own, exchange(sent), estimate, gradient, offsets))
    return place_call(returned, offsets)


def fits_strips(start_image, sensitivity, kspace, sampled, offsets):
    strips = lax.axis_size("tm")
    frames, _, width, length = start_image.shape
    coils = sensitivity.shape[0]
    kinds = 3 * len(pair_list(strips))
    return (
        frames == 1
        and width == strips * BS
        and strips == SUBLANES
        and coils % SUBLANES == 0
        and ITERS == 2
        and length % LANES == 0
        and 2 * (length // BS) <= LANES
        and kinds + 2 <= LANES
    )


def body(*args):
    return (strips_body if fits_strips(*args) else whole_body)(*args)


def solution(mesh):
    placed = (
        P(("cuts", "tm"), None, None, None),
        P("cuts", None, None, None),
        P(("cuts", "tm"), None, None, None, None),
        P(("cuts", "tm"), None, None),
        P("cuts", None),
    )
    return jax.shard_map(
        body,
        mesh=mesh,
        in_specs=placed,
        out_specs=P(("cuts", "tm"), None, None, None),
        check_vma=False,
    )
```

```python
import math

import jax
import jax.numpy as jnp
import ml_dtypes
import numpy as np
from jax import lax
from jax.experimental import pallas as pl
from jax.experimental.pallas import tpu as pltpu
from jax.sharding import PartitionSpec as P

BS = 16
ITERS = 2
NEWTON = 4
LANES = 128
SUBLANES = 8


shrink_ratio = 0.5
epsilon = 1e-06


def dft_tables(length):
    indices = jnp.arange(length, dtype=jnp.int32)
    phases = indices[:, None] * indices[None, :] % length
    angles = phases.astype(jnp.float32) * (2.0 * math.pi / length)
    norm_scale = 1.0 / math.sqrt(length)
    return (
        (jnp.cos(angles) * norm_scale).astype(jnp.bfloat16),
        (jnp.sin(angles) * norm_scale).astype(jnp.bfloat16),
    )


def forward(real_part, imag_part, cosine_table, sine_table):
    out_real = jnp.dot(real_part, cosine_table, preferred_element_type=jnp.float32) + jnp.dot(
        imag_part, sine_table, preferred_element_type=jnp.float32
    )
    out_imag = jnp.dot(imag_part, cosine_table, preferred_element_type=jnp.float32) - jnp.dot(
        real_part, sine_table, preferred_element_type=jnp.float32
    )
    return (out_real, out_imag)


def inverse(real_part, imag_part, cosine_table, sine_table):
    out_real = jnp.dot(real_part, cosine_table, preferred_element_type=jnp.float32) - jnp.dot(
        imag_part, sine_table, preferred_element_type=jnp.float32
    )
    out_imag = jnp.dot(imag_part, cosine_table, preferred_element_type=jnp.float32) + jnp.dot(
        real_part, sine_table, preferred_element_type=jnp.float32
    )
    return (out_real, out_imag)


def coil_spectra(field, sens_real, sens_imag, cosine_table, sine_table):
    coils, width, length = sens_real.shape
    coil_real = (
        (sens_real * field[0] - sens_imag * field[1])
        .astype(jnp.bfloat16)
        .reshape(coils * width, length)
    )
    coil_imag = (
        (sens_real * field[1] + sens_imag * field[0])
        .astype(jnp.bfloat16)
        .reshape(coils * width, length)
    )
    spec_real, spec_imag = forward(coil_real, coil_imag, cosine_table, sine_table)
    return (spec_real.reshape(coils, width, length), spec_imag.reshape(coils, width, length))


def frame_terms(field, sensitivity, data, lines, cosine_table, sine_table):
    sens_real = sensitivity[:, 0].astype(jnp.float32)
    sens_imag = sensitivity[:, 1].astype(jnp.float32)
    coils, width, length = sens_real.shape
    weight = lines.astype(jnp.float32)[:, None, :]
    spec_real, spec_imag = coil_spectra(field, sens_real, sens_imag, cosine_table, sine_table)
    misfit_real = (weight * (spec_real - data[:, 0].astype(jnp.float32))).astype(jnp.bfloat16)
    misfit_imag = (weight * (spec_imag - data[:, 1].astype(jnp.float32))).astype(jnp.bfloat16)
    back_real, back_imag = inverse(
        misfit_real.reshape(coils * width, length),
        misfit_imag.reshape(coils * width, length),
        cosine_table,
        sine_table,
    )
    back_real = back_real.reshape(coils, width, length)
    back_imag = back_imag.reshape(coils, width, length)
    grad_real = jnp.sum(sens_real * back_real + sens_imag * back_imag, axis=0)
    grad_imag = jnp.sum(sens_real * back_imag - sens_imag * back_real, axis=0)
    gradient = jnp.stack([grad_real, grad_imag])
    numerator = jnp.sum(gradient * gradient)
    probe_real, probe_imag = coil_spectra(gradient, sens_real, sens_imag, cosine_table, sine_table)
    denominator = jnp.sum(weight * (probe_real * probe_real + probe_imag * probe_imag))
    return (gradient, numerator, denominator)


def shrink(casorati):
    highest = lax.Precision.HIGHEST
    gram = jnp.einsum("bfv,bgv->bfg", casorati, casorati, precision=highest)
    frames = gram.shape[1]
    identity = jnp.eye(frames, dtype=jnp.float32)
    shrink_level = shrink_ratio * jnp.trace(gram, axis1=1, axis2=2) / frames + epsilon
    system = gram + shrink_level[:, None, None] * identity
    row_bound = jnp.max(jnp.sum(jnp.abs(system), axis=2), axis=1)
    approx = identity[None] / row_bound[:, None, None]
    for newton in range(NEWTON):
        product = jnp.einsum("bfg,bgh->bfh", system, approx, precision=highest)
        approx = jnp.einsum("bfg,bgh->bfh", approx, 2.0 * identity - product, precision=highest)
    return casorati - shrink_level[:, None, None] * jnp.einsum(
        "bfg,bgv->bfv", approx, casorati, precision=highest
    )


def to_blocks(field):
    frames, parts, width, length = field.shape
    blocks = field.reshape(frames, parts, width // BS, BS, length // BS, BS)
    blocks = blocks.transpose(2, 4, 0, 1, 3, 5)
    return blocks.reshape(width // BS * (length // BS), frames, parts * BS * BS)


def from_blocks(blocks, width, length):
    frames = blocks.shape[1]
    field = blocks.reshape(width // BS, length // BS, frames, 2, BS, BS)
    field = field.transpose(2, 3, 0, 4, 1, 5)
    return field.reshape(frames, 2, width, length)


def whole_body(start_image, sensitivity, kspace, sampled, offsets):
    width, length = (start_image.shape[2], start_image.shape[3])
    cosine_table, sine_table = dft_tables(length)
    estimate = start_image

    def per_frame(frame_items):
        field, data, lines = frame_items
        return frame_terms(field, sensitivity, data, lines, cosine_table, sine_table)

    for iteration in range(ITERS):
        gradient, numerator, denominator = lax.map(per_frame, (estimate, kspace, sampled))
        offset_pair = offsets[iteration]
        totals = lax.psum((jnp.sum(numerator), jnp.sum(denominator)), "tm")
        step_length = totals[0] / (totals[1] + epsilon)
        moved = estimate - step_length * gradient
        rolled = jnp.roll(moved, (offset_pair[0], offset_pair[1]), axis=(2, 3))
        casorati = lax.all_to_all(to_blocks(rolled), "tm", split_axis=0, concat_axis=1, tiled=True)
        shrunk = shrink(casorati)
        returned = lax.all_to_all(shrunk, "tm", split_axis=1, concat_axis=0, tiled=True)
        placed = from_blocks(returned, width, length)
        estimate = jnp.roll(placed, (-offset_pair[0], -offset_pair[1]), axis=(2, 3))
    return estimate


def iota(shape, dim):
    return lax.broadcasted_iota(jnp.int32, shape, dim)


def in_block(column, shift, block, length):
    moved = column + shift
    moved = jnp.where(moved >= length, moved - length, moved)
    return (moved >= block * BS) & (moved < block * BS + BS)


def offset_row(offsets_ref, iteration, axis, lanes):
    at = 2 * iteration + axis
    return jnp.concatenate([offsets_ref[at : at + 1, :]] * (lanes // LANES), axis=1)


def upper_rows(offsets_ref, length):
    edge = offset_row(offsets_ref, 0, 0, length) - offset_row(offsets_ref, 1, 0, length)
    return jnp.where(edge < 0, edge + BS, edge)


def wide_table(length):
    indices = np.arange(length, dtype=np.int32)
    phases = indices[:, None] * indices[None, :] % length
    angles = phases.astype(np.float32) * np.float32(2.0 * math.pi / length)
    norm_scale = np.float32(1.0 / math.sqrt(length))
    cosine = (np.cos(angles) * norm_scale).astype(ml_dtypes.bfloat16)
    sine = (np.sin(angles) * norm_scale).astype(ml_dtypes.bfloat16)
    return np.block([[cosine, -sine], [sine, cosine]])


def pair_list(frames):
    return [(f, g) for f in range(frames) for g in range(f, frames)]


def pair_select(frames, lanes):
    table = np.zeros((frames * frames, lanes), np.float32)
    for place, (f, g) in enumerate(pair_list(frames)):
        table[f * frames + g, place] = 1.0
        table[g * frames + f, place] = 1.0
    return table


def pieces(x):
    first = x.astype(jnp.bfloat16)
    rest = x - first.astype(jnp.float32)
    second = rest.astype(jnp.bfloat16)
    third = (rest - second.astype(jnp.float32)).astype(jnp.bfloat16)
    return jnp.concatenate([first, second, third], axis=0)


def pick(x, ones):
    rows = x.shape[0]
    out = mxu(pieces(x), ones.astype(jnp.float32).astype(jnp.bfloat16))
    return out[:rows] + out[rows : 2 * rows] + out[2 * rows :]


def pick_rows(ones, x):
    rows = x.shape[0]
    out = lax.dot_general(
        ones.astype(jnp.float32).astype(jnp.bfloat16), pieces(x), (((1,), (1,)), ((), ())), preferred_element_type=jnp.float32
    )
    return out[:, :rows] + out[:, rows : 2 * rows] + out[:, 2 * rows :]


def mxu(a, b):
    return jnp.dot(a, b, preferred_element_type=jnp.float32)


def fold(x):
    rows, length = x.shape
    return jnp.sum(x.reshape(rows // 8, 8, length), axis=0)


def frame_kernel(
    offsets_hbm, start_hbm, sens_hbm, data_hbm, lines_hbm, table_hbm, out_ref, strip_ref, copied_ref,
    offsets_ref, start_ref, sens_ref, data_ref, lines_ref, table_ref, grad, left, right, sems, chunk_sems,
):
    chunks, coils, _, rows, length = sens_ref.shape
    start_copy, lines_copy, table_copy, offsets_copy = (
        pltpu.make_async_copy(source, target, sems.at[k])
        for k, (source, target) in enumerate(
            ((start_hbm, start_ref), (lines_hbm, lines_ref), (table_hbm, table_ref), (offsets_hbm, offsets_ref))
        )
    )
    sens_copy = [
        pltpu.make_async_copy(sens_hbm.at[:, :, pl.ds(i * rows, rows), :], sens_ref.at[i], chunk_sems.at[0, i])
        for i in range(chunks)
    ]
    data_copy = [
        pltpu.make_async_copy(data_hbm.at[0, :, :, pl.ds(i * rows, rows), :], data_ref.at[i], chunk_sems.at[1, i])
        for i in range(chunks)
    ]
    offsets_copy.start()
    start_copy.start()
    lines_copy.start()
    sens_copy[0].start()
    table_copy.start()
    for copy in sens_copy[1:] + data_copy:
        copy.start()
    strips = out_ref.shape[0]
    halves = length // LANES
    strip = 2 * BS

    def coil_image(i, a, b):
        for c in range(coils):
            sr = sens_ref[i, c, 0].astype(jnp.float32)
            si = sens_ref[i, c, 1].astype(jnp.float32)
            at = slice(c * rows, (c + 1) * rows)
            left[i, at, :length] = (sr * a - si * b).astype(jnp.bfloat16)
            left[i, at, length:] = (sr * b + si * a).astype(jnp.bfloat16)

    def post(kind, image):
        shift = offsets_ref[0, 0]
        for part in range(2):
            rolled = pltpu.roll(image[part], shift, 0)
            for half in range(halves):
                base = (kind * halves + half) * strip + part * BS
                out_ref[:, base : base + BS, :] = rolled[:, half * LANES : (half + 1) * LANES].reshape(strips, BS, LANES)

    offsets_copy.wait()
    start_copy.wait()
    lines_copy.wait()
    copied = jnp.zeros(copied_ref.shape, jnp.int32)
    for k in range(ITERS):
        for axis in range(2):
            copied = jnp.where(iota(copied.shape, 0) == 2 * k + axis, offsets_ref[k, axis], copied)
    copied_ref[...] = copied
    weight = lines_ref[0].astype(jnp.float32)
    post(0, start_ref.at[0])
    for target in range(strips):
        for half in range(halves):
            base = 2 * halves * strip + half * coils
            out_ref[target, base : base + coils, :] = weight[:, half * LANES : (half + 1) * LANES]
    spec = []
    for i in range(chunks):
        sens_copy[i].wait()
        if i == 0:
            table_copy.wait()
        coil_image(i, start_ref[0, 0, i * rows : (i + 1) * rows], start_ref[0, 1, i * rows : (i + 1) * rows])
        spec.append(mxu(left[i], table_ref[...]))
    home = []
    for i in range(chunks):
        data_copy[i].wait()
        for c in range(coils):
            at = slice(c * rows, (c + 1) * rows)
            w = weight[c : c + 1]
            right[i, at, :length] = (w * (spec[i][at, :length] - data_ref[i, c, 0].astype(jnp.float32))).astype(jnp.bfloat16)
            right[i, at, length:] = (w * (data_ref[i, c, 1].astype(jnp.float32) - spec[i][at, length:])).astype(jnp.bfloat16)
        home.append(mxu(right[i], table_ref[...]))
    num = jnp.zeros((8, length), jnp.float32)
    probe = []
    for i in range(chunks):
        for first in range(0, rows, 2 * BS):
            some = slice(first, first + 2 * BS)
            gr = jnp.zeros((2 * BS, length), jnp.float32)
            gi = jnp.zeros((2 * BS, length), jnp.float32)
            for c in range(coils):
                sr = sens_ref[i, c, 0, some].astype(jnp.float32)
                si = sens_ref[i, c, 1, some].astype(jnp.float32)
                at = slice(c * rows + first, c * rows + first + 2 * BS)
                br, bi = home[i][at, :length], home[i][at, length:]
                gr = gr + (sr * br - si * bi)
                gi = gi - (sr * bi + si * br)
            grad[0, i * rows + first : i * rows + first + 2 * BS, :] = gr
            grad[1, i * rows + first : i * rows + first + 2 * BS, :] = gi
            num = num + fold(gr * gr + gi * gi)
        coil_image(i, grad[0, i * rows : (i + 1) * rows], grad[1, i * rows : (i + 1) * rows])
        probe.append(mxu(left[i], table_ref[...]))
    post(1, grad)
    me = lax.axis_index("tm")
    each = rows // BS
    pair = []
    for place in (lax.rem(me + strips - 1, strips), me):
        pair.append((place // each, pl.ds(pl.multiple_of(lax.rem(place, each) * BS, BS), BS)))
    shift = offsets_ref[0, 0]
    for c in range(coils):
        for part in range(2):
            two = jnp.concatenate([sens_ref[i, c, part, at, :] for i, at in pair], axis=0).astype(jnp.float32)
            strip_ref[c, part] = pltpu.roll(two, shift, 0)[BS:]
    den = jnp.zeros((8, length), jnp.float32)
    for i in range(chunks):
        for c in range(coils):
            at = slice(c * rows, (c + 1) * rows)
            pr, pi = probe[i][at, :length], probe[i][at, length:]
            den = den + weight[c : c + 1] * fold(pr * pr + pi * pi)
    numer = jnp.sum(jnp.sum(num, axis=0, keepdims=True), axis=1, keepdims=True)
    denom = jnp.sum(jnp.sum(den, axis=0, keepdims=True), axis=1, keepdims=True)
    sums = jnp.where(iota((8, LANES), 0) == 0, numer, denom)
    base = 2 * halves * strip + halves * coils
    for target in range(strips):
        out_ref[target, base : base + 8, :] = sums


def newton_inverse(system, held, frames):
    place = iota(system[0].shape, 0)
    unit = [(place == f).astype(jnp.float32) for f in range(frames)]
    bound = jnp.max(sum(jnp.abs(tile) for tile in system), axis=0, keepdims=True)
    scale = 1.0 / bound

    def times(ref, tiles):
        out = []
        for f in range(frames):
            terms = [ref[f * frames + g : f * frames + g + 1, :] * tiles[g] for g in range(frames)]
            while len(terms) > 1:
                terms = [a + b for a, b in zip(terms[::2], terms[1::2])]
            out.append(terms[0])
        return out

    power = [unit[f] - scale * system[f] for f in range(frames)]
    total = [unit[f] + power[f] for f in range(frames)]
    for newton in range(1, NEWTON):
        for f in range(frames):
            held[newton, f * frames : (f + 1) * frames, :] = power[f]
        power = times(held.at[newton], power)
        for f in range(frames):
            held[0, f * frames : (f + 1) * frames, :] = power[f]
        added = times(held.at[0], total)
        total = [total[f] + added[f] for f in range(frames)]
    return [scale * tile for tile in total]


def shrink_factors(gram, held, frames):
    lanes = gram.shape[1]
    place = iota((frames, lanes), 0)
    tiles = [gram[f * frames : (f + 1) * frames, :] for f in range(frames)]
    trace = sum(gram[f * frames + f : f * frames + f + 1, :] for f in range(frames))
    level = shrink_ratio * trace / frames + epsilon
    system = [tiles[f] + jnp.where(place == f, level, 0.0) for f in range(frames)]
    approx = newton_inverse(system, held, frames)
    return jnp.concatenate([level * tile for tile in approx], axis=0)


def middle_kernel(
    offsets_ref, mail_ref, sens_ref, table_ref,
    out_ref, own_ref, est_ref, grad_ref,
    terms, held, spread, left, right,
):
    frames = mail_ref.shape[0]
    coils, _, _, length = sens_ref.shape
    pairs = pair_list(frames)
    strip = 2 * BS
    halves = length // LANES

    def mail(f, kind, first, rows):
        return jnp.concatenate(
            [
                mail_ref[f, (kind * halves + half) * strip + first : (kind * halves + half) * strip + first + rows, :]
                for half in range(halves)
            ],
            axis=1,
        )

    def mask(f):
        base = 2 * halves * strip
        return jnp.concatenate(
            [mail_ref[f, base + half * coils : base + (half + 1) * coils, :] for half in range(halves)], axis=1
        )

    place = 2 * halves * strip + halves * coils
    totals = sum(mail_ref[f, place : place + 8, :] for f in range(frames))
    step = totals[:1] / (totals[1:2] + epsilon)
    step = jnp.concatenate([step] * halves, axis=1)
    for f in range(frames):
        est_ref[f] = mail(f, 0, 0, strip) - step * mail(f, 1, 0, strip)
    for f, g in pairs:
        tile = fold(est_ref[f] * est_ref[g])
        for place in {f * frames + g, g * frames + f}:
            for half in range(length // LANES):
                terms[half, place * 8 : place * 8 + 8, :] = tile[:, half * LANES : (half + 1) * LANES]
    count = frames * frames
    sums = jnp.concatenate(
        [sum(terms[half, pl.ds(s, count, stride=8), :] for s in range(8)) for half in range(length // LANES)], axis=1
    )
    tall = in_block(iota((length, LANES), 0), offset_row(offsets_ref, 0, 1, LANES), iota((length, LANES), 1), length)
    broad = in_block(iota((LANES, length), 1), offset_row(offsets_ref, 0, 1, length), iota((LANES, length), 0), length)
    factors = shrink_factors(pick(sums, tall), held, frames)
    spread[...] = pick(factors, broad)
    moved = [est_ref[f] for f in range(frames)]
    for f in range(frames):
        total = spread[f * frames : f * frames + 1, :] * moved[0]
        for g in range(1, frames):
            total = total + spread[f * frames + g : f * frames + g + 1, :] * moved[g]
        grad_ref[f] = moved[f] - total
    for f in range(frames):
        est_ref[f] = grad_ref[f]

    num = jnp.zeros((8, length), jnp.float32)
    den = jnp.zeros((8, length), jnp.float32)
    group = left.shape[1] // (coils * BS)

    def coil_image(index, values):
        for k, (a, b) in enumerate(values):
            for c in range(coils):
                sr, si = sens_ref[c, 0], sens_ref[c, 1]
                at = slice((k * coils + c) * BS, (k * coils + c + 1) * BS)
                left[index, at, :length] = (sr * a - si * b).astype(jnp.bfloat16)
                left[index, at, length:] = (sr * b + si * a).astype(jnp.bfloat16)

    edge = upper_rows(offsets_ref, length)
    low = [(iota((8, length), 0) + 8 * t >= edge) for t in range(BS // 8)]
    block = len(pairs)
    span = out_ref.shape[2]

    def rows_of(product):
        return [
            sum(product[p * BS + 8 * t : p * BS + 8 * t + 8] for p in range(2)) for t in range(BS // 8)
        ]

    def put(part, place, tile):
        for half in range(length // LANES):
            terms[half, (part * span + place) * 8 : (part * span + place) * 8 + 8, :] = tile[
                :, half * LANES : (half + 1) * LANES
            ]

    def put_kind(kind, product_of):
        for place, pair in enumerate(pairs):
            rows = rows_of(product_of(*pair))
            put(0, kind * block + place, sum(jnp.where(low[t], rows[t], 0.0) for t in range(BS // 8)))
            put(1, kind * block + place, sum(jnp.where(low[t], 0.0, rows[t]) for t in range(BS // 8)))

    groups = [range(at, at + group) for at in range(0, frames, group)]
    weights = [mask(f) for f in range(frames)]
    spec = []
    for index, members in enumerate(groups):
        coil_image(
            index,
            [(est_ref[f, :BS, :] - mail(f, 0, 0, BS), est_ref[f, BS:strip, :] - mail(f, 0, BS, BS)) for f in members],
        )
        spec.append(mxu(left[index], table_ref[...]))
    for part in range(2):
        for place in range(3 * block, span):
            put(part, place, jnp.zeros((8, length), jnp.float32))
    put_kind(0, lambda f, g: est_ref[f] * est_ref[g])
    home = []
    for index, members in enumerate(groups):
        for k, f in enumerate(members):
            for c in range(coils):
                at = slice((k * coils + c) * BS, (k * coils + c + 1) * BS)
                w = weights[f][c : c + 1]
                right[index, at, :length] = w.astype(jnp.bfloat16) * spec[index][at, :length].astype(jnp.bfloat16)
                right[index, at, length:] = (-w).astype(jnp.bfloat16) * spec[index][at, length:].astype(jnp.bfloat16)
        home.append(mxu(right[index], table_ref[...]))
    probe = []
    for index, members in enumerate(groups):
        values = []
        for k, f in enumerate(members):
            gr = mail(f, 1, 0, BS)
            gi = mail(f, 1, BS, BS)
            for c in range(coils):
                at = slice((k * coils + c) * BS, (k * coils + c + 1) * BS)
                sr, si = sens_ref[c, 0], sens_ref[c, 1]
                br, bi = home[index][at, :length], home[index][at, length:]
                gr = gr + (sr * br - si * bi)
                gi = gi - (sr * bi + si * br)
            grad_ref[f, :BS, :] = gr
            grad_ref[f, BS:strip, :] = gi
            num = num + fold(gr * gr + gi * gi)
            values.append((gr, gi))
        coil_image(index, values)
        probe.append(mxu(left[index], table_ref[...]))
    put_kind(1, lambda f, g: est_ref[f] * grad_ref[g] + est_ref[g] * grad_ref[f])
    put_kind(2, lambda f, g: grad_ref[f] * grad_ref[g])
    for index, members in enumerate(groups):
        for k, f in enumerate(members):
            for c in range(coils):
                at = slice((k * coils + c) * BS, (k * coils + c + 1) * BS)
                pr, pi = probe[index][at, :length], probe[index][at, length:]
                den = den + weights[f][c : c + 1] * fold(pr * pr + pi * pi)
    numer = jnp.sum(jnp.sum(num, axis=0, keepdims=True), axis=1, keepdims=True)
    denom = jnp.sum(jnp.sum(den, axis=0, keepdims=True), axis=1, keepdims=True)

    blocks = length // BS
    shift = offset_row(offsets_ref, 1, 1, length)
    member = in_block(iota((blocks, length), 1), shift, iota((blocks, length), 0), length)
    lane = iota((blocks, span), 1)
    packs = []
    for part in range(2):
        sums = jnp.concatenate(
            [
                sum(terms[half, pl.ds(part * span * 8 + s, span, stride=8), :] for s in range(8))
                for half in range(length // LANES)
            ],
            axis=1,
        )
        pack = pick_rows(member, sums)
        pack = jnp.where(lane == 3 * block, numer, jnp.where(lane == 3 * block + 1, denom, pack))
        own_ref[part * blocks : (part + 1) * blocks, :] = pack
        packs.append(pack)
    me = lax.axis_index("tm")
    strips = out_ref.shape[0]
    before = lax.rem(me + strips - 1, strips)
    for target in range(strips):
        out_ref[target] = jnp.where(before == target, packs[1], packs[0])


def last_kernel(offsets_ref, own_ref, heard_ref, est_ref, grad_ref, select_ref, out_ref, held, spread):
    frames, strip, length = est_ref.shape
    strips, blocks, span = heard_ref.shape
    block = len(pair_list(frames))
    me = lax.axis_index("tm")
    numer = jnp.zeros((1, 1), jnp.float32)
    denom = jnp.zeros((1, 1), jnp.float32)
    for k in range(strips):
        numer = numer + heard_ref[k, 0:1, 3 * block : 3 * block + 1]
        denom = denom + heard_ref[k, 0:1, 3 * block + 1 : 3 * block + 2]
    step = numer / (denom + epsilon)
    after = lax.rem(me + 1, strips)
    before = lax.rem(me + strips - 1, strips)
    total = own_ref[...] + jnp.concatenate([heard_ref[after], heard_ref[before]], axis=0)
    cross = pltpu.roll(total, span - block, 1)
    square = pltpu.roll(total, span - 2 * block, 1)
    gram = total - step * cross + step * step * square
    gram = jnp.concatenate([gram, jnp.zeros((LANES - 2 * blocks, span), jnp.float32)], axis=0)
    gram = jnp.where(iota(gram.shape, 1) < block, gram, 0.0)
    gram = pick_rows(select_ref[...], gram)
    factors = shrink_factors(gram, held, frames)
    shift = offset_row(offsets_ref, 1, 1, length)
    column = iota((LANES, length), 1)
    row = iota((LANES, length), 0)
    broad = [in_block(column, shift, row - part * blocks, length).astype(jnp.float32) for part in range(2)]
    spread[...] = pick(factors, jnp.concatenate(broad, axis=1))
    edge = upper_rows(offsets_ref, length)
    moved = [est_ref[f] - step * grad_ref[f] for f in range(frames)]
    for t in range(BS // 8):
        low = iota((8, length), 0) + 8 * t >= edge
        for f in range(frames):
            total = [jnp.zeros((8, length), jnp.float32)] * 2
            for g in range(frames):
                at = f * frames + g
                factor = jnp.where(low, spread[at : at + 1, :length], spread[at : at + 1, length:])
                total = [total[p] + factor * moved[g][p * BS + 8 * t : p * BS + 8 * t + 8] for p in range(2)]
            for p in range(2):
                rows = slice(p * BS + 8 * t, p * BS + 8 * t + 8)
                out_ref[f, rows, :] = moved[f][rows] - total[p]


def place_kernel(offsets_ref, strips_ref, out_hbm, whole, sems):
    strips, _, length = strips_ref.shape
    width = strips * BS
    shift = offset_row(offsets_ref, 0, 0, length)
    copies = []
    for part in range(2):
        image = strips_ref[:, part * BS : (part + 1) * BS, :].reshape(width, length)
        step = 1
        while step < BS:
            image = jnp.where((shift & step) != 0, pltpu.roll(image, width - step, 0), image)
            step *= 2
        whole[part] = image
        copies.append(pltpu.make_async_copy(whole.at[part], out_hbm.at[0, part], sems.at[part]))
        copies[-1].start()
    for copy in copies:
        copy.wait()


def vmem():
    return pl.BlockSpec(memory_space=pltpu.VMEM)


def hbm():
    return pl.BlockSpec(memory_space=pltpu.HBM)


def f32(*shape):
    return jax.ShapeDtypeStruct(shape, jnp.float32)


def exchange(blocks):
    return lax.all_to_all(blocks, "tm", split_axis=0, concat_axis=0, tiled=True)


def params(mebibytes=16):
    return pltpu.CompilerParams(vmem_limit_bytes=mebibytes * 1024 * 1024)


def frame_call(start_image, sensitivity, kspace, sampled, offsets, table):
    _, _, width, length = start_image.shape
    coils = sensitivity.shape[0]
    rows = width
    chunks = width // rows
    return pl.pallas_call(
        frame_kernel,
        out_shape=(
            pltpu.VMEM((width // BS, length // LANES * (4 * BS + coils) + 8, LANES), jnp.float32),
            pltpu.VMEM((coils, 2, BS, length), jnp.float32),
            pltpu.VMEM((SUBLANES, LANES), jnp.int32),
        ),
        in_specs=[hbm()] * 6,
        out_specs=(vmem(),) * 3,
        scratch_shapes=[
            pltpu.SMEM(offsets.shape, jnp.int32),
            pltpu.VMEM(start_image.shape, jnp.float32),
            pltpu.VMEM((chunks, coils, 2, rows, length), jnp.bfloat16),
            pltpu.VMEM((chunks, coils, 2, rows, length), jnp.bfloat16),
            pltpu.VMEM(sampled.shape, jnp.int32),
            pltpu.VMEM(table.shape, jnp.bfloat16),
            pltpu.VMEM((2, width, length), jnp.float32),
            pltpu.VMEM((chunks, coils * rows, 2 * length), jnp.bfloat16),
            pltpu.VMEM((chunks, coils * rows, 2 * length), jnp.bfloat16),
            pltpu.SemaphoreType.DMA((4,)),
            pltpu.SemaphoreType.DMA((2, chunks)),
        ],
        compiler_params=params(60),
        name="frame_gradient",
    )(offsets, start_image, sensitivity, kspace, sampled, table)


def middle_call(mail, sens, offsets, table):
    frames = mail.shape[0]
    coils, _, _, length = sens.shape
    count = frames * frames
    blocks = length // BS
    group = frames
    return pl.pallas_call(
        middle_kernel,
        out_shape=(
            f32(frames, blocks, LANES),
            f32(2 * blocks, LANES),
            f32(frames, 2 * BS, length),
            f32(frames, 2 * BS, length),
        ),
        in_specs=[vmem()] * 4,
        out_specs=(vmem(),) * 4,
        scratch_shapes=[
            pltpu.VMEM((length // LANES, 2 * LANES * 8, LANES), jnp.float32),
            pltpu.VMEM((NEWTON, count, LANES), jnp.float32),
            pltpu.VMEM((count, length), jnp.float32),
            pltpu.VMEM((frames // group, group * coils * BS, 2 * length), jnp.bfloat16),
            pltpu.VMEM((frames // group, group * coils * BS, 2 * length), jnp.bfloat16),
        ],
        compiler_params=params(),
        name="strip_shrink_gradient",
    )(offsets, mail, sens, table)


def last_call(own, heard, estimate, gradient, offsets):
    frames, strip, length = estimate.shape
    count = frames * frames
    return pl.pallas_call(
        last_kernel,
        out_shape=f32(frames, strip, length),
        in_specs=[vmem()] * 6,
        out_specs=vmem(),
        scratch_shapes=[
            pltpu.VMEM((NEWTON, count, LANES), jnp.float32),
            pltpu.VMEM((count, 2 * length), jnp.float32),
        ],
        compiler_params=params(),
        name="strip_shrink",
    )(offsets, own, heard, estimate, gradient, jnp.asarray(pair_select(frames, LANES)))


def place_call(strips, offsets):
    count, strip, length = strips.shape
    width = count * strip // 2
    return pl.pallas_call(
        place_kernel,
        out_shape=f32(1, 2, width, length),
        in_specs=[vmem()] * 2,
        out_specs=hbm(),
        scratch_shapes=[pltpu.VMEM((2, width, length), jnp.float32), pltpu.SemaphoreType.DMA((2,))],
        compiler_params=params(),
        name="frame_place",
    )(offsets, strips)


def strips_body(start_image, sensitivity, kspace, sampled, offsets):
    table = jnp.asarray(wide_table(start_image.shape[3]))
    mail, sens, offsets = frame_call(start_image, sensitivity, kspace, sampled, offsets, table)
    mail = exchange(mail)
    sent, own, estimate, gradient = middle_call(mail, sens, offsets, table)
    returned = exchange(last_call(own, exchange(sent), estimate, gradient, offsets))
    return place_call(returned, offsets)


def fits_strips(start_image, sensitivity, kspace, sampled, offsets):
    strips = lax.axis_size("tm")
    frames, _, width, length = start_image.shape
    coils = sensitivity.shape[0]
    kinds = 3 * len(pair_list(strips))
    return (
        frames == 1
        and width == strips * BS
        and strips == SUBLANES
        and coils % SUBLANES == 0
        and ITERS == 2
        and length % LANES == 0
        and 2 * (length // BS) <= LANES
        and kinds + 2 <= LANES
    )


def body(*args):
    return (strips_body if fits_strips(*args) else whole_body)(*args)


def solution(mesh):
    placed = (
        P(("cuts", "tm"), None, None, None),
        P("cuts", None, None, None),
        P(("cuts", "tm"), None, None, None, None),
        P(("cuts", "tm"), None, None),
        P("cuts", None),
    )
    return jax.shard_map(
        body,
        mesh=mesh,
        in_specs=placed,
        out_specs=P(("cuts", "tm"), None, None, None),
        check_vma=False,
    )
```
